32 devices in a mesh: src: 4 (over z), gx: 2 (over y), gy: 4 (over x, core).
Axes of the slice: x: 2, y: 2, z: 4, core: 2. Of those that a mesh axis runs over, the one named last changes fastest.
Arguments:
- adjoint_now: float32 [4, 2, 8, 128, 512], P('src', None, 'gx', 'gy'), may hold values from -6 to 6
- adjoint_before: float32 [4, 2, 8, 128, 512], P('src', None, 'gx', 'gy'), may hold values from -6 to 6
- forward_field: bfloat16 [3, 4, 2, 8, 128, 512], P(None, 'src', None, 'gx', 'gy'), may hold values from -6 to 6
- velocity: float32 [8, 128, 512], P('gx', 'gy'), may hold values from 0.2 to 0.4
- thomsen_eps: float32 [8, 128, 512], P('gx', 'gy'), may hold values from 0.05 to 0.35
- thomsen_delta: float32 [8, 128, 512], P('gx', 'gy'), may hold values from 0 to 0.25
- tilt_level: int32 [8, 128, 512], P('gx', 'gy'), may hold values from 0 to 31
- azimuth_level: int32 [8, 128, 512], P('gx', 'gy'), may hold values from 0 to 31
- channel_cell: int32 [4, 1536], P('src'), may hold values from 0 to 1023
- channel_count: int32 [4], P('src'), may hold values from 512 to 1536, as said below
- residual_trace: float32 [4, 3, 1536], P('src'), may hold values from -6 to 6
Outputs:
- adjoint_next: float32 [4, 2, 8, 128, 512], P('src', None, 'gx', 'gy')
- grad_velocity: float32 [8, 128, 512], P('gx', 'gy', 'src')
- grad_epsilon: float32 [8, 128, 512], P('gx', 'gy', 'src')
- grad_delta: float32 [8, 128, 512], P('gx', 'gy', 'src')
The draws below stay inside these ranges and needn't reach their ends.
Inputs may be any that keep to these rules, and one draw needn't show every extreme that they name: `channel_count`: some virtual source has 1536 live channels and some other has 512.
All inputs are finite; a program needn't handle non-finite values.
Results may differ from the reference program's by a relative error of at most 0.0003.
Values sent between devices are 32-bit elements; how exact they have to be, the bound alone decides.
No kernel may reach another device: no remote copies, remote signals or barrier semaphores. Data moves between devices by JAX's collectives and lax.ppermute only.
A program may use at most 64 MiB of HBM per device.

```python
import math
import jax
import jax.numpy as jnp

NZ = 512
STEPS = 3
LEVELS = 32
CH_MAX = 1536
NX = 8
NY = 128
SOURCES = 4


def draw_channel_count(key, part):
    key_base = jax.random.fold_in(key, 11)
    key_most = jax.random.fold_in(key, 12)
    key_least = jax.random.fold_in(key, 13)
    counts_base = jax.random.randint(key_base, (SOURCES,), CH_MAX // 3, CH_MAX + 1)
    busiest = jax.random.randint(key_most, (), 0, SOURCES)
    offset_draw = jax.random.randint(key_least, (), 0, SOURCES - 1)
    lightest = (busiest + 1 + offset_draw) % SOURCES
    counts_base = counts_base.at[busiest].set(CH_MAX)
    counts_base = counts_base.at[lightest].set(CH_MAX // 3)
    return counts_base.astype(jnp.int32)


def plant(entries, stream_key, least, top_value):
    place = [jax.random.randint(jax.random.fold_in(stream_key, axis), (), 0, length) for axis, length in enumerate(entries.shape)]
    longest = entries.shape.index(max(entries.shape))
    beside = place[:longest] + [(place[longest] + 1) % entries.shape[longest]] + place[longest + 1:]
    return entries.at[tuple(place)].set(least).at[tuple(beside)].set(top_value)


def steps_of(own_key, shape, cuts, smallest, high):
    factor_of, own = 1.0, jax.random.fold_in(own_key, 6)
    for dim, shards_of in cuts:
        steps = jnp.exp(jax.random.uniform(jax.random.fold_in(own, dim), (shards_of,), jnp.float32, smallest / len(cuts), high / len(cuts)))
        factor_of = factor_of * jnp.repeat(steps, shape[dim] // shards_of).reshape([-1 if axis == dim else 1 for axis in range(len(shape))])
    return factor_of


def bell_draw(own_key, shape, deviation, limit, pieces=(), kind=jnp.bfloat16):
    level = steps_of(own_key, shape, pieces, -0.22, 0.18) if pieces else 1.0
    drawn = jax.random.normal(own_key, shape, jnp.float32) * deviation * level
    return jnp.minimum(jnp.maximum(drawn, -limit), limit).astype(kind)


def setup_inputs(seed: int = 0) -> dict:
    splits = jax.random.split(jax.random.key(seed), 12)
    adjoint_now = bell_draw(splits[0], (SOURCES, 2, NX, NY, NZ), 1.0, 6.0, ((0, 4), (2, 2), (3, 4)), jnp.float32)
    adjoint_before = bell_draw(splits[1], (SOURCES, 2, NX, NY, NZ), 1.0, 6.0, ((0, 4), (2, 2), (3, 4)), jnp.float32)
    forward_field = bell_draw(splits[2], (STEPS, SOURCES, 2, NX, NY, NZ), 1.0, 6.0, ((1, 4), (3, 2), (4, 4)))
    velocity = jnp.clip(jnp.exp(math.log(0.4) - 0.6931472 * jax.random.uniform(splits[3], (NX, NY, NZ), jnp.float32) ** steps_of(splits[3], (NX, NY, NZ), ((0, 2), (1, 4)), -0.2, 0.2)), 0.2, 0.4)
    thomsen_eps = jnp.clip(0.05 + 0.29999999 * jax.random.uniform(splits[4], (NX, NY, NZ), jnp.float32) ** steps_of(splits[4], (NX, NY, NZ), ((0, 2), (1, 4)), -0.2, 0.2), 0.05, 0.35)
    thomsen_delta = jnp.clip(0.25 * jax.random.uniform(splits[5], (NX, NY, NZ), jnp.float32) ** steps_of(splits[5], (NX, NY, NZ), ((0, 2), (1, 4)), -0.2, 0.2), 0.0, 0.25)
    tilt_level = plant(jax.random.randint(splits[6], (NX, NY, NZ), 0, LEVELS), jax.random.fold_in(splits[6], 1), 0, LEVELS - 1).astype(jnp.int32)
    azimuth_level = plant(jax.random.randint(splits[7], (NX, NY, NZ), 0, LEVELS), jax.random.fold_in(splits[7], 1), 0, LEVELS - 1).astype(jnp.int32)
    channel_cell = plant(jax.random.randint(splits[8], (SOURCES, CH_MAX), 0, NX * NY), jax.random.fold_in(splits[8], 1), 0, (NX * NY) - 1).astype(jnp.int32)
    channel_count = draw_channel_count(jax.random.fold_in(splits[11], 71), 0)
    residual_trace = bell_draw(splits[10], (SOURCES, STEPS, CH_MAX), 1.0, 6.0, ((0, 4),), jnp.float32)
    return dict(adjoint_now=adjoint_now, adjoint_before=adjoint_before, forward_field=forward_field, velocity=velocity, thomsen_eps=thomsen_eps, thomsen_delta=thomsen_delta, tilt_level=tilt_level, azimuth_level=azimuth_level, channel_cell=channel_cell, channel_count=channel_count, residual_trace=residual_trace)


def derivatives(padded):
    center = padded[..., 1:-1, 1:-1, 1:-1]
    second_x = padded[..., 2:, 1:-1, 1:-1] + padded[..., :-2, 1:-1, 1:-1] - 2.0 * center
    second_y = padded[..., 1:-1, 2:, 1:-1] + padded[..., 1:-1, :-2, 1:-1] - 2.0 * center
    second_z = padded[..., 1:-1, 1:-1, 2:] + padded[..., 1:-1, 1:-1, :-2] - 2.0 * center
    mixed_xy = 0.25 * (padded[..., 2:, 2:, 1:-1] - padded[..., 2:, :-2, 1:-1] - padded[..., :-2, 2:, 1:-1] + padded[..., :-2, :-2, 1:-1])
    mixed_yz = 0.25 * (padded[..., 1:-1, 2:, 2:] - padded[..., 1:-1, 2:, :-2] - padded[..., 1:-1, :-2, 2:] + padded[..., 1:-1, :-2, :-2])
    mixed_xz = 0.25 * (padded[..., 2:, 1:-1, 2:] - padded[..., 2:, 1:-1, :-2] - padded[..., :-2, 1:-1, 2:] + padded[..., :-2, 1:-1, :-2])
    return (second_x, second_y, second_z, mixed_xy, mixed_yz, mixed_xz)

def tilt_weights(tilt_level, azimuth_level):
    theta = tilt_level.astype(jnp.float32) * (0.5 * math.pi / LEVELS)
    azimuth = azimuth_level.astype(jnp.float32) * (2.0 * math.pi / LEVELS)
    sin_t = jnp.sin(theta)
    cos_t = jnp.cos(theta)
    sin_p = jnp.sin(azimuth)
    cos_p = jnp.cos(azimuth)
    return (sin_t * sin_t * cos_p * cos_p, sin_t * sin_t * sin_p * sin_p, cos_t * cos_t, 2.0 * sin_t * sin_t * sin_p * cos_p, 2.0 * sin_t * cos_t * sin_p, 2.0 * sin_t * cos_t * cos_p)

def split_operators(padded, weights):
    parts = derivatives(padded)
    axial = weights[0] * parts[0]
    for index in range(1, 6):
        axial = axial + weights[index] * parts[index]
    laplace = parts[0] + parts[1] + parts[2]
    return (laplace[..., 0, :, :, :] - axial[..., 0, :, :, :], axial[..., 1, :, :, :])

def reference(adjoint_now, adjoint_before, forward_field, velocity, thomsen_eps, thomsen_delta, tilt_level, azimuth_level, channel_cell, channel_count, residual_trace):
    weights = tilt_weights(tilt_level, azimuth_level)
    speed_sq = velocity * velocity
    stretch = 1.0 + 2.0 * thomsen_eps
    root = jnp.sqrt(1.0 + 2.0 * thomsen_delta)
    live = jnp.arange(CH_MAX, dtype=jnp.int32)[None, :] < channel_count[:, None]
    loads = jnp.where(live[:, None, :], residual_trace, jnp.zeros_like(residual_trace))
    rows_src = jnp.arange(SOURCES, dtype=jnp.int32)[:, None, None]
    rows_time = jnp.arange(STEPS, dtype=jnp.int32)[None, :, None]
    surface = jnp.zeros((SOURCES, STEPS, NX * NY), residual_trace.dtype)
    surface = surface.at[rows_src, rows_time, channel_cell[:, None, :]].add(loads)
    surface = surface.reshape(SOURCES, STEPS, NX, NY)
    grad_velocity = jnp.zeros_like(velocity)
    grad_epsilon = jnp.zeros_like(velocity)
    grad_delta = jnp.zeros_like(velocity)
    finals = []
    for source in range(SOURCES):
        current = adjoint_now[source]
        previous = adjoint_before[source]
        for time_step in range(STEPS):
            padded = jnp.pad(current, ((0, 0), (1, 1), (1, 1), (1, 1)))
            horiz_p, axial_q = split_operators(padded, weights)
            update_p = stretch * horiz_p + root * axial_q
            update_q = root * horiz_p + axial_q
            following = 2.0 * current - previous + speed_sq * jnp.stack([update_p, update_q])
            following = following.at[0, :, :, 0].add(surface[source, time_step])
            forward_p = forward_field[time_step, source, 0].astype(jnp.float32)
            forward_q = forward_field[time_step, source, 1].astype(jnp.float32)
            grad_velocity = grad_velocity + 2.0 * velocity * (forward_p * update_p + forward_q * update_q)
            grad_epsilon = grad_epsilon + 2.0 * speed_sq * forward_p * horiz_p
            grad_delta = grad_delta + speed_sq / root * (forward_p * axial_q + forward_q * horiz_p)
            previous = current
            current = following
        finals.append(current)
    return (jnp.stack(finals), grad_velocity, grad_epsilon, grad_delta)
```

```python
import math

import jax
import jax.numpy as jnp
from jax import lax
from jax.experimental import pallas as pl
from jax.experimental.pallas import tpu as pltpu
from jax.sharding import PartitionSpec as P

LEVELS = 32
LANES = 128
HALO = 4
VMEM_LIMIT = 16 * 1024 * 1024
F32 = jnp.float32


def run_kernel(body, ins, outs, scratch=None, smem=(), name=None, flops=0):
    scratch = scratch or {}
    names = list(ins) + list(outs) + list(scratch)

    def kernel(*refs):
        body(dict(zip(names, refs)))

    results = pl.pallas_call(
        kernel,
        name=name,
        out_shape=[jax.ShapeDtypeStruct(shape, F32) for shape in outs.values()],
        in_specs=[
            pl.BlockSpec(memory_space=pltpu.SMEM if key in smem else pltpu.VMEM) for key in ins
        ],
        out_specs=[pl.BlockSpec(memory_space=pltpu.VMEM)] * len(outs),
        scratch_shapes=[pltpu.VMEM(shape, F32) for shape in scratch.values()],
        compiler_params=pltpu.CompilerParams(vmem_limit_bytes=VMEM_LIMIT),
        cost_estimate=pl.CostEstimate(flops=flops, bytes_accessed=flops // 8, transcendentals=0),
    )(*ins.values())
    return dict(zip(outs, results))


def pair_swaps(count, first):
    pairs = []
    for low in range(first, count - 1, 2):
        pairs += [(low, low + 1), (low + 1, low)]
    return pairs


def swap(block, axis, count, first):
    return lax.ppermute(block, axis, pair_swaps(count, first))


def lanes_of(j):
    return pl.ds(j * LANES, LANES)


def is_odd(axis):
    return lax.rem(lax.axis_index(axis), 2)


class Tile:
    def __init__(self, mesh, velocity, steps):
        self.nx, self.ny, self.nz = velocity.shape
        self.steps = steps
        self.nj = self.nz // LANES
        self.rows = self.ny + 2 * HALO
        self.gx, self.gy, self.src = mesh.shape["gx"], mesh.shape["gy"], mesh.shape["src"]
        self.far = self.gx > 2

    def place(self, m):
        return m + is_odd("gx") * (self.nx - 1 - 2 * m)

    def phase(self, t, m):
        if m == self.nx or m == -1:
            return t + 2 if (m == self.nx or self.far) else 0
        if t < 0:
            return 0
        return max(self.phase(t - 1, k) for k in (m - 1, m, m + 1))


def rolled(value, by, axis):
    return pltpu.roll(value, by % value.shape[axis], axis)


def pack_edges(tile, raw):
    shape = (9, tile.nx // 2, 2 * HALO, tile.nz)

    def body(r):
        odd = is_odd("gy") == 1
        low_half = lax.broadcasted_iota(jnp.int32, (8, tile.nz), 0) < HALO

        def rows(item, m, start):
            here = tile.place(m)
            if item < 4:
                ref = r["now"] if item < 2 else r["before"]
                return ref[0, item % 2, here, pl.ds(start, 8), :]
            ref = r[("velocity", "eps", "delta", "tilt", "azimuth")[item - 4]]
            return ref[here, pl.ds(start, 8), :].astype(F32)

        for item in range(9):
            for pair in range(tile.nx // 2):
                a, b = 2 * pair, 2 * pair + 1
                top = jnp.where(
                    low_half,
                    rolled(rows(item, a, tile.ny - 8), HALO, 0),
                    rows(item, b, tile.ny - 8),
                )
                bottom = jnp.where(low_half, rows(item, a, 0), rolled(rows(item, b, 0), HALO, 0))
                r["even"][item, pair] = jnp.where(odd, bottom, top)
                r["odd"][item, pair] = jnp.where(odd, top, bottom)

    out = run_kernel(body, raw, {"even": shape, "odd": shape}, name="pack_edges", flops=10**6)
    return out["even"], out["odd"]


def halo_rows(tile, r, item, m):
    odd = is_odd("gy") == 1
    low_half = lax.broadcasted_iota(jnp.int32, (8, tile.nz), 0) < HALO
    even_got, odd_got = r["got_even"][item, m // 2], r["got_odd"][item, m // 2]
    upper = jnp.where(odd, odd_got, even_got)
    lower = jnp.where(odd, even_got, odd_got)
    if m % 2 == 0:
        return jnp.where(low_half, upper, rolled(lower, HALO, 0))
    return jnp.where(low_half, rolled(upper, HALO, 0), lower)


def edge_planes(tile, now, got_even, got_odd):
    outs = {"near": (2, tile.rows, tile.nz)}
    if tile.far:
        outs["far"] = (2, tile.rows, tile.nz)

    def body(r):
        for key in outs:
            m = tile.nx - 1 if key == "near" else 0
            for c in range(2):
                r[key][c, : tile.ny] = r["now"][0, c, tile.place(m)]
                r[key][c, tile.ny :] = halo_rows(tile, r, c, m)

    ins = {"now": now, "got_even": got_even, "got_odd": got_odd}
    return run_kernel(body, ins, outs, name="edge_planes", flops=10**5)


def angle_tables(rows):
    level = lax.broadcasted_iota(jnp.int32, (rows, LANES), 1).astype(F32)
    theta = level * (0.5 * math.pi / LEVELS)
    azimuth = level * (2.0 * math.pi / LEVELS)
    sin_t, cos_t, sin_p, cos_p = jnp.sin(theta), jnp.cos(theta), jnp.sin(azimuth), jnp.cos(azimuth)
    return (
        sin_t * sin_t,
        0.5 * sin_t * cos_t,
        cos_t * cos_t,
        cos_p * cos_p,
        sin_p * sin_p,
        0.5 * sin_p * cos_p,
        sin_p,
        cos_p,
    )


def store_weights(out, m, rows, j, tables, sign, velocity, eps, delta, tilt, azimuth):
    def look(table, level):
        return jnp.take_along_axis(table, level, axis=1)

    sin2_t, sincos_t, cos2_t = (look(tables[k], tilt) for k in range(3))
    cos2_p, sin2_p, sincos_p, sin_p, cos_p = (look(tables[k], azimuth) for k in range(3, 8))
    speed_sq = velocity * velocity
    root = jnp.sqrt(1.0 + 2.0 * delta)
    values = (
        sin2_t * cos2_p,
        sin2_t * sin2_p,
        cos2_t,
        sign * (sin2_t * sincos_p),
        sincos_t * sin_p,
        sign * (sincos_t * cos_p),
        speed_sq * (1.0 + 2.0 * eps),
        speed_sq * root,
        speed_sq,
    )
    for k, value in enumerate(values):
        out[k, m, rows, lanes_of(j)] = value


def x_sign():
    return 1.0 - 2.0 * is_odd("gx").astype(F32)


def own_weights(tile, raw):
    coefs = ("velocity", "eps", "delta", "tilt", "azimuth")

    def body(r):
        tables = angle_tables(8)
        sign = x_sign()

        def plane(m, _):
            here = tile.place(m)
            for j in range(tile.nj):
                for start in range(0, tile.ny, 8):
                    rows = pl.ds(start, 8)
                    store_weights(
                        r["w"], m, rows, j, tables, sign,
                        *(r[key][here, rows, lanes_of(j)] for key in coefs),
                    )
            return 0

        lax.fori_loop(0, tile.nx, plane, 0)

    ins = {key: raw[key] for key in coefs}
    out = run_kernel(
        body, ins, {"w": (9, tile.nx, tile.ny, tile.nz)}, name="own_weights", flops=3 * 10**6
    )
    return out["w"]


def surface_load(tile, cell, count, trace):
    channels = cell.shape[1]
    width = tile.ny * tile.gy

    def body(r):
        start_x = lax.axis_index("gx") * tile.nx
        start_y = lax.axis_index("gy") * tile.ny
        cell_here = r["cell"][...]
        slots = lax.broadcasted_iota(jnp.int32, (1, channels), 1)
        live = slots < r["count"][0]
        if width & (width - 1) == 0:
            row_of = cell_here & (width - 1)
        else:
            row_of = lax.rem(cell_here, jnp.full_like(cell_here, width))
        place = lax.broadcasted_iota(jnp.int32, (tile.rows, 1), 0)
        place = jnp.where(place >= tile.ny + HALO, place - tile.rows, place) + start_y
        onehot = jnp.where(row_of == place, 1.0, 0.0)
        first = lax.broadcasted_iota(jnp.int32, (tile.rows, LANES), 1) == 0
        pad = jnp.zeros((LANES - tile.steps, channels), F32)
        trace_here = r["trace"][0]
        for m in range(tile.nx):
            low = (start_x + tile.place(m)) * width
            inside = live & (cell_here >= low) & (cell_here < low + width)
            load = jnp.concatenate([jnp.where(inside, trace_here, 0.0), pad], axis=0)
            columns = lax.dot_general(
                onehot, load, (((1,), (1,)), ((), ())),
                precision=lax.Precision.HIGHEST, preferred_element_type=F32,
            )
            for t in range(tile.steps):
                column = columns if t == 0 else rolled(columns, -t, 1)
                r["surface"][t, m] = jnp.where(first, column, 0.0)

    out = run_kernel(
        body,
        {"cell": cell, "count": count, "trace": trace},
        {"surface": (tile.steps, tile.nx, tile.rows, LANES)},
        smem=("count",),
        name="surface_load",
        flops=2 * 10**6,
    )
    return out["surface"]


def halo_state(tile, got_even, got_odd):
    def body(r):
        tables = angle_tables(8)
        sign = x_sign()
        for m in range(tile.nx):
            for item in range(4):
                r["uh"][item, m] = halo_rows(tile, r, item, m)
            coefs = [halo_rows(tile, r, item, m) for item in range(4, 9)]
            for j in range(tile.nj):
                part = [value[:, j * LANES : (j + 1) * LANES] for value in coefs]
                store_weights(
                    r["wh"], m, pl.ds(0, 8), j, tables, sign, *part[:3],
                    part[3].astype(jnp.int32), part[4].astype(jnp.int32),
                )

    outs = {"uh": (4, tile.nx, 8, tile.nz), "wh": (9, tile.nx, 8, tile.nz)}
    out = run_kernel(
        body, {"got_even": got_even, "got_odd": got_odd}, outs, name="halo_state", flops=10**6
    )
    return out["uh"], out["wh"]


class Stage:
    def __init__(self, tile, state, ops, pieces, name):
        self.tile, self.state, self.ops, self.pieces, self.name = tile, state, ops, pieces, name
        self.ins, self.outs, self.scratch = {}, {}, {}

    def need(self, key):
        if key not in self.outs and key not in self.scratch:
            self.ins[key] = self.state[key]

    def run(self):
        tile = self.tile
        for t, m in self.ops:
            last = t == tile.steps - 1
            for key in ("w", "forward"):
                self.need(key)
            for k in (m - 1, m, m + 1):
                if k == -1 and not tile.far:
                    continue
                if k in (-1, tile.nx):
                    self.need(("xf", t) if k == -1 else ("xn", t))
                elif t == 0:
                    for key in ("now", "uh"):
                        self.need(key)
                else:
                    self.need(("u", t, k))
            if t <= 1:
                for key in ("before" if t == 0 else "now", "uh"):
                    self.need(key)
            else:
                self.need(("u", t - 1, m))
            if not last:
                self.need("wh")
            self.need("surface")
            if t > 0:
                self.need(("g", t - 1, m))
            rows = tile.ny if last else tile.rows
            self.outs[("u", t + 1, m)] = (2, rows, tile.nz)
            total = (tile.nj, 3, tile.ny, LANES)
            if last and any(m in planes for planes in self.pieces):
                self.scratch[("g", t, m)] = total
            else:
                self.outs[("g", t, m)] = total
        for planes in self.pieces:
            for m in planes:
                self.need(("g", tile.steps - 1, m))
            for k in range(tile.src):
                self.outs[("s", planes, k)] = (len(planes), 3, tile.ny, tile.nz // tile.src)
        flops = len(self.ops) * 2 * 10**6 + 10**5
        out = run_kernel(self.body, self.ins, self.outs, self.scratch, name=self.name, flops=flops)
        self.state.update(out)

    def body(self, r):
        tile = self.tile
        for t, m in self.ops:
            self.update(r, t, m)
        me = lax.axis_index("src")
        per = tile.nj // tile.src
        for planes in self.pieces:
            for i, m in enumerate(planes):
                for k in range(tile.src):
                    owner = jnp.bitwise_xor(me, k)
                    for part in range(per):
                        r[("s", planes, k)][i, :, :, lanes_of(part)] = r[("g", tile.steps - 1, m)][
                            owner * per + part
                        ]

    def field(self, r, t, m, c, j):
        tile, lanes = self.tile, lanes_of(j)
        if m == -1:
            return r[("xf", t)][c, :, lanes] if tile.far else None
        if m == tile.nx:
            return r[("xn", t)][c, :, lanes]
        if t > 0:
            return r[("u", t, m)][c, :, lanes]
        ref, item = (r["now"], c) if t == 0 else (r["before"], 2 + c)
        return jnp.concatenate(
            [ref[0, c, tile.place(m), :, lanes], r["uh"][item, m, :, lanes]], axis=0
        )

    def update(self, r, t, m):
        tile = self.tile
        last = t == tile.steps - 1
        rows = tile.ny if last else tile.rows
        lane = lax.broadcasted_iota(jnp.int32, (tile.rows, LANES), 1)
        at_first, at_last = lane == 0, lane == LANES - 1

        def weight(k, j):
            own = r["w"][k, m, :, lanes_of(j)]
            return own if last else jnp.concatenate([own, r["wh"][k, m, :, lanes_of(j)]], axis=0)

        centers, halves = [], []
        for c in range(2):
            center = [self.field(r, t, m, c, j) for j in range(tile.nj)]
            total_x, diff_x = [], []
            for j in range(tile.nj):
                above, below = self.field(r, t, m + 1, c, j), self.field(r, t, m - 1, c, j)
                total_x.append(above if below is None else above + below)
                diff_x.append(above if below is None else above - below)
            centers.append(center)
            halves.append((total_x, diff_x))

        def deeper(blocks):
            moved = [rolled(block, -1, 1) for block in blocks] + [0.0]
            return [jnp.where(at_last, moved[j + 1], moved[j]) for j in range(tile.nj)]

        def shallower(blocks):
            moved = [rolled(block, 1, 1) for block in blocks] + [0.0]
            return [jnp.where(at_first, moved[j - 1], moved[j]) for j in range(tile.nj)]

        shifted = []
        for c in range(2):
            diff_x = halves[c][1]
            shifted.append(
                (deeper(centers[c]), shallower(centers[c]), deeper(diff_x), shallower(diff_x))
            )

        def both(block):
            return rolled(block, -1, 0)[:rows], rolled(block, 1, 0)[:rows]

        for j in range(tile.nj):
            weights = [weight(k, j) for k in range(6)]
            results = []
            for c in range(2):
                center = centers[c][j]
                total_x, diff_x = halves[c][0][j], halves[c][1][j]
                below, above, diff_below, diff_above = (part[j] for part in shifted[c])
                total_z, slope_z = (below + above)[:rows], below - above
                mixed_xz = (diff_below - diff_above)[:rows]
                up, down = both(center)
                total_y = up + down
                up, down = both(diff_x)
                mixed_xy = up - down
                up, down = both(slope_z)
                mixed_yz = up - down
                total_x, center = total_x[:rows], center[:rows]
                axial = (
                    weights[0] * total_x + weights[1] * total_y + weights[2] * total_z
                    + weights[3] * mixed_xy + weights[4] * mixed_yz + weights[5] * mixed_xz
                )
                if c == 0:
                    results.append(total_x + total_y + total_z - 4.0 * center - axial)
                else:
                    results.append(axial - 2.0 * center)
            horiz, axial = results
            stretched, rooted, speed_sq = (weight(k, j) for k in range(6, 9))
            before = [self.field(r, t - 1, m, c, j)[:rows] for c in range(2)]
            new_p = (
                2.0 * centers[0][j][:rows] - before[0] + stretched * horiz + rooted * axial
            )
            new_q = 2.0 * centers[1][j][:rows] - before[1] + rooted * horiz + speed_sq * axial
            if j == 0:
                new_p = new_p + r["surface"][t, m][:rows]
            r[("u", t + 1, m)][0, :, lanes_of(j)] = new_p
            r[("u", t + 1, m)][1, :, lanes_of(j)] = new_q
            here = tile.place(m)
            forward_p = r["forward"][t, 0, 0, here, :, lanes_of(j)].astype(F32)
            forward_q = r["forward"][t, 0, 1, here, :, lanes_of(j)].astype(F32)
            horiz, axial = horiz[: tile.ny], axial[: tile.ny]
            terms = (
                forward_p * horiz,
                forward_p * axial + forward_q * horiz,
                forward_q * axial,
            )
            for k, term in enumerate(terms):
                if t > 0:
                    term = term + r[("g", t - 1, m)][j, k]
                r[("g", t, m)][j, k] = term


def combine(tile, state, pieces, raw):
    depth = tile.nz // tile.src
    ins = {key: raw[key] for key in ("velocity", "eps", "delta")}
    for planes in pieces:
        ins[("s", planes, 0)] = state[("s", planes, 0)]
        for k in range(1, tile.src):
            ins[("r", planes, k)] = state[("r", planes, k)]
    shape = (tile.nx, tile.ny, depth)

    def body(r):
        lanes = pl.ds(pl.multiple_of(lax.axis_index("src") * depth, LANES), depth)
        for planes in pieces:
            for i, m in enumerate(planes):
                here = tile.place(m)
                sums = []
                for item in range(3):
                    total = r[("s", planes, 0)][i, item]
                    for k in range(1, tile.src):
                        total = total + r[("r", planes, k)][i, item]
                    sums.append(total)
                velocity = r["velocity"][here, :, lanes]
                root = jnp.sqrt(1.0 + 2.0 * r["delta"][here, :, lanes])
                stretch = 1.0 + 2.0 * r["eps"][here, :, lanes]
                speed_sq = velocity * velocity
                r["gv"][here] = 2.0 * velocity * (stretch * sums[0] + root * sums[1] + sums[2])
                r["ge"][here] = 2.0 * speed_sq * sums[0]
                r["gd"][here] = speed_sq / root * sums[1]

    out = run_kernel(body, ins, {"gv": shape, "ge": shape, "gd": shape}, name="combine", flops=10**6)
    return out["gv"], out["ge"], out["gd"]


def final_fields(tile, state):
    keys = [("u", tile.steps, m) for m in range(tile.nx)]

    def body(r):
        for m, key in enumerate(keys):
            for c in range(2):
                r["out"][0, c, tile.place(m)] = r[key][c]

    outs = {"out": (1, 2, tile.nx, tile.ny, tile.nz)}
    return run_kernel(body, {key: state[key] for key in keys}, outs, name="final_fields", flops=10**6)["out"]


def on_device(
    mesh,
    adjoint_now,
    adjoint_before,
    forward_field,
    velocity,
    thomsen_eps,
    thomsen_delta,
    tilt_level,
    azimuth_level,
    channel_cell,
    channel_count,
    residual_trace,
):
    tile = Tile(mesh, velocity, forward_field.shape[0])
    raw = {
        "now": adjoint_now,
        "before": adjoint_before,
        "velocity": velocity,
        "eps": thomsen_eps,
        "delta": thomsen_delta,
        "tilt": tilt_level,
        "azimuth": azimuth_level,
    }
    send_even, send_odd = pack_edges(tile, raw)
    got_even = swap(send_even, "gy", tile.gy, 0)
    got_odd = swap(send_odd, "gy", tile.gy, 1)
    state = {"now": adjoint_now, "before": adjoint_before, "forward": forward_field}
    state["w"] = own_weights(tile, raw)
    state["surface"] = surface_load(tile, channel_cell, channel_count, residual_trace)

    def exchange(t, near, far):
        state[("xn", t)] = swap(near, "gx", tile.gx, 0)
        if tile.far:
            state[("xf", t)] = swap(far, "gx", tile.gx, 1)

    edges = edge_planes(tile, adjoint_now, got_even, got_odd)
    exchange(0, edges["near"], edges.get("far"))
    state["uh"], state["wh"] = halo_state(tile, got_even, got_odd)

    ops = [(t, m) for t in range(tile.steps) for m in range(tile.nx)]
    last = tile.steps - 1
    ready = {m: tile.phase(last, m) for m in range(tile.nx)}
    issue = {}
    for m in range(tile.nx):
        issue.setdefault(max(ready[m], 1), []).append(m)
    pieces = []
    edge = {tile.nx - 1} | ({0} if tile.far else set())
    for phase in range(tile.steps + 1):
        mine = [op for op in ops if tile.phase(*op) == phase]
        front = [op for op in mine if phase > 0 and op[0] == phase - 1 and op[1] in edge]
        bulk = [op for op in mine if op not in front]
        done = [tuple(issue[phase])] if phase in issue else []
        pieces += done
        if phase == tile.steps:
            front, bulk = mine, []
        if front:
            Stage(tile, state, front, [] if bulk else done, f"front_{phase}").run()
            if phase < tile.steps:
                exchange(phase, state[("u", phase, tile.nx - 1)], state.get(("u", phase, 0)))
        if bulk:
            Stage(tile, state, bulk, done, f"bulk_{phase}").run()
        for planes in done:
            for k in range(1, tile.src):
                state[("r", planes, k)] = lax.ppermute(
                    state[("s", planes, k)], "src", [(i, i ^ k) for i in range(tile.src)]
                )
    following = final_fields(tile, state)
    return (following, *combine(tile, state, pieces, raw))


def solution(mesh):
    placed = (
        P("src", None, "gx", "gy", None),
        P("src", None, "gx", "gy", None),
        P(None, "src", None, "gx", "gy", None),
        P("gx", "gy", None),
        P("gx", "gy", None),
        P("gx", "gy", None),
        P("gx", "gy", None),
        P("gx", "gy", None),
        P("src", None),
        P("src"),
        P("src", None, None),
    )

    def program(*args):
        return on_device(mesh, *args)

    return jax.shard_map(
        program,
        mesh=mesh,
        in_specs=placed,
        out_specs=(
            P("src", None, "gx", "gy", None),
            P("gx", "gy", "src"),
            P("gx", "gy", "src"),
            P("gx", "gy", "src"),
        ),
        check_vma=False,
    )
```

```python
import math

import jax
import jax.numpy as jnp
from jax import lax
from jax.experimental import pallas as pl
from jax.experimental.pallas import tpu as pltpu
from jax.sharding import PartitionSpec as P

LEVELS = 32
LANES = 128
HALO = 4
VMEM_LIMIT = 8 * 1024 * 1024
F32 = jnp.float32


def run_kernel(body, ins, outs, scratch=None, spaces=None, copies=0, name=None, flops=0, final=False):
    scratch, spaces = scratch or {}, spaces or {}
    names = list(ins) + list(outs) + list(scratch) + ["done"]
    ins = {
        key: pltpu.with_memory_space_constraint(value, pltpu.HBM)
        if spaces.get(key) == pltpu.HBM
        else value
        for key, value in ins.items()
    }

    def kernel(*refs):
        body(dict(zip(names, refs)))

    results = pl.pallas_call(
        kernel,
        name=name,
        out_shape=[
            jax.ShapeDtypeStruct(shape, F32) if final else pltpu.VMEM(shape, kind)
            for shape, kind in (
                entry if isinstance(entry[0], tuple) else (entry, F32) for entry in outs.values()
            )
        ],
        in_specs=[
            pl.BlockSpec(memory_space=spaces.get(key, pltpu.VMEM)) for key in ins
        ],
        out_specs=[pl.BlockSpec(memory_space=pltpu.VMEM)] * len(outs),
        scratch_shapes=list(scratch.values())
        + [pltpu.SemaphoreType.DMA((copies,))] * (copies > 0),
        compiler_params=pltpu.CompilerParams(vmem_limit_bytes=VMEM_LIMIT),
        cost_estimate=pl.CostEstimate(flops=flops, bytes_accessed=flops // 8, transcendentals=0),
    )(*ins.values())
    return dict(zip(outs, results))


def pair_swaps(count, first):
    pairs = []
    for low in range(first, count - 1, 2):
        pairs += [(low, low + 1), (low + 1, low)]
    return pairs


def swap(block, axis, count, first):
    return lax.ppermute(block, axis, pair_swaps(count, first))


def lanes_of(j):
    return pl.ds(j * LANES, LANES)


def is_odd(axis):
    return lax.rem(lax.axis_index(axis), 2)


class Tile:
    def __init__(self, mesh, velocity, steps):
        self.nx, self.ny, self.nz = velocity.shape
        self.steps = steps
        self.nj = self.nz // LANES
        self.rows = self.ny + 2 * HALO
        self.gx, self.gy, self.src = mesh.shape["gx"], mesh.shape["gy"], mesh.shape["src"]
        self.far = self.gx > 2

    def place(self, m):
        return m + is_odd("gx") * (self.nx - 1 - 2 * m)

    def phase(self, t, m):
        if m == self.nx or m == -1:
            return t + 2 if (m == self.nx or self.far) else 0
        if t < 0:
            return 0
        return max(self.phase(t - 1, k) for k in (m - 1, m, m + 1))


def rolled(value, by, axis):
    return pltpu.roll(value, by % value.shape[axis], axis)


UNITS = (
    [("now", c, 0, 2) for c in range(2)]
    + [("before", c, 0, 2) for c in range(2)]
    + [(key, 0, 0, 2) for key in ("velocity", "eps", "delta", "tilt", "azimuth")]
    + [("now", 0, 2, 1), ("now", 1, 2, 1)]
)
ITEMS = [("now", 0), ("now", 1), ("before", 0), ("before", 1)] + [
    (key, 0) for key in ("velocity", "eps", "delta", "tilt", "azimuth")
]


def edge_rows():
    placed, at = [], 0
    for key, c, first, count in UNITS:
        placed.append((key, c, first, count, at))
        at += count
    return placed, at


def pack_edges(tile, raw):
    placed, per_plane = edge_rows()
    total = per_plane * tile.nx
    assert total % 8 == 0
    outs = {"even": (total, tile.nz), "odd": (total, tile.nz), "near": (2, tile.ny, tile.nz)}
    if tile.far:
        outs["far"] = outs["near"]
    outs.update({key: (value.shape, value.dtype) for key, value in raw.items()})

    def body(r):
        copies = []
        for i, key in enumerate(raw):
            copies.append(pltpu.make_async_copy(r[key + "_hbm"], r[key], r["done"].at[i]))
            copies[-1].start()
        for copy in copies:
            copy.wait()
        for c in range(2):
            r["near"][c] = r["now"][0, c, tile.place(tile.nx - 1)]
            if tile.far:
                r["far"][c] = r["now"][0, c, tile.place(0)]

        odd = is_odd("gy") == 1
        sub = lax.broadcasted_iota(jnp.int32, (8, tile.nz), 0)

        def rows_of(key, c, m, end):
            here = tile.place(m)
            rows = pl.ds(tile.ny - 8 if end == "_top" else 0, 8)
            ref = r[key].at[0, c] if key in ("now", "before") else r[key]
            return ref[here, rows, :].astype(F32)

        for end in ("_top", "_low"):
            blocks = [None] * (total // 8)
            for m in range(tile.nx):
                for key, c, first, count, at in placed:
                    place = at + m * per_plane
                    while count:
                        slot, some = place % 8, min(count, 8 - place % 8)
                        from_row = first if end == "_low" else 8 - first - some
                        if end == "_top" and some < count:
                            from_row = 8 - first - count
                        block = rows_of(key, c, m, end)
                        moved = rolled(block, slot - from_row, 0) if slot != from_row else block
                        old = blocks[place // 8]
                        blocks[place // 8] = (
                            moved if old is None else jnp.where(sub >= slot, moved, old)
                        )
                        place, count, first = place + some, count - some, first + some
            for i, block in enumerate(blocks):
                rows = pl.ds(8 * i, 8)
                if end == "_top":
                    r["even"][rows, :] = block
                    r["odd"][rows, :] = block
                else:
                    r["even"][rows, :] = jnp.where(odd, block, r["even"][rows, :])
                    r["odd"][rows, :] = jnp.where(odd, r["odd"][rows, :], block)

    ins = {key + "_hbm": value for key, value in raw.items()}
    spaces = {key: pltpu.HBM for key in ins}
    return run_kernel(
        body, ins, outs, spaces=spaces, copies=len(raw), name="pack_edges", flops=10**6
    )


def halo_block(tile, r, key, c, m):
    placed, per_plane = edge_rows()
    odd = is_odd("gy") == 1
    sub = lax.broadcasted_iota(jnp.int32, (8, tile.nz), 0)
    result = jnp.zeros((8, tile.nz), F32)
    for name, part, first, count, at in placed:
        if (name, part) != (key, c):
            continue
        place = at + m * per_plane
        slot = place % 8
        assert slot + count <= 8
        rows = pl.ds(place - slot, 8)
        even_got, odd_got = r["got_even"][rows, :], r["got_odd"][rows, :]
        upper = jnp.where(odd, odd_got, even_got)
        lower = jnp.where(odd, even_got, odd_got)
        upper = rolled(upper, first - slot, 0) if slot != first else upper
        bottom = 8 - first - count
        lower = rolled(lower, bottom - slot, 0) if slot != bottom else lower
        result = jnp.where((sub >= first) & (sub < first + count), upper, result)
        result = jnp.where((sub >= bottom) & (sub < bottom + count), lower, result)
    return result


def angle_tables(rows):
    level = lax.broadcasted_iota(jnp.int32, (rows, LANES), 1).astype(F32)
    theta = level * (0.5 * math.pi / LEVELS)
    azimuth = level * (2.0 * math.pi / LEVELS)
    sin_t, cos_t, sin_p, cos_p = jnp.sin(theta), jnp.cos(theta), jnp.sin(azimuth), jnp.cos(azimuth)
    return (
        sin_t * sin_t,
        0.5 * sin_t * cos_t,
        cos_t * cos_t,
        cos_p * cos_p,
        sin_p * sin_p,
        0.5 * sin_p * cos_p,
        sin_p,
        cos_p,
    )


def store_weights(out, m, rows, j, tables, sign, velocity, eps, delta, tilt, azimuth):
    def look(table, level):
        return jnp.take_along_axis(table, level, axis=1)

    sin2_t, sincos_t, cos2_t = (look(tables[k], tilt) for k in range(3))
    cos2_p, sin2_p, sincos_p, sin_p, cos_p = (look(tables[k], azimuth) for k in range(3, 8))
    speed_sq = velocity * velocity
    root = jnp.sqrt(1.0 + 2.0 * delta)
    values = (
        sin2_t * cos2_p,
        sin2_t * sin2_p,
        cos2_t,
        sign * (sin2_t * sincos_p),
        sincos_t * sin_p,
        sign * (sincos_t * cos_p),
        speed_sq * (1.0 + 2.0 * eps),
        speed_sq * root,
        speed_sq,
    )
    for k, value in enumerate(values):
        out[k, m, rows, lanes_of(j)] = value


def x_sign():
    return 1.0 - 2.0 * is_odd("gx").astype(F32)


def own_state(tile, raw, forward):
    coefs = ("velocity", "eps", "delta", "tilt", "azimuth")

    def body(r):
        copy = pltpu.make_async_copy(r["forward_hbm"], r["forward"], r["done"].at[0])
        copy.start()
        tables = angle_tables(8)
        sign = x_sign()

        def plane(m, _):
            here = tile.place(m)
            for j in range(tile.nj):
                for start in range(0, tile.ny, 8):
                    rows = pl.ds(start, 8)
                    store_weights(
                        r["w"], m, rows, j, tables, sign,
                        *(r[key][here, rows, lanes_of(j)] for key in coefs),
                    )
            return 0

        lax.fori_loop(0, tile.nx, plane, 0)
        copy.wait()

    ins = {key: raw[key] for key in coefs}
    ins["forward_hbm"] = forward
    outs = {"w": (9, tile.nx, tile.ny, tile.nz), "forward": (forward.shape, forward.dtype)}
    return run_kernel(
        body, ins, outs, spaces={"forward_hbm": pltpu.HBM}, copies=1, name="own_state",
        flops=3 * 10**6,
    )


def surface_load(tile, cell, count, trace, after):
    channels = cell.shape[1]
    width = tile.ny * tile.gy

    def body(r):
        start_x = lax.axis_index("gx") * tile.nx
        start_y = lax.axis_index("gy") * tile.ny
        cell_here = r["cell"][...]
        slots = lax.broadcasted_iota(jnp.int32, (1, channels), 1)
        live = slots < r["count"][0]
        if width & (width - 1) == 0:
            row_of = cell_here & (width - 1)
        else:
            row_of = lax.rem(cell_here, jnp.full_like(cell_here, width))
        place = lax.broadcasted_iota(jnp.int32, (tile.rows, 1), 0)
        place = jnp.where(place >= tile.ny + HALO, place - tile.rows, place) + start_y
        onehot = jnp.where(row_of == place, 1.0, 0.0)
        first = lax.broadcasted_iota(jnp.int32, (tile.rows, LANES), 1) == 0
        pad = jnp.zeros((LANES - tile.steps, channels), F32)
        trace_here = r["trace"][0]
        for m in range(tile.nx):
            low = (start_x + tile.place(m)) * width
            inside = live & (cell_here >= low) & (cell_here < low + width)
            load = jnp.concatenate([jnp.where(inside, trace_here, 0.0), pad], axis=0)
            columns = lax.dot_general(
                onehot, load, (((1,), (1,)), ((), ())),
                precision=lax.Precision.HIGHEST, preferred_element_type=F32,
            )
            for t in range(tile.steps):
                column = columns if t == 0 else rolled(columns, -t, 1)
                r["surface"][t, m] = jnp.where(first, column, 0.0)

    ins = {"cell": cell, "count": count, "trace": trace, "after": after}
    outs = {"surface": (tile.steps, tile.nx, tile.rows, LANES)}
    out = run_kernel(
        body, ins, outs, spaces={"count": pltpu.SMEM}, name="surface_load", flops=2 * 10**6
    )
    return out["surface"]


def halo_state(tile, got_even, got_odd, after):
    outs = {"uh": (4, tile.nx, 8, tile.nz), "wh": (9, tile.nx, 8, tile.nz), "near": (2, 8, tile.nz)}
    if tile.far:
        outs["far"] = outs["near"]

    def body(r):
        tables = angle_tables(8)
        sign = x_sign()
        for m in range(tile.nx):
            for item, (key, c) in enumerate(ITEMS[:4]):
                block = halo_block(tile, r, key, c, m)
                r["uh"][item, m] = block
                if item < 2 and m == tile.nx - 1:
                    r["near"][c] = block
                if item < 2 and m == 0 and tile.far:
                    r["far"][c] = block
            coefs = [halo_block(tile, r, key, c, m) for key, c in ITEMS[4:]]
            for j in range(tile.nj):
                part = [value[:, j * LANES : (j + 1) * LANES] for value in coefs]
                store_weights(
                    r["wh"], m, pl.ds(0, 8), j, tables, sign, *part[:3],
                    part[3].astype(jnp.int32), part[4].astype(jnp.int32),
                )

    ins = {"got_even": got_even, "got_odd": got_odd, "after": after}
    return run_kernel(body, ins, outs, name="halo_state", flops=10**6)


class Stage:
    def __init__(self, tile, state, ops, pieces, name, after=None):
        self.tile, self.state, self.ops, self.pieces, self.name = tile, state, ops, pieces, name
        self.ins, self.outs, self.scratch = {}, {}, {}
        if after is not None:
            self.ins["after"] = after

    def need(self, key):
        if key not in self.outs and key not in self.scratch:
            self.ins[key] = self.state[key]

    def run(self):
        tile = self.tile
        for t, m in self.ops:
            last = t == tile.steps - 1
            for key in ("w", "forward"):
                self.need(key)
            for k in (m - 1, m, m + 1):
                if k == -1 and not tile.far:
                    continue
                if k in (-1, tile.nx):
                    key = "xf" if k == -1 else "xn"
                    self.need((key, t))
                    if t == 0:
                        self.need((key + "h", t))
                elif t == 0:
                    for key in ("now", "uh"):
                        self.need(key)
                else:
                    self.need(("u", t, k))
            if t <= 1:
                for key in ("before" if t == 0 else "now", "uh"):
                    self.need(key)
            else:
                self.need(("u", t - 1, m))
            if not last:
                self.need("wh")
            self.need("surface")
            if t > 0:
                self.need(("g", t - 1, m))
            rows = tile.ny if last else tile.rows
            self.outs[("u", t + 1, m)] = (2, rows, tile.nz)
            total = (tile.nj, 3, tile.ny, LANES)
            if last and any(m in planes for planes in self.pieces):
                self.scratch[("g", t, m)] = pltpu.VMEM(total, F32)
            else:
                self.outs[("g", t, m)] = total
        for planes in self.pieces:
            for m in planes:
                self.need(("g", tile.steps - 1, m))
            block = (len(planes), 3, tile.ny, tile.nz // tile.src)
            if self.halved(planes):
                self.outs[("keep", planes)] = (2, *block)
                self.outs[("send", planes)] = (2, *block)
            else:
                for k in range(tile.src):
                    self.outs[("s", planes, k)] = block
        flops = len(self.ops) * 2 * 10**6 + 10**5
        out = run_kernel(self.body, self.ins, self.outs, self.scratch, name=self.name, flops=flops)
        self.state.update(out)

    def body(self, r):
        tile = self.tile
        for t, m in self.ops:
            self.update(r, t, m)
        me = lax.axis_index("src")
        per = tile.nj // tile.src
        for planes in self.pieces:
            for i, m in enumerate(planes):
                for k in range(tile.src):
                    owner = jnp.bitwise_xor(me, k)
                    if self.halved(planes):
                        target = r[("send" if k % 2 else "keep", planes)].at[k // 2]
                    else:
                        target = r[("s", planes, k)]
                    for part in range(per):
                        target[i, :, :, lanes_of(part)] = r[("g", tile.steps - 1, m)][
                            owner * per + part
                        ]

    def halved(self, planes):
        return self.tile.src == 4 and self.tile.nx - 1 not in planes

    def field(self, r, t, m, c, j):
        tile, lanes = self.tile, lanes_of(j)
        if m == -1 and not tile.far:
            return None
        if m in (-1, tile.nx):
            key = "xf" if m == -1 else "xn"
            block = r[(key, t)][c, :, lanes]
            return jnp.concatenate([block, r[(key + "h", t)][c, :, lanes]], axis=0) if t == 0 else block
        if t > 0:
            return r[("u", t, m)][c, :, lanes]
        ref, item = (r["now"], c) if t == 0 else (r["before"], 2 + c)
        return jnp.concatenate(
            [ref[0, c, tile.place(m), :, lanes], r["uh"][item, m, :, lanes]], axis=0
        )

    def update(self, r, t, m):
        tile = self.tile
        last = t == tile.steps - 1
        rows = tile.ny if last else tile.rows
        lane = lax.broadcasted_iota(jnp.int32, (tile.rows, LANES), 1)
        at_first, at_last = lane == 0, lane == LANES - 1

        def weight(k, j):
            own = r["w"][k, m, :, lanes_of(j)]
            return own if last else jnp.concatenate([own, r["wh"][k, m, :, lanes_of(j)]], axis=0)

        centers, halves = [], []
        for c in range(2):
            center = [self.field(r, t, m, c, j) for j in range(tile.nj)]
            total_x, diff_x = [], []
            for j in range(tile.nj):
                above, below = self.field(r, t, m + 1, c, j), self.field(r, t, m - 1, c, j)
                total_x.append(above if below is None else above + below)
                diff_x.append(above if below is None else above - below)
            centers.append(center)
            halves.append((total_x, diff_x))

        def deeper(blocks):
            moved = [rolled(block, -1, 1) for block in blocks] + [0.0]
            return [jnp.where(at_last, moved[j + 1], moved[j]) for j in range(tile.nj)]

        def shallower(blocks):
            moved = [rolled(block, 1, 1) for block in blocks] + [0.0]
            return [jnp.where(at_first, moved[j - 1], moved[j]) for j in range(tile.nj)]

        shifted = []
        for c in range(2):
            diff_x = halves[c][1]
            shifted.append(
                (deeper(centers[c]), shallower(centers[c]), deeper(diff_x), shallower(diff_x))
            )

        def both(block):
            return rolled(block, -1, 0)[:rows], rolled(block, 1, 0)[:rows]

        for j in range(tile.nj):
            weights = [weight(k, j) for k in range(6)]
            results = []
            for c in range(2):
                center = centers[c][j]
                total_x, diff_x = halves[c][0][j], halves[c][1][j]
                below, above, diff_below, diff_above = (part[j] for part in shifted[c])
                total_z, slope_z = (below + above)[:rows], below - above
                mixed_xz = (diff_below - diff_above)[:rows]
                up, down = both(center)
                total_y = up + down
                up, down = both(diff_x)
                mixed_xy = up - down
                up, down = both(slope_z)
                mixed_yz = up - down
                total_x, center = total_x[:rows], center[:rows]
                axial = (
                    weights[0] * total_x + weights[1] * total_y + weights[2] * total_z
                    + weights[3] * mixed_xy + weights[4] * mixed_yz + weights[5] * mixed_xz
                )
                if c == 0:
                    results.append(total_x + total_y + total_z - 4.0 * center - axial)
                else:
                    results.append(axial - 2.0 * center)
            horiz, axial = results
            stretched, rooted, speed_sq = (weight(k, j) for k in range(6, 9))
            before = [self.field(r, t - 1, m, c, j)[:rows] for c in range(2)]
            new_p = (
                2.0 * centers[0][j][:rows] - before[0] + stretched * horiz + rooted * axial
            )
            new_q = 2.0 * centers[1][j][:rows] - before[1] + rooted * horiz + speed_sq * axial
            if j == 0:
                new_p = new_p + r["surface"][t, m][:rows]
            r[("u", t + 1, m)][0, :, lanes_of(j)] = new_p
            r[("u", t + 1, m)][1, :, lanes_of(j)] = new_q
            here = tile.place(m)
            forward_p = r["forward"][t, 0, 0, here, :, lanes_of(j)].astype(F32)
            forward_q = r["forward"][t, 0, 1, here, :, lanes_of(j)].astype(F32)
            horiz, axial = horiz[: tile.ny], axial[: tile.ny]
            terms = (
                forward_p * horiz,
                forward_p * axial + forward_q * horiz,
                forward_q * axial,
            )
            for k, term in enumerate(terms):
                if t > 0:
                    term = term + r[("g", t - 1, m)][j, k]
                r[("g", t, m)][j, k] = term


def xor_swap(tile, block, k):
    return lax.ppermute(block, "src", [(i, i ^ k) for i in range(tile.src)])


def add_halves(keep, got):
    block = keep.shape[1:]

    def body(r):
        r["own"][...] = r["keep"][0] + r["got"][0]
        r["passed"][...] = r["keep"][1] + r["got"][1]

    out = run_kernel(
        body, {"keep": keep, "got": got}, {"own": block, "passed": block}, name="add_halves",
        flops=10**5,
    )
    return out["own"], out["passed"]


def combine(tile, state, pieces):
    depth = tile.nz // tile.src
    ins = {key: state[key] for key in ("velocity", "eps", "delta")}
    for planes in pieces:
        ins[("s", planes, 0)] = state[("s", planes, 0)]
        for k in range(1, tile.src):
            if ("r", planes, k) in state:
                ins[("r", planes, k)] = state[("r", planes, k)]
    shape = (tile.nx, tile.ny, depth)

    def body(r):
        lanes = pl.ds(pl.multiple_of(lax.axis_index("src") * depth, LANES), depth)
        for planes in pieces:
            for i, m in enumerate(planes):
                here = tile.place(m)
                sums = []
                for item in range(3):
                    total = r[("s", planes, 0)][i, item]
                    for k in range(1, tile.src):
                        if ("r", planes, k) in r:
                            total = total + r[("r", planes, k)][i, item]
                    sums.append(total)
                velocity = r["velocity"][here, :, lanes]
                root = jnp.sqrt(1.0 + 2.0 * r["delta"][here, :, lanes])
                stretch = 1.0 + 2.0 * r["eps"][here, :, lanes]
                speed_sq = velocity * velocity
                r["gv"][here] = 2.0 * velocity * (stretch * sums[0] + root * sums[1] + sums[2])
                r["ge"][here] = 2.0 * speed_sq * sums[0]
                r["gd"][here] = speed_sq / root * sums[1]

    out = run_kernel(body, ins, {"gv": shape, "ge": shape, "gd": shape}, name="combine", flops=10**6, final=True)
    return out["gv"], out["ge"], out["gd"]


def final_fields(tile, state):
    keys = [("u", tile.steps, m) for m in range(tile.nx)]

    def body(r):
        for m, key in enumerate(keys):
            for c in range(2):
                r["out"][0, c, tile.place(m)] = r[key][c]

    outs = {"out": (1, 2, tile.nx, tile.ny, tile.nz)}
    out = run_kernel(
        body, {key: state[key] for key in keys}, outs, name="final_fields", flops=10**6, final=True
    )
    return out["out"]


def on_device(
    mesh,
    adjoint_now,
    adjoint_before,
    forward_field,
    velocity,
    thomsen_eps,
    thomsen_delta,
    tilt_level,
    azimuth_level,
    channel_cell,
    channel_count,
    residual_trace,
):
    tile = Tile(mesh, velocity, forward_field.shape[0])
    raw = {
        "now": adjoint_now,
        "before": adjoint_before,
        "velocity": velocity,
        "eps": thomsen_eps,
        "delta": thomsen_delta,
        "tilt": tilt_level,
        "azimuth": azimuth_level,
    }
    edges = pack_edges(tile, raw)
    state = {key: edges[key] for key in raw}

    def exchange(key, t, near, far):
        state[("xn" + key, t)] = swap(near, "gx", tile.gx, 0)
        if tile.far:
            state[("xf" + key, t)] = swap(far, "gx", tile.gx, 1)

    exchange("", 0, edges["near"], edges.get("far"))
    got_odd = swap(edges["odd"], "gy", tile.gy, 1)
    got_even = swap(edges["even"], "gy", tile.gy, 0)
    state.update(own_state(tile, state, forward_field))
    halo = halo_state(tile, got_even, got_odd, state["w"])
    state["uh"], state["wh"] = halo["uh"], halo["wh"]
    exchange("h", 0, halo["near"], halo.get("far"))
    state["surface"] = surface_load(
        tile, channel_cell, channel_count, residual_trace, halo["uh"]
    )

    ops = [(t, m) for t in range(tile.steps) for m in range(tile.nx)]
    last = tile.steps - 1
    ready = {m: tile.phase(last, m) for m in range(tile.nx)}
    issue = {}
    for m in range(tile.nx):
        issue.setdefault(1 if ready[m] <= 1 else tile.steps, []).append(m)
    pieces = []
    edge = {tile.nx - 1} | ({0} if tile.far else set())
    for phase in range(tile.steps + 1):
        mine = [op for op in ops if tile.phase(*op) == phase]
        after = state.get("token")
        front = [op for op in mine if phase > 0 and op[0] == phase - 1 and op[1] in edge]
        bulk = [op for op in mine if op not in front]
        done = [tuple(issue[phase])] if phase in issue else []
        pieces += done
        if phase == tile.steps:
            front, bulk = mine, []
        if front:
            Stage(tile, state, front, [] if bulk else done, f"front_{phase}", after).run()
            if phase < tile.steps:
                exchange("", phase, state[("u", phase, tile.nx - 1)], state.get(("u", phase, 0)))
        if bulk:
            Stage(tile, state, bulk, done, f"bulk_{phase}").run()
            state["token"] = state[("g", *next(op for op in bulk if ("g", *op) in state))]
        for planes in done:
            if ("send", planes) in state:
                got = xor_swap(tile, state[("send", planes)], 1)
                state[("s", planes, 0)], passed = add_halves(state[("keep", planes)], got)
                state[("r", planes, 2)] = xor_swap(tile, passed, 2)
            else:
                for k in range(1, tile.src):
                    state[("r", planes, k)] = xor_swap(tile, state[("s", planes, k)], k)
    following = final_fields(tile, state)
    return (following, *combine(tile, state, pieces))


def solution(mesh):
    placed = (
        P("src", None, "gx", "gy", None),
        P("src", None, "gx", "gy", None),
        P(None, "src", None, "gx", "gy", None),
        P("gx", "gy", None),
        P("gx", "gy", None),
        P("gx", "gy", None),
        P("gx", "gy", None),
        P("gx", "gy", None),
        P("src", None),
        P("src"),
        P("src", None, None),
    )

    def program(*args):
        return on_device(mesh, *args)

    return jax.shard_map(
        program,
        mesh=mesh,
        in_specs=placed,
        out_specs=(
            P("src", None, "gx", "gy", None),
            P("gx", "gy", "src"),
            P("gx", "gy", "src"),
            P("gx", "gy", "src"),
        ),
        check_vma=False,
    )
```

```python
import math

import jax
import jax.numpy as jnp
from jax import lax
from jax.experimental import pallas as pl
from jax.experimental.pallas import tpu as pltpu
from jax.sharding import PartitionSpec as P

LEVELS = 32
LANES = 128
HALO = 4
VMEM_LIMIT = 8 * 1024 * 1024
F32 = jnp.float32


def run_kernel(body, ins, outs, scratch=None, spaces=None, copies=0, name=None, flops=0, final=False):
    scratch, spaces = scratch or {}, spaces or {}
    names = list(ins) + list(outs) + list(scratch) + ["done"]
    ins = {
        key: pltpu.with_memory_space_constraint(value, pltpu.HBM)
        if spaces.get(key) == pltpu.HBM
        else value
        for key, value in ins.items()
    }

    def kernel(*refs):
        body(dict(zip(names, refs)))

    results = pl.pallas_call(
        kernel,
        name=name,
        out_shape=[
            jax.ShapeDtypeStruct(shape, F32) if final else pltpu.VMEM(shape, kind)
            for shape, kind in (
                entry if isinstance(entry[0], tuple) else (entry, F32) for entry in outs.values()
            )
        ],
        in_specs=[
            pl.BlockSpec(memory_space=spaces.get(key, pltpu.VMEM)) for key in ins
        ],
        out_specs=[pl.BlockSpec(memory_space=pltpu.VMEM)] * len(outs),
        scratch_shapes=list(scratch.values())
        + [pltpu.SemaphoreType.DMA((copies,))] * (copies > 0),
        compiler_params=pltpu.CompilerParams(vmem_limit_bytes=VMEM_LIMIT),
        cost_estimate=pl.CostEstimate(flops=flops, bytes_accessed=flops // 8, transcendentals=0),
    )(*ins.values())
    return dict(zip(outs, results))


def pair_swaps(count, first):
    pairs = []
    for low in range(first, count - 1, 2):
        pairs += [(low, low + 1), (low + 1, low)]
    return pairs


def swap(block, axis, count, first):
    return lax.ppermute(block, axis, pair_swaps(count, first))


def swap_rows(tile, block, first):
    pairs = dict(pair_swaps(tile.gy, first))
    across = dict(pair_swaps(tile.src, 0))
    joint = []
    for s in range(tile.src):
        for y in range(tile.gy):
            target = (s, pairs[y]) if y in pairs else (across.get(s, s), y)
            joint.append((s * tile.gy + y, target[0] * tile.gy + target[1]))
    return lax.ppermute(block, ("src", "gy"), joint)


def lanes_of(j):
    return pl.ds(j * LANES, LANES)


def is_odd(axis):
    return lax.rem(lax.axis_index(axis), 2)


class Tile:
    def __init__(self, mesh, velocity, steps):
        self.nx, self.ny, self.nz = velocity.shape
        self.steps = steps
        self.nj = self.nz // LANES
        self.rows = self.ny + 2 * HALO
        self.gx, self.gy, self.src = mesh.shape["gx"], mesh.shape["gy"], mesh.shape["src"]
        self.far = self.gx > 2
        self.plan, self.second = self.reduction()

    def reduction(self):
        last = self.steps - 1
        ready = [self.phase(last, m) for m in range(self.nx)]
        if self.src == 4 and ready == [0, 1, 2, 3]:
            return {(0, 1): (1, "a"), (2,): (2, "b"), (3,): (3, None)}, {"a": 2, "b": 3}
        pieces = {}
        for m, phase in enumerate(ready):
            pieces.setdefault(phase, []).append(m)
        return {tuple(planes): (phase, None) for phase, planes in pieces.items()}, {}

    def place(self, m):
        return m + is_odd("gx") * (self.nx - 1 - 2 * m)

    def phase(self, t, m):
        if m == self.nx or m == -1:
            return t + 2 if (m == self.nx or self.far) else 0
        if t < 0:
            return 0
        return max(self.phase(t - 1, k) for k in (m - 1, m, m + 1))

    def edge(self, m):
        return m == self.nx - 1 or (m == 0 and self.far)


def rolled(value, by, axis):
    return pltpu.roll(value, by % value.shape[axis], axis)


ITEMS = [("now", 0), ("now", 1), ("before", 0), ("before", 1)] + [
    (key, 0) for key in ("velocity", "eps", "delta", "tilt", "azimuth")
]


def edge_rows(tile):
    placed = [
        (item, m, 0, 2, 2 * (item * tile.nx + m)) for item in range(len(ITEMS)) for m in range(tile.nx)
    ]
    base = 2 * len(ITEMS) * tile.nx
    placed += [(item, m, 2, 1, base + item * tile.nx + m) for item in range(2) for m in range(tile.nx)]
    return placed, base + 2 * tile.nx


def pack_edges(tile, raw):
    placed, total = edge_rows(tile)
    assert tile.nx % 4 == 0
    outs = {"even": (total, tile.nz), "odd": (total, tile.nz), "near": (2, tile.ny, tile.nz)}
    if tile.far:
        outs["far"] = outs["near"]
    outs.update({key: (value.shape, value.dtype) for key, value in raw.items()})

    def body(r):
        copies = {}
        for i, key in enumerate(raw):
            copies[key] = pltpu.make_async_copy(r[key + "_hbm"], r[key], r["done"].at[i])
            copies[key].start()
        odd = is_odd("gy") == 1
        sub = lax.broadcasted_iota(jnp.int32, (8, tile.nz), 0)
        blocks = {}
        for item, m, first, count, place in placed:
            key, c = ITEMS[item]
            if key in copies:
                copies.pop(key).wait()
                if key == "now":
                    for part in range(2):
                        r["near"][part] = r["now"][0, part, tile.place(tile.nx - 1)]
                        if tile.far:
                            r["far"][part] = r["now"][0, part, tile.place(0)]
            here, slot = tile.place(m), place % 8
            ref = r[key].at[0, c] if key in ("now", "before") else r[key]
            for end, start, from_row in (("top", tile.ny - 8, 8 - first - count), ("low", 0, first)):
                block = ref[here, pl.ds(start, 8), :].astype(F32)
                moved = rolled(block, slot - from_row, 0) if slot != from_row else block
                old = blocks.get(end)
                blocks[end] = moved if slot == 0 else jnp.where(sub >= slot, moved, old)
            if slot + count == 8:
                rows = pl.ds(place - slot, 8)
                r["even"][rows, :] = jnp.where(odd, blocks["low"], blocks["top"])
                r["odd"][rows, :] = jnp.where(odd, blocks["top"], blocks["low"])

    ins = {key + "_hbm": value for key, value in raw.items()}
    spaces = {key: pltpu.HBM for key in ins}
    return run_kernel(
        body, ins, outs, spaces=spaces, copies=len(raw), name="pack_edges", flops=10**6
    )


def halo_block(tile, r, item, m):
    odd = is_odd("gy") == 1
    has_upper = lax.axis_index("gy") < tile.gy - 1
    has_lower = lax.axis_index("gy") > 0
    sub = lax.broadcasted_iota(jnp.int32, (8, tile.nz), 0)
    result = jnp.zeros((8, tile.nz), F32)
    for i, plane, first, count, place in edge_rows(tile)[0]:
        if (i, plane) != (item, m):
            continue
        slot = place % 8
        rows = pl.ds(place - slot, 8)
        even_got, odd_got = r["got_even"][rows, :], r["got_odd"][rows, :]
        upper = jnp.where(odd, odd_got, even_got)
        lower = jnp.where(odd, even_got, odd_got)
        upper = rolled(upper, first - slot, 0) if slot != first else upper
        bottom = 8 - first - count
        lower = rolled(lower, bottom - slot, 0) if slot != bottom else lower
        result = jnp.where((sub >= first) & (sub < first + count) & has_upper, upper, result)
        result = jnp.where((sub >= bottom) & (sub < bottom + count) & has_lower, lower, result)
    return result


def angle_tables(rows):
    level = lax.broadcasted_iota(jnp.int32, (rows, LANES), 1).astype(F32)
    theta = level * (0.5 * math.pi / LEVELS)
    azimuth = level * (2.0 * math.pi / LEVELS)
    sin_t, cos_t, sin_p, cos_p = jnp.sin(theta), jnp.cos(theta), jnp.sin(azimuth), jnp.cos(azimuth)
    return sin_t, cos_t, sin_p, cos_p


def store_weights(out, m, rows, j, tables, sign, velocity, eps, delta, tilt, azimuth):
    def look(table, level):
        return jnp.take_along_axis(table, level, axis=1)

    sin_t, cos_t = look(tables[0], tilt), look(tables[1], tilt)
    sin_p, cos_p = look(tables[2], azimuth), look(tables[3], azimuth)
    sin2_t, half_t = sin_t * sin_t, 0.5 * sin_t * cos_t
    speed_sq = velocity * velocity
    root = jnp.sqrt(1.0 + 2.0 * delta)
    values = (
        sin2_t * (cos_p * cos_p),
        sin2_t * (sin_p * sin_p),
        cos_t * cos_t,
        (0.5 * sign) * (sin2_t * (sin_p * cos_p)),
        half_t * sin_p,
        sign * (half_t * cos_p),
        speed_sq * (1.0 + 2.0 * eps),
        speed_sq * root,
        speed_sq,
    )
    for k, value in enumerate(values):
        out[k, m, rows, lanes_of(j)] = value


def x_sign():
    return 1.0 - 2.0 * is_odd("gx").astype(F32)


def own_state(tile, raw, forward):
    coefs = ("velocity", "eps", "delta", "tilt", "azimuth")

    def body(r):
        copy = pltpu.make_async_copy(r["forward_hbm"], r["forward"], r["done"].at[0])
        copy.start()
        tables = angle_tables(8)
        sign = x_sign()

        def plane(m, _):
            here = tile.place(m)
            for j in range(tile.nj):
                for start in range(0, tile.ny, 8):
                    rows = pl.ds(start, 8)
                    store_weights(
                        r["w"], m, rows, j, tables, sign,
                        *(r[key][here, rows, lanes_of(j)] for key in coefs),
                    )
            return 0

        lax.fori_loop(0, tile.nx, plane, 0)
        copy.wait()

    ins = {key: raw[key] for key in coefs}
    ins["forward_hbm"] = forward
    outs = {"w": (9, tile.nx, tile.ny, tile.nz), "forward": (forward.shape, forward.dtype)}
    return run_kernel(
        body, ins, outs, spaces={"forward_hbm": pltpu.HBM}, copies=1, name="own_state",
        flops=3 * 10**6,
    )


def surface_load(tile, cell, count, trace, after):
    channels = cell.shape[1]
    width = tile.ny * tile.gy

    def body(r):
        start_x = lax.axis_index("gx") * tile.nx
        start_y = lax.axis_index("gy") * tile.ny
        cell_here = r["cell"][...]
        slots = lax.broadcasted_iota(jnp.int32, (1, channels), 1)
        live = slots < r["count"][...].reshape(1, 1)
        if width & (width - 1) == 0:
            row_of = cell_here & (width - 1)
        else:
            row_of = lax.rem(cell_here, jnp.full_like(cell_here, width))
        place = lax.broadcasted_iota(jnp.int32, (tile.rows, 1), 0)
        place = jnp.where(place >= tile.ny + HALO, place - tile.rows, place) + start_y
        onehot = jnp.where(row_of == place, 1.0, 0.0)
        first = lax.broadcasted_iota(jnp.int32, (tile.rows, LANES), 1) == 0
        pad = jnp.zeros((8 - tile.steps, channels), F32)
        trace_here = r["trace"][0]
        loads = []
        for m in range(tile.nx):
            low = (start_x + tile.place(m)) * width
            inside = live & (cell_here >= low) & (cell_here < low + width)
            loads += [jnp.where(inside, trace_here, 0.0), pad]
        rest, parts = jnp.concatenate(loads, axis=0), []
        for _ in range(3):
            part = rest.astype(jnp.bfloat16)
            rest = rest - part.astype(F32)
            parts.append(part.astype(F32))
        group = 8 * tile.nx
        if 3 * group < LANES:
            parts.append(jnp.zeros((LANES - 3 * group, channels), F32))
        columns = lax.dot_general(
            onehot.astype(jnp.bfloat16), jnp.concatenate(parts, axis=0).astype(jnp.bfloat16),
            (((1,), (1,)), ((), ())), preferred_element_type=F32,
        )
        columns = columns + (rolled(columns, -group, 1) + rolled(columns, -2 * group, 1))
        for m in range(tile.nx):
            for t in range(tile.steps):
                column = rolled(columns, -8 * m - t, 1) if m + t else columns
                r["surface"][t, m] = jnp.where(first, column, 0.0)

    assert tile.steps <= 8 and 24 * tile.nx <= LANES
    ins = {"cell": cell, "count": count, "trace": trace, "after": after}
    outs = {"surface": (tile.steps, tile.nx, tile.rows, LANES)}
    out = run_kernel(body, ins, outs, name="surface_load", flops=2 * 10**6)
    return out["surface"]


def halo_state(tile, got_even, got_odd, after):
    outs = {"uh": (4, tile.nx, 8, tile.nz), "wh": (9, tile.nx, 8, tile.nz), "near": (2, 8, tile.nz)}
    if tile.far:
        outs["far"] = outs["near"]

    def body(r):
        tables = angle_tables(8)
        sign = x_sign()
        for m in range(tile.nx):
            for item in range(4):
                block = halo_block(tile, r, item, m)
                r["uh"][item, m] = block
                if item < 2 and m == tile.nx - 1:
                    r["near"][item] = block
                if item < 2 and m == 0 and tile.far:
                    r["far"][item] = block
            coefs = [halo_block(tile, r, item, m) for item in range(4, 9)]
            for j in range(tile.nj):
                part = [value[:, j * LANES : (j + 1) * LANES] for value in coefs]
                store_weights(
                    r["wh"], m, pl.ds(0, 8), j, tables, sign, *part[:3],
                    part[3].astype(jnp.int32), part[4].astype(jnp.int32),
                )

    ins = {"got_even": got_even, "got_odd": got_odd, "after": after}
    return run_kernel(body, ins, outs, name="halo_state", flops=10**6)


class Stage:
    def __init__(self, tile, state, ops, pieces, name, after=None):
        self.tile, self.state, self.ops, self.pieces, self.name = tile, state, ops, pieces, name
        self.ins, self.outs, self.scratch = {}, {}, {}
        if after is not None:
            self.ins["after"] = after

    def need(self, key):
        if key not in self.outs and key not in self.scratch:
            self.ins[key] = self.state[key]

    def run(self):
        tile = self.tile
        for t, m in self.ops:
            last = t == tile.steps - 1
            for key in ("w", "forward"):
                self.need(key)
            for k in (m - 1, m, m + 1):
                if k == -1 and not tile.far:
                    continue
                if k in (-1, tile.nx):
                    key = "xf" if k == -1 else "xn"
                    self.need((key, t))
                    if t == 0:
                        self.need((key + "h", t))
                elif t == 0:
                    for key in ("now", "uh"):
                        self.need(key)
                else:
                    self.need(("u", t, k))
            if t <= 1:
                for key in ("before" if t == 0 else "now", "uh"):
                    self.need(key)
            else:
                self.need(("u", t - 1, m))
            if not last:
                self.need("wh")
            self.need("surface")
            if t > 0:
                self.need(("g", t - 1, m))
            rows = tile.ny if last else tile.rows
            self.outs[("u", t + 1, m)] = (2, rows, tile.nz)
            if not last and tile.edge(m):
                self.outs[("e", t + 1, m)] = (2 * tile.ny + 8, tile.nz)
            total = (tile.nj, 3, tile.ny, LANES)
            if last and any(m in planes for planes in self.pieces):
                self.scratch[("g", t, m)] = pltpu.VMEM(total, F32)
            else:
                self.outs[("g", t, m)] = total
        for planes in self.pieces:
            for m in planes:
                self.need(("g", tile.steps - 1, m))
            block = (len(planes), 3, tile.ny, tile.nz // tile.src)
            if self.halved(planes):
                self.outs[("keep", planes)] = (2, *block)
                self.outs[("send", planes)] = (2, *block)
            else:
                for k in range(tile.src):
                    self.outs[("s", planes, k)] = block
        flops = len(self.ops) * 2 * 10**6 + 10**5
        out = run_kernel(self.body, self.ins, self.outs, self.scratch, name=self.name, flops=flops)
        self.state.update(out)

    def body(self, r):
        tile = self.tile
        for t, m in self.ops:
            self.update(r, t, m)
        me = lax.axis_index("src")
        per = tile.nj // tile.src
        for planes in self.pieces:
            for i, m in enumerate(planes):
                for k in range(tile.src):
                    owner = jnp.bitwise_xor(me, k)
                    if self.halved(planes):
                        target = r[("send" if k % 2 else "keep", planes)].at[k // 2]
                    else:
                        target = r[("s", planes, k)]
                    for part in range(per):
                        target[i, :, :, lanes_of(part)] = r[("g", tile.steps - 1, m)][
                            owner * per + part
                        ]

    def halved(self, planes):
        return self.tile.plan[planes][1] is not None

    def field(self, r, t, m, c, j):
        tile, lanes = self.tile, lanes_of(j)
        if m == -1 and not tile.far:
            return None
        if m in (-1, tile.nx):
            key = "xf" if m == -1 else "xn"
            if t == 0:
                own, halo = r[(key, t)][c, :, lanes], r[(key + "h", t)][c, :, lanes]
            else:
                own = r[(key, t)][pl.ds(c * tile.ny, tile.ny), lanes]
                halo = r[(key, t)][pl.ds(2 * tile.ny, 8), lanes]
                if c == 1:
                    sub = lax.broadcasted_iota(jnp.int32, (8, LANES), 0)
                    halo = jnp.where(sub < HALO, rolled(halo, -2, 0), rolled(halo, 2, 0))
            return jnp.concatenate([own, halo], axis=0)
        if t > 0:
            return r[("u", t, m)][c, :, lanes]
        ref, item = (r["now"], c) if t == 0 else (r["before"], 2 + c)
        return jnp.concatenate(
            [ref[0, c, tile.place(m), :, lanes], r["uh"][item, m, :, lanes]], axis=0
        )

    def update(self, r, t, m):
        tile = self.tile
        last = t == tile.steps - 1
        rows = tile.ny if last else tile.rows
        lane = lax.broadcasted_iota(jnp.int32, (tile.rows, LANES), 1)
        at_first, at_last = lane == 0, lane == LANES - 1

        def weight(k, j):
            own = r["w"][k, m, :, lanes_of(j)]
            return own if last else jnp.concatenate([own, r["wh"][k, m, :, lanes_of(j)]], axis=0)

        centers, halves = [], []
        for c in range(2):
            center = [self.field(r, t, m, c, j) for j in range(tile.nj)]
            total_x, diff_x = [], []
            for j in range(tile.nj):
                above, below = self.field(r, t, m + 1, c, j), self.field(r, t, m - 1, c, j)
                total_x.append(above if below is None else above + below)
                diff_x.append(above if below is None else above - below)
            centers.append(center)
            halves.append((total_x, diff_x))

        def deeper(blocks):
            moved = [rolled(block, -1, 1) for block in blocks] + [0.0]
            return [jnp.where(at_last, moved[j + 1], moved[j]) for j in range(tile.nj)]

        def shallower(blocks):
            moved = [rolled(block, 1, 1) for block in blocks] + [0.0]
            return [jnp.where(at_first, moved[j - 1], moved[j]) for j in range(tile.nj)]

        shifted = []
        for c in range(2):
            diff_x = halves[c][1]
            shifted.append(
                (deeper(centers[c]), shallower(centers[c]), deeper(diff_x), shallower(diff_x))
            )

        def both(block):
            return rolled(block, -1, 0)[:rows], rolled(block, 1, 0)[:rows]

        for j in range(tile.nj):
            weights = [weight(k, j) for k in range(6)]
            results = []
            for c in range(2):
                center = centers[c][j]
                total_x, diff_x = halves[c][0][j], halves[c][1][j]
                below, above, diff_below, diff_above = (part[j] for part in shifted[c])
                total_z, slope_z = (below + above)[:rows], below - above
                mixed_xz = (diff_below - diff_above)[:rows]
                up, down = both(center)
                total_y = up + down
                up, down = both(diff_x)
                mixed_xy = up - down
                up, down = both(slope_z)
                mixed_yz = up - down
                total_x, center = total_x[:rows], center[:rows]
                axial = (
                    weights[0] * total_x + weights[1] * total_y + weights[2] * total_z
                    + weights[3] * mixed_xy + weights[4] * mixed_yz + weights[5] * mixed_xz
                )
                if c == 0:
                    results.append(total_x + total_y + total_z - 4.0 * center - axial)
                else:
                    results.append(axial - 2.0 * center)
            horiz, axial = results
            stretched, rooted, speed_sq = (weight(k, j) for k in range(6, 9))
            before = [self.field(r, t - 1, m, c, j)[:rows] for c in range(2)]
            new_p = (
                2.0 * centers[0][j][:rows] - before[0] + stretched * horiz + rooted * axial
            )
            new_q = 2.0 * centers[1][j][:rows] - before[1] + rooted * horiz + speed_sq * axial
            if j == 0:
                new_p = new_p + r["surface"][t, m][:rows]
            r[("u", t + 1, m)][0, :, lanes_of(j)] = new_p
            r[("u", t + 1, m)][1, :, lanes_of(j)] = new_q
            if ("e", t + 1, m) in r:
                edge, lanes = r[("e", t + 1, m)], lanes_of(j)
                edge[: tile.ny, lanes] = new_p[: tile.ny]
                edge[tile.ny : 2 * tile.ny, lanes] = new_q[: tile.ny]
                sub = lax.broadcasted_iota(jnp.int32, (8, LANES), 0)
                p_rows, q_rows = new_p[tile.ny :], new_q[tile.ny :]
                q_rows = jnp.where(sub < HALO, rolled(q_rows, 2, 0), rolled(q_rows, -2, 0))
                edge[2 * tile.ny :, lanes] = jnp.where((sub < 2) | (sub >= 6), p_rows, q_rows)
            here = tile.place(m)
            forward_p = r["forward"][t, 0, 0, here, :, lanes_of(j)].astype(F32)
            forward_q = r["forward"][t, 0, 1, here, :, lanes_of(j)].astype(F32)
            horiz, axial = horiz[: tile.ny], axial[: tile.ny]
            terms = (
                forward_p * horiz,
                forward_p * axial + forward_q * horiz,
                forward_q * axial,
            )
            for k, term in enumerate(terms):
                if t > 0:
                    term = term + r[("g", t - 1, m)][j, k]
                r[("g", t, m)][j, k] = term


def xor_swap(tile, block, k):
    return lax.ppermute(block, "src", [(i, i ^ k) for i in range(tile.src)])


def add_halves(tile, state, pieces, after):
    ins, outs, count = {"after": after}, {}, 0
    for planes in pieces:
        ins[("keep", planes)], ins[("got", planes)] = state[("keep", planes)], state[("got", planes)]
        outs[("s", planes, 0)] = state[("keep", planes)].shape[1:]
        count += len(planes)
    outs["passed"] = (count, *outs[("s", pieces[0], 0)][1:])

    def body(r):
        at = 0
        for planes in pieces:
            keep, got = r[("keep", planes)], r[("got", planes)]
            r[("s", planes, 0)][...] = keep[0] + got[0]
            r["passed"][at : at + len(planes)] = keep[1] + got[1]
            at += len(planes)

    state.update(run_kernel(body, ins, outs, name="add_halves", flops=10**5))
    passed = xor_swap(tile, state["passed"], 2)
    at = 0
    for planes in pieces:
        state[("r", planes, 2)] = (passed, at)
        at += len(planes)


def combine(tile, state, pieces):
    depth = tile.nz // tile.src
    ins = {key: state[key] for key in ("velocity", "eps", "delta")}
    starts = {}
    for planes in pieces:
        ins[("s", planes, 0)] = state[("s", planes, 0)]
        for k in range(1, tile.src):
            if ("r", planes, k) in state:
                ins[("r", planes, k)], starts[(planes, k)] = state[("r", planes, k)]
    shape = (tile.nx, tile.ny, depth)

    def body(r):
        lanes = pl.ds(pl.multiple_of(lax.axis_index("src") * depth, LANES), depth)
        for planes in pieces:
            for i, m in enumerate(planes):
                here = tile.place(m)
                sums = []
                for item in range(3):
                    total = r[("s", planes, 0)][i, item]
                    for k in range(1, tile.src):
                        if (planes, k) in starts:
                            total = total + r[("r", planes, k)][starts[(planes, k)] + i, item]
                    sums.append(total)
                velocity = r["velocity"][here, :, lanes]
                root = jnp.sqrt(1.0 + 2.0 * r["delta"][here, :, lanes])
                stretch = 1.0 + 2.0 * r["eps"][here, :, lanes]
                speed_sq = velocity * velocity
                r["gv"][here] = 2.0 * velocity * (stretch * sums[0] + root * sums[1] + sums[2])
                r["ge"][here] = 2.0 * speed_sq * sums[0]
                r["gd"][here] = speed_sq / root * sums[1]

    out = run_kernel(body, ins, {"gv": shape, "ge": shape, "gd": shape}, name="combine", flops=10**6, final=True)
    return out["gv"], out["ge"], out["gd"]


def final_fields(tile, state):
    keys = [("u", tile.steps, m) for m in range(tile.nx)]

    def body(r):
        for m, key in enumerate(keys):
            for c in range(2):
                r["out"][0, c, tile.place(m)] = r[key][c]

    outs = {"out": (1, 2, tile.nx, tile.ny, tile.nz)}
    out = run_kernel(
        body, {key: state[key] for key in keys}, outs, name="final_fields", flops=10**6, final=True
    )
    return out["out"]


def on_device(
    mesh,
    adjoint_now,
    adjoint_before,
    forward_field,
    velocity,
    thomsen_eps,
    thomsen_delta,
    tilt_level,
    azimuth_level,
    channel_cell,
    channel_count,
    residual_trace,
):
    tile = Tile(mesh, velocity, forward_field.shape[0])
    raw = {
        "now": adjoint_now,
        "before": adjoint_before,
        "velocity": velocity,
        "eps": thomsen_eps,
        "delta": thomsen_delta,
        "tilt": tilt_level,
        "azimuth": azimuth_level,
    }
    edges = pack_edges(tile, raw)
    state = {key: edges[key] for key in raw}

    def exchange(key, t, near, far):
        state[("xn" + key, t)] = swap(near, "gx", tile.gx, 0)
        if tile.far:
            state[("xf" + key, t)] = swap(far, "gx", tile.gx, 1)

    got_even = swap_rows(tile, edges["even"], 0)
    exchange("", 0, edges["near"], edges.get("far"))
    got_odd = swap_rows(tile, edges["odd"], 1)
    state.update(own_state(tile, state, forward_field))
    state["surface"] = surface_load(
        tile, channel_cell, channel_count, residual_trace, state["w"]
    )
    halo = halo_state(tile, got_even, got_odd, state["surface"])
    state["uh"], state["wh"] = halo["uh"], halo["wh"]
    exchange("h", 0, halo["near"], halo.get("far"))

    ops = [(t, m) for t in range(tile.steps) for m in range(tile.nx)]
    pieces = list(tile.plan)
    for phase in range(tile.steps + 1):
        mine = [op for op in ops if max(tile.phase(*op), op[0] // 2) == phase]
        front = [op for op in mine if phase > 0 and op[0] == phase - 1 and tile.edge(op[1])]
        bulk = [op for op in mine if op not in front]
        done = [planes for planes in pieces if tile.plan[planes][0] == phase]
        if phase == tile.steps:
            front, bulk = mine, []
        if front:
            Stage(tile, state, front, [] if bulk else done, f"front_{phase}", state.get("token")).run()
            state["token"] = state[("u", phase, tile.nx - 1)]
            if phase < tile.steps:
                exchange("", phase, state[("e", phase, tile.nx - 1)], state.get(("e", phase, 0)))
        if bulk:
            Stage(tile, state, bulk, done, f"bulk_{phase}").run()
            state["token"] = state[("u", bulk[0][0] + 1, bulk[0][1])]
        for planes in done:
            if ("send", planes) in state:
                state[("got", planes)] = xor_swap(tile, state[("send", planes)], 1)
                continue
            for k in range(1, tile.src):
                state[("r", planes, k)] = (xor_swap(tile, state[("s", planes, k)], k), 0)
        for name, when in tile.second.items():
            if when == phase:
                carried = [planes for planes in pieces if tile.plan[planes][1] == name]
                add_halves(tile, state, carried, state["token"])
    following = final_fields(tile, state)
    return (following, *combine(tile, state, pieces))


def solution(mesh):
    placed = (
        P("src", None, "gx", "gy", None),
        P("src", None, "gx", "gy", None),
        P(None, "src", None, "gx", "gy", None),
        P("gx", "gy", None),
        P("gx", "gy", None),
        P("gx", "gy", None),
        P("gx", "gy", None),
        P("gx", "gy", None),
        P("src", None),
        P("src"),
        P("src", None, None),
    )

    def program(*args):
        return on_device(mesh, *args)

    return jax.shard_map(
        program,
        mesh=mesh,
        in_specs=placed,
        out_specs=(
            P("src", None, "gx", "gy", None),
            P("gx", "gy", "src"),
            P("gx", "gy", "src"),
            P("gx", "gy", "src"),
        ),
        check_vma=False,
    )
```

```python
import math

import jax
import jax.numpy as jnp
from jax import lax
from jax.experimental import pallas as pl
from jax.experimental.pallas import tpu as pltpu
from jax.sharding import PartitionSpec as P

LEVELS = 32
LANES = 128
HALO = 4
ORDER = (2, 3, 1)
WAVE = (
    {(0, 1): (1, "a"), (2,): (2, "b"), (3,): (3, None)},
    {"a": (2, 2, False), "b": (3, 2, True)},
)
VMEM_LIMIT = 8 * 1024 * 1024
F32 = jnp.float32


def run_kernel(body, ins, outs, scratch=None, spaces=None, copies=0, name=None, flops=0, final=False):
    scratch, spaces = scratch or {}, spaces or {}
    names = list(ins) + list(outs) + list(scratch) + ["done"]
    ins = {
        key: pltpu.with_memory_space_constraint(value, pltpu.HBM)
        if spaces.get(key) == pltpu.HBM
        else value
        for key, value in ins.items()
    }

    def kernel(*refs):
        body(dict(zip(names, refs)))

    results = pl.pallas_call(
        kernel,
        name=name,
        out_shape=[
            jax.ShapeDtypeStruct(shape, F32) if final else pltpu.VMEM(shape, kind)
            for shape, kind in (
                entry if isinstance(entry[0], tuple) else (entry, F32) for entry in outs.values()
            )
        ],
        in_specs=[
            pl.BlockSpec(memory_space=spaces.get(key, pltpu.VMEM)) for key in ins
        ],
        out_specs=[pl.BlockSpec(memory_space=pltpu.VMEM)] * len(outs),
        scratch_shapes=list(scratch.values())
        + [pltpu.SemaphoreType.DMA((copies,))] * (copies > 0),
        compiler_params=pltpu.CompilerParams(vmem_limit_bytes=VMEM_LIMIT),
        cost_estimate=pl.CostEstimate(flops=flops, bytes_accessed=flops // 8, transcendentals=0),
    )(*ins.values())
    return dict(zip(outs, results))


def pair_swaps(count, first):
    pairs = []
    for low in range(first, count - 1, 2):
        pairs += [(low, low + 1), (low + 1, low)]
    return pairs


def swap(block, axis, count, first):
    return lax.ppermute(block, axis, pair_swaps(count, first))


def swap_rows(tile, block, first):
    pairs = dict(pair_swaps(tile.gy, first))
    across = dict(pair_swaps(tile.src, 0))
    joint = []
    for s in range(tile.src):
        for y in range(tile.gy):
            target = (s, pairs[y]) if y in pairs else (across.get(s, s), y)
            joint.append((s * tile.gy + y, target[0] * tile.gy + target[1]))
    return lax.ppermute(block, ("src", "gy"), joint)


def lanes_of(j):
    return pl.ds(j * LANES, LANES)


def is_odd(axis):
    return lax.rem(lax.axis_index(axis), 2)


class Tile:
    def __init__(self, mesh, velocity, steps):
        self.nx, self.ny, self.nz = velocity.shape
        self.steps = steps
        self.nj = self.nz // LANES
        self.rows = self.ny + 2 * HALO
        self.gx, self.gy, self.src = mesh.shape["gx"], mesh.shape["gy"], mesh.shape["src"]
        self.far = self.gx > 2
        self.plan, self.second = self.reduction()

    def reduction(self):
        last = self.steps - 1
        ready = [self.phase(last, m) for m in range(self.nx)]
        if self.src == 4 and ready == [0, 1, 2, 3]:
            return WAVE
        pieces = {}
        for m, phase in enumerate(ready):
            pieces.setdefault(phase, []).append(m)
        return {tuple(planes): (phase, None) for phase, planes in pieces.items()}, {}

    def place(self, m):
        return m + is_odd("gx") * (self.nx - 1 - 2 * m)

    def phase(self, t, m):
        if m == self.nx or m == -1:
            return t + 2 if (m == self.nx or self.far) else 0
        if t < 0:
            return 0
        return max(self.phase(t - 1, k) for k in (m - 1, m, m + 1))

    def edge(self, m):
        return m == self.nx - 1 or (m == 0 and self.far)


def rolled(value, by, axis):
    return pltpu.roll(value, by % value.shape[axis], axis)


ITEMS = [("now", 0), ("now", 1), ("before", 0), ("before", 1)] + [
    (key, 0) for key in ("velocity", "eps", "delta", "tilt", "azimuth")
]


def edge_rows(tile):
    placed = [
        (item, m, 0, 2, 2 * (item * tile.nx + m)) for item in range(len(ITEMS)) for m in range(tile.nx)
    ]
    base = 2 * len(ITEMS) * tile.nx
    placed += [(item, m, 2, 1, base + item * tile.nx + m) for item in range(2) for m in range(tile.nx)]
    return placed, base + 2 * tile.nx


def pack_edges(tile, raw):
    placed, total = edge_rows(tile)
    assert tile.nx % 4 == 0
    outs = {"odd": (total, tile.nz), "even": (total, tile.nz), "near": (2, tile.ny, tile.nz)}
    if tile.far:
        outs["far"] = outs["near"]
    outs.update({key: (value.shape, value.dtype) for key, value in raw.items()})

    def body(r):
        copies = {}
        for i, key in enumerate(raw):
            copies[key] = pltpu.make_async_copy(r[key + "_hbm"], r[key], r["done"].at[i])
            copies[key].start()
        odd = is_odd("gy") == 1
        sub = lax.broadcasted_iota(jnp.int32, (8, tile.nz), 0)
        blocks = {}
        for item, m, first, count, place in placed:
            key, c = ITEMS[item]
            if key in copies:
                copies.pop(key).wait()
                if key == "now":
                    for part in range(2):
                        r["near"][part] = r["now"][0, part, tile.place(tile.nx - 1)]
                        if tile.far:
                            r["far"][part] = r["now"][0, part, tile.place(0)]
            here, slot = tile.place(m), place % 8
            ref = r[key].at[0, c] if key in ("now", "before") else r[key]
            for end, start, from_row in (("top", tile.ny - 8, 8 - first - count), ("low", 0, first)):
                block = ref[here, pl.ds(start, 8), :].astype(F32)
                moved = rolled(block, slot - from_row, 0) if slot != from_row else block
                old = blocks.get(end)
                blocks[end] = moved if slot == 0 else jnp.where(sub >= slot, moved, old)
            if slot + count == 8:
                rows = pl.ds(place - slot, 8)
                r["even"][rows, :] = jnp.where(odd, blocks["low"], blocks["top"])
                r["odd"][rows, :] = jnp.where(odd, blocks["top"], blocks["low"])

    ins = {key + "_hbm": value for key, value in raw.items()}
    spaces = {key: pltpu.HBM for key in ins}
    return run_kernel(
        body, ins, outs, spaces=spaces, copies=len(raw), name="pack_edges", flops=10**6
    )


def halo_block(tile, r, item, m):
    odd = is_odd("gy") == 1
    has_upper = lax.axis_index("gy") < tile.gy - 1
    has_lower = lax.axis_index("gy") > 0
    sub = lax.broadcasted_iota(jnp.int32, (8, tile.nz), 0)
    result = jnp.zeros((8, tile.nz), F32)
    for i, plane, first, count, place in edge_rows(tile)[0]:
        if (i, plane) != (item, m):
            continue
        slot = place % 8
        rows = pl.ds(place - slot, 8)
        even_got, odd_got = r["got_even"][rows, :], r["got_odd"][rows, :]
        upper = jnp.where(odd, odd_got, even_got)
        lower = jnp.where(odd, even_got, odd_got)
        upper = rolled(upper, first - slot, 0) if slot != first else upper
        bottom = 8 - first - count
        lower = rolled(lower, bottom - slot, 0) if slot != bottom else lower
        result = jnp.where((sub >= first) & (sub < first + count) & has_upper, upper, result)
        result = jnp.where((sub >= bottom) & (sub < bottom + count) & has_lower, lower, result)
    return result


def angle_tables(rows):
    level = lax.broadcasted_iota(jnp.int32, (rows, LANES), 1).astype(F32)
    theta = level * (0.5 * math.pi / LEVELS)
    azimuth = level * (2.0 * math.pi / LEVELS)
    sin_t, cos_t, sin_p, cos_p = jnp.sin(theta), jnp.cos(theta), jnp.sin(azimuth), jnp.cos(azimuth)
    return sin_t, cos_t, sin_p, cos_p


def store_weights(out, m, rows, j, tables, sign, velocity, eps, delta, tilt, azimuth):
    def look(table, level):
        return jnp.take_along_axis(table, level, axis=1)

    sin_t, cos_t = look(tables[0], tilt), look(tables[1], tilt)
    sin_p, cos_p = look(tables[2], azimuth), look(tables[3], azimuth)
    sin2_t, half_t = sin_t * sin_t, 0.5 * sin_t * cos_t
    speed_sq = velocity * velocity
    root = jnp.sqrt(1.0 + 2.0 * delta)
    values = (
        sin2_t * (cos_p * cos_p),
        sin2_t * (sin_p * sin_p),
        cos_t * cos_t,
        (0.5 * sign) * (sin2_t * (sin_p * cos_p)),
        half_t * sin_p,
        sign * (half_t * cos_p),
        speed_sq * (1.0 + 2.0 * eps),
        speed_sq * root,
        speed_sq,
    )
    for k, value in enumerate(values):
        out[k, m, rows, lanes_of(j)] = value


def x_sign():
    return 1.0 - 2.0 * is_odd("gx").astype(F32)


def own_state(tile, raw, forward):
    coefs = ("velocity", "eps", "delta", "tilt", "azimuth")

    def body(r):
        copy = pltpu.make_async_copy(r["forward_hbm"], r["forward"], r["done"].at[0])
        copy.start()
        tables = angle_tables(8)
        sign = x_sign()

        def plane(m, _):
            here = tile.place(m)
            for j in range(tile.nj):
                for start in range(0, tile.ny, 8):
                    rows = pl.ds(start, 8)
                    store_weights(
                        r["w"], m, rows, j, tables, sign,
                        *(r[key][here, rows, lanes_of(j)] for key in coefs),
                    )
            return 0

        lax.fori_loop(0, tile.nx, plane, 0)
        copy.wait()

    ins = {key: raw[key] for key in coefs}
    ins["forward_hbm"] = forward
    outs = {"w": (9, tile.nx, tile.ny, tile.nz), "forward": (forward.shape, forward.dtype)}
    return run_kernel(
        body, ins, outs, spaces={"forward_hbm": pltpu.HBM}, copies=1, name="own_state",
        flops=3 * 10**6,
    )


def surface_load(tile, cell, count, trace, after):
    channels = cell.shape[1]
    width = tile.ny * tile.gy

    def body(r):
        start_x = lax.axis_index("gx") * tile.nx
        start_y = lax.axis_index("gy") * tile.ny
        cell_here = r["cell"][...]
        slots = lax.broadcasted_iota(jnp.int32, (1, channels), 1)
        live = slots < r["count"][...].reshape(1, 1)
        if width & (width - 1) == 0:
            row_of = cell_here & (width - 1)
        else:
            row_of = lax.rem(cell_here, jnp.full_like(cell_here, width))
        place = lax.broadcasted_iota(jnp.int32, (tile.rows, 1), 0)
        place = jnp.where(place >= tile.ny + HALO, place - tile.rows, place) + start_y
        onehot = jnp.where(row_of == place, 1.0, 0.0)
        first = lax.broadcasted_iota(jnp.int32, (tile.rows, LANES), 1) == 0
        pad = jnp.zeros((8 - tile.steps, channels), F32)
        trace_here = r["trace"][0]
        loads = []
        for m in range(tile.nx):
            low = (start_x + tile.place(m)) * width
            inside = live & (cell_here >= low) & (cell_here < low + width)
            loads += [jnp.where(inside, trace_here, 0.0), pad]
        rest, parts = jnp.concatenate(loads, axis=0), []
        for _ in range(3):
            part = rest.astype(jnp.bfloat16)
            rest = rest - part.astype(F32)
            parts.append(part.astype(F32))
        group = 8 * tile.nx
        if 3 * group < LANES:
            parts.append(jnp.zeros((LANES - 3 * group, channels), F32))
        columns = lax.dot_general(
            onehot.astype(jnp.bfloat16), jnp.concatenate(parts, axis=0).astype(jnp.bfloat16),
            (((1,), (1,)), ((), ())), preferred_element_type=F32,
        )
        columns = columns + (rolled(columns, -group, 1) + rolled(columns, -2 * group, 1))
        for m in range(tile.nx):
            for t in range(tile.steps):
                column = rolled(columns, -8 * m - t, 1) if m + t else columns
                r["surface"][t, m] = jnp.where(first, column, 0.0)

    assert tile.steps <= 8 and 24 * tile.nx <= LANES
    ins = {"cell": cell, "count": count, "trace": trace, "after": after}
    outs = {"surface": (tile.steps, tile.nx, tile.rows, LANES)}
    out = run_kernel(body, ins, outs, name="surface_load", flops=2 * 10**6)
    return out["surface"]


def halo_edges(tile, got_even, got_odd, after):
    outs = {"near": (2, 8, tile.nz)}
    if tile.far:
        outs["far"] = outs["near"]

    def body(r):
        for key in outs:
            for c in range(2):
                r[key][c] = halo_block(tile, r, c, tile.nx - 1 if key == "near" else 0)

    ins = {"got_odd": got_odd, "got_even": got_even, "after": after}
    return run_kernel(body, ins, outs, name="halo_edges", flops=10**5)


def halo_state(tile, got_even, got_odd, after):
    outs = {"uh": (4, tile.nx, 8, tile.nz), "wh": (9, tile.nx, 8, tile.nz)}

    def body(r):
        tables = angle_tables(8)
        sign = x_sign()
        for m in range(tile.nx):
            for item in range(4):
                r["uh"][item, m] = halo_block(tile, r, item, m)
            coefs = [halo_block(tile, r, item, m) for item in range(4, 9)]
            for j in range(tile.nj):
                part = [value[:, j * LANES : (j + 1) * LANES] for value in coefs]
                store_weights(
                    r["wh"], m, pl.ds(0, 8), j, tables, sign, *part[:3],
                    part[3].astype(jnp.int32), part[4].astype(jnp.int32),
                )

    ins = {"got_odd": got_odd, "got_even": got_even, "after": after}
    return run_kernel(body, ins, outs, name="halo_state", flops=10**6)


class Stage:
    def __init__(self, tile, state, ops, pieces, name, after=None):
        self.tile, self.state, self.ops, self.pieces, self.name = tile, state, ops, pieces, name
        self.ins, self.outs, self.scratch = {}, {}, {}
        if after is not None:
            self.ins["after"] = after

    def need(self, key):
        if key not in self.outs and key not in self.scratch:
            self.ins[key] = self.state[key]

    def run(self):
        tile = self.tile
        for t, m in self.ops:
            last = t == tile.steps - 1
            for key in ("w", "forward"):
                self.need(key)
            for k in (m - 1, m, m + 1):
                if k == -1 and not tile.far:
                    continue
                if k in (-1, tile.nx):
                    key = "xf" if k == -1 else "xn"
                    self.need((key, t))
                    if t == 0:
                        self.need((key + "h", t))
                elif t == 0:
                    for key in ("now", "uh"):
                        self.need(key)
                else:
                    self.need(("u", t, k))
            if t <= 1:
                for key in ("before" if t == 0 else "now", "uh"):
                    self.need(key)
            else:
                self.need(("u", t - 1, m))
            if not last:
                self.need("wh")
            self.need("surface")
            if t > 0:
                self.need(("g", t - 1, m))
            rows = tile.ny if last else tile.rows
            self.outs[("u", t + 1, m)] = (2, rows, tile.nz)
            if not last and tile.edge(m):
                self.outs[("e", t + 1, m)] = (2 * tile.ny + 8, tile.nz)
            total = (tile.nj, 3, tile.ny, LANES)
            if last and any(m in planes for planes in self.pieces):
                self.scratch[("g", t, m)] = pltpu.VMEM(total, F32)
            else:
                self.outs[("g", t, m)] = total
        for planes in self.pieces:
            for m in planes:
                self.need(("g", tile.steps - 1, m))
            block = (len(planes), 3, tile.ny, tile.nz // tile.src)
            if self.halved(planes):
                self.outs[("keep", planes)] = (2, *block)
                self.outs[("send", planes)] = (2, *block)
            else:
                for k in range(tile.src):
                    self.outs[("s", planes, k)] = block
        flops = len(self.ops) * 2 * 10**6 + 10**5
        out = run_kernel(self.body, self.ins, self.outs, self.scratch, name=self.name, flops=flops)
        self.state.update(out)

    def body(self, r):
        tile = self.tile
        for t, m in self.ops:
            self.update(r, t, m)
        me = lax.axis_index("src")
        per = tile.nj // tile.src
        for planes in self.pieces:
            for i, m in enumerate(planes):
                for k in range(tile.src):
                    owner = jnp.bitwise_xor(me, k)
                    if self.halved(planes):
                        second = tile.second[tile.plan[planes][1]][1]
                        first = 1 if second > 1 else 2
                        kind = "keep" if k in (0, second) else "send"
                        target = r[(kind, planes)].at[0 if k in (0, first) else 1]
                    else:
                        target = r[("s", planes, k)]
                    for part in range(per):
                        target[i, :, :, lanes_of(part)] = r[("g", tile.steps - 1, m)][
                            owner * per + part
                        ]

    def halved(self, planes):
        return self.tile.plan[planes][1] is not None

    def field(self, r, t, m, c, j):
        tile, lanes = self.tile, lanes_of(j)
        if m == -1 and not tile.far:
            return None
        if m in (-1, tile.nx):
            key = "xf" if m == -1 else "xn"
            if t == 0:
                own, halo = r[(key, t)][c, :, lanes], r[(key + "h", t)][c, :, lanes]
            else:
                own = r[(key, t)][pl.ds(c * tile.ny, tile.ny), lanes]
                halo = r[(key, t)][pl.ds(2 * tile.ny, 8), lanes]
                if c == 1:
                    sub = lax.broadcasted_iota(jnp.int32, (8, LANES), 0)
                    halo = jnp.where(sub < HALO, rolled(halo, -2, 0), rolled(halo, 2, 0))
            return jnp.concatenate([own, halo], axis=0)
        if t > 0:
            return r[("u", t, m)][c, :, lanes]
        ref, item = (r["now"], c) if t == 0 else (r["before"], 2 + c)
        return jnp.concatenate(
            [ref[0, c, tile.place(m), :, lanes], r["uh"][item, m, :, lanes]], axis=0
        )

    def update(self, r, t, m):
        tile = self.tile
        last = t == tile.steps - 1
        rows = tile.ny if last else tile.rows
        lane = lax.broadcasted_iota(jnp.int32, (tile.rows, LANES), 1)
        at_first, at_last = lane == 0, lane == LANES - 1

        def weight(k, j):
            own = r["w"][k, m, :, lanes_of(j)]
            return own if last else jnp.concatenate([own, r["wh"][k, m, :, lanes_of(j)]], axis=0)

        centers, halves = [], []
        for c in range(2):
            center = [self.field(r, t, m, c, j) for j in range(tile.nj)]
            total_x, diff_x = [], []
            for j in range(tile.nj):
                above, below = self.field(r, t, m + 1, c, j), self.field(r, t, m - 1, c, j)
                total_x.append(above if below is None else above + below)
                diff_x.append(above if below is None else above - below)
            centers.append(center)
            halves.append((total_x, diff_x))

        def deeper(blocks):
            moved = [rolled(block, -1, 1) for block in blocks] + [0.0]
            return [jnp.where(at_last, moved[j + 1], moved[j]) for j in range(tile.nj)]

        def shallower(blocks):
            moved = [rolled(block, 1, 1) for block in blocks] + [0.0]
            return [jnp.where(at_first, moved[j - 1], moved[j]) for j in range(tile.nj)]

        shifted = []
        for c in range(2):
            diff_x = halves[c][1]
            shifted.append(
                (deeper(centers[c]), shallower(centers[c]), deeper(diff_x), shallower(diff_x))
            )

        def both(block):
            return rolled(block, -1, 0)[:rows], rolled(block, 1, 0)[:rows]

        for j in range(tile.nj):
            weights = [weight(k, j) for k in range(6)]
            results = []
            for c in range(2):
                center = centers[c][j]
                total_x, diff_x = halves[c][0][j], halves[c][1][j]
                below, above, diff_below, diff_above = (part[j] for part in shifted[c])
                total_z, slope_z = (below + above)[:rows], below - above
                mixed_xz = (diff_below - diff_above)[:rows]
                up, down = both(center)
                total_y = up + down
                up, down = both(diff_x)
                mixed_xy = up - down
                up, down = both(slope_z)
                mixed_yz = up - down
                total_x, center = total_x[:rows], center[:rows]
                axial = (
                    weights[0] * total_x + weights[1] * total_y + weights[2] * total_z
                    + weights[3] * mixed_xy + weights[4] * mixed_yz + weights[5] * mixed_xz
                )
                if c == 0:
                    results.append(total_x + total_y + total_z - 4.0 * center - axial)
                else:
                    results.append(axial - 2.0 * center)
            horiz, axial = results
            stretched, rooted, speed_sq = (weight(k, j) for k in range(6, 9))
            before = [self.field(r, t - 1, m, c, j)[:rows] for c in range(2)]
            new_p = (
                2.0 * centers[0][j][:rows] - before[0] + stretched * horiz + rooted * axial
            )
            new_q = 2.0 * centers[1][j][:rows] - before[1] + rooted * horiz + speed_sq * axial
            if j == 0:
                new_p = new_p + r["surface"][t, m][:rows]
            r[("u", t + 1, m)][0, :, lanes_of(j)] = new_p
            r[("u", t + 1, m)][1, :, lanes_of(j)] = new_q
            if ("e", t + 1, m) in r:
                edge, lanes = r[("e", t + 1, m)], lanes_of(j)
                edge[: tile.ny, lanes] = new_p[: tile.ny]
                edge[tile.ny : 2 * tile.ny, lanes] = new_q[: tile.ny]
                sub = lax.broadcasted_iota(jnp.int32, (8, LANES), 0)
                p_rows, q_rows = new_p[tile.ny :], new_q[tile.ny :]
                q_rows = jnp.where(sub < HALO, rolled(q_rows, 2, 0), rolled(q_rows, -2, 0))
                edge[2 * tile.ny :, lanes] = jnp.where((sub < 2) | (sub >= 6), p_rows, q_rows)
            here = tile.place(m)
            forward_p = r["forward"][t, 0, 0, here, :, lanes_of(j)].astype(F32)
            forward_q = r["forward"][t, 0, 1, here, :, lanes_of(j)].astype(F32)
            horiz, axial = horiz[: tile.ny], axial[: tile.ny]
            terms = (
                forward_p * horiz,
                forward_p * axial + forward_q * horiz,
                forward_q * axial,
            )
            for k, term in enumerate(terms):
                if t > 0:
                    term = term + r[("g", t - 1, m)][j, k]
                r[("g", t, m)][j, k] = term


def xor_swap(tile, block, k):
    return lax.ppermute(block, "src", [(i, i ^ k) for i in range(tile.src)])


def second_round(tile, state, pieces, k, after, along):
    ins, outs, start = {"after": after}, {}, 0
    if along is not None:
        ins["along"] = state[("s", along, k)]
        start = len(along)
    count = start
    for planes in pieces:
        ins[("keep", planes)], ins[("got", planes)] = state[("keep", planes)], state[("got", planes)]
        outs[("s", planes, 0)] = state[("keep", planes)].shape[1:]
        count += len(planes)
    outs["passed"] = (count, *outs[("s", pieces[0], 0)][1:])

    def body(r):
        if along is not None:
            r["passed"][:start] = r["along"][...]
        at = start
        for planes in pieces:
            keep, got = r[("keep", planes)], r[("got", planes)]
            r[("s", planes, 0)][...] = keep[0] + got[0]
            r["passed"][at : at + len(planes)] = keep[1] + got[1]
            at += len(planes)

    state.update(run_kernel(body, ins, outs, name="second_round", flops=10**5))
    got = xor_swap(tile, state["passed"], k)
    at = start
    if along is not None:
        state[("r", along, k)] = (got, 0)
    for planes in pieces:
        state[("r", planes, k)] = (got, at)
        at += len(planes)


def combine(tile, state, pieces):
    depth = tile.nz // tile.src
    ins = {key: state[key] for key in ("velocity", "eps", "delta")}
    starts = {}
    for k in ORDER:
        for planes in pieces:
            if ("r", planes, k) in state:
                ins[("r", planes, k)], starts[(planes, k)] = state[("r", planes, k)]
    for planes in pieces:
        ins[("s", planes, 0)] = state[("s", planes, 0)]
    shape = (tile.nx, tile.ny, depth)

    def body(r):
        lanes = pl.ds(pl.multiple_of(lax.axis_index("src") * depth, LANES), depth)
        for planes in pieces:
            for i, m in enumerate(planes):
                here = tile.place(m)
                sums = []
                for item in range(3):
                    total = r[("s", planes, 0)][i, item]
                    for k in range(1, tile.src):
                        if (planes, k) in starts:
                            total = total + r[("r", planes, k)][starts[(planes, k)] + i, item]
                    sums.append(total)
                velocity = r["velocity"][here, :, lanes]
                root = jnp.sqrt(1.0 + 2.0 * r["delta"][here, :, lanes])
                stretch = 1.0 + 2.0 * r["eps"][here, :, lanes]
                speed_sq = velocity * velocity
                r["gv"][here] = 2.0 * velocity * (stretch * sums[0] + root * sums[1] + sums[2])
                r["ge"][here] = 2.0 * speed_sq * sums[0]
                r["gd"][here] = speed_sq / root * sums[1]

    out = run_kernel(body, ins, {"gv": shape, "ge": shape, "gd": shape}, name="combine", flops=10**6, final=True)
    return out["gv"], out["ge"], out["gd"]


def final_fields(tile, state):
    keys = [("u", tile.steps, m) for m in range(tile.nx)]

    def body(r):
        for m, key in enumerate(keys):
            for c in range(2):
                r["out"][0, c, tile.place(m)] = r[key][c]


    outs = {"out": (1, 2, tile.nx, tile.ny, tile.nz)}
    out = run_kernel(
        body, {key: state[key] for key in keys}, outs, name="final_fields", flops=10**6, final=True
    )
    return out["out"]


def on_device(
    mesh,
    adjoint_now,
    adjoint_before,
    forward_field,
    velocity,
    thomsen_eps,
    thomsen_delta,
    tilt_level,
    azimuth_level,
    channel_cell,
    channel_count,
    residual_trace,
):
    tile = Tile(mesh, velocity, forward_field.shape[0])
    raw = {
        "now": adjoint_now,
        "before": adjoint_before,
        "velocity": velocity,
        "eps": thomsen_eps,
        "delta": thomsen_delta,
        "tilt": tilt_level,
        "azimuth": azimuth_level,
    }
    edges = pack_edges(tile, raw)
    state = {key: edges[key] for key in raw}

    def exchange(key, t, near, far):
        state[("xn" + key, t)] = swap(near, "gx", tile.gx, 0)
        if tile.far:
            state[("xf" + key, t)] = swap(far, "gx", tile.gx, 1)

    got_odd = swap_rows(tile, edges["odd"], 1)
    got_even = swap_rows(tile, edges["even"], 0)
    exchange("", 0, edges["near"], edges.get("far"))
    state.update(own_state(tile, state, forward_field))
    state["surface"] = surface_load(
        tile, channel_cell, channel_count, residual_trace, state["w"]
    )
    halo = halo_edges(tile, got_even, got_odd, state["surface"])
    exchange("h", 0, halo["near"], halo.get("far"))
    state.update(halo_state(tile, got_even, got_odd, halo["near"]))

    ops = [(t, m) for t in range(tile.steps) for m in range(tile.nx)]
    pieces = list(tile.plan)
    for phase in range(tile.steps + 1):
        mine = [op for op in ops if max(tile.phase(*op), op[0] // 2) == phase]
        front = [op for op in mine if phase > 0 and op[0] == phase - 1 and tile.edge(op[1])]
        bulk = [op for op in mine if op not in front]
        done = [planes for planes in pieces if tile.plan[planes][0] == phase]
        if phase == tile.steps:
            front, bulk = mine, []
        if front:
            Stage(tile, state, front, [] if bulk else done, f"front_{phase}", state.get("token")).run()
            state["token"] = state[("u", phase, tile.nx - 1)]
            if phase < tile.steps:
                exchange("", phase, state[("e", phase, tile.nx - 1)], state.get(("e", phase, 0)))
        if bulk:
            Stage(tile, state, bulk, done, f"bulk_{phase}").run()
            state["token"] = state[("u", bulk[0][0] + 1, bulk[0][1])]
        later = [(name, k) for name, (when, k, _) in tile.second.items() if when == phase]
        direct = [planes for planes in done if tile.plan[planes][1] is None]
        joined = [k for name, k in later if tile.second[name][2] and direct]
        for planes in done:
            if planes not in direct:
                first = 1 if tile.second[tile.plan[planes][1]][1] > 1 else 2
                state[("got", planes)] = xor_swap(tile, state[("send", planes)], first)
                continue
            for k in range(tile.src - 1, 0, -1):
                if k not in joined:
                    state[("r", planes, k)] = (xor_swap(tile, state[("s", planes, k)], k), 0)
        for name, k in later:
            group = [planes for planes in pieces if tile.plan[planes][1] == name]
            along = direct[0] if k in joined else None
            after = state["token"]
            second_round(tile, state, group, k, after, along)
            if phase < tile.steps:
                state["token"] = state["passed"]
    following = final_fields(tile, state)
    return (following, *combine(tile, state, pieces))


def solution(mesh):
    placed = (
        P("src", None, "gx", "gy", None),
        P("src", None, "gx", "gy", None),
        P(None, "src", None, "gx", "gy", None),
        P("gx", "gy", None),
        P("gx", "gy", None),
        P("gx", "gy", None),
        P("gx", "gy", None),
        P("gx", "gy", None),
        P("src", None),
        P("src"),
        P("src", None, None),
    )

    def program(*args):
        return on_device(mesh, *args)

    return jax.shard_map(
        program,
        mesh=mesh,
        in_specs=placed,
        out_specs=(
            P("src", None, "gx", "gy", None),
            P("gx", "gy", "src"),
            P("gx", "gy", "src"),
            P("gx", "gy", "src"),
        ),
        check_vma=False,
    )
```

```python
import math

import jax
import jax.numpy as jnp
from jax import lax
from jax.experimental import pallas as pl
from jax.experimental.pallas import tpu as pltpu
from jax.sharding import PartitionSpec as P

LEVELS = 32
LANES = 128
HALO = 4
ORDER = (3, 2, 1)
WAVE = (
    {(0, 1): (1, "a"), (2,): (2, "b"), (3,): (3, None)},
    {"a": (2, 2, False), "b": (3, 3, True)},
)
VMEM_LIMIT = 8 * 1024 * 1024
F32 = jnp.float32


def run_kernel(body, ins, outs, scratch=None, spaces=None, copies=0, name=None, flops=0, final=False):
    scratch, spaces = scratch or {}, spaces or {}
    names = list(ins) + list(outs) + list(scratch) + ["done"]
    ins = {
        key: pltpu.with_memory_space_constraint(value, pltpu.HBM)
        if spaces.get(key) == pltpu.HBM
        else value
        for key, value in ins.items()
    }

    def kernel(*refs):
        body(dict(zip(names, refs)))

    results = pl.pallas_call(
        kernel,
        name=name,
        out_shape=[
            jax.ShapeDtypeStruct(shape, F32) if final else pltpu.VMEM(shape, kind)
            for shape, kind in (
                entry if isinstance(entry[0], tuple) else (entry, F32) for entry in outs.values()
            )
        ],
        in_specs=[
            pl.BlockSpec(memory_space=spaces.get(key, pltpu.VMEM)) for key in ins
        ],
        out_specs=[pl.BlockSpec(memory_space=pltpu.VMEM)] * len(outs),
        scratch_shapes=list(scratch.values())
        + [pltpu.SemaphoreType.DMA((copies,))] * (copies > 0),
        compiler_params=pltpu.CompilerParams(vmem_limit_bytes=VMEM_LIMIT),
        cost_estimate=pl.CostEstimate(flops=flops, bytes_accessed=flops // 8, transcendentals=0),
    )(*ins.values())
    return dict(zip(outs, results))


def pair_swaps(count, first):
    pairs = []
    for low in range(first, count - 1, 2):
        pairs += [(low, low + 1), (low + 1, low)]
    return pairs


def swap(block, axis, count, first):
    return lax.ppermute(block, axis, pair_swaps(count, first))


def swap_rows(tile, block, first):
    pairs = dict(pair_swaps(tile.gy, first))
    across = dict(pair_swaps(tile.src, 0))
    joint = []
    for s in range(tile.src):
        for y in range(tile.gy):
            target = (s, pairs[y]) if y in pairs else (across.get(s, s), y)
            joint.append((s * tile.gy + y, target[0] * tile.gy + target[1]))
    return lax.ppermute(block, ("src", "gy"), joint)


def lanes_of(j):
    return pl.ds(j * LANES, LANES)


def is_odd(axis):
    return lax.rem(lax.axis_index(axis), 2)


class Tile:
    def __init__(self, mesh, velocity, steps):
        self.nx, self.ny, self.nz = velocity.shape
        self.steps = steps
        self.nj = self.nz // LANES
        self.rows = self.ny + 2 * HALO
        self.gx, self.gy, self.src = mesh.shape["gx"], mesh.shape["gy"], mesh.shape["src"]
        self.far = self.gx > 2
        self.plan, self.second = self.reduction()

    def reduction(self):
        last = self.steps - 1
        ready = [self.phase(last, m) for m in range(self.nx)]
        if self.src == 4 and ready == [0, 1, 2, 3]:
            return WAVE
        pieces = {}
        for m, phase in enumerate(ready):
            pieces.setdefault(phase, []).append(m)
        return {tuple(planes): (phase, None) for phase, planes in pieces.items()}, {}

    def place(self, m):
        return m + is_odd("gx") * (self.nx - 1 - 2 * m)

    def phase(self, t, m):
        if m == self.nx or m == -1:
            return t + 2 if (m == self.nx or self.far) else 0
        if t < 0:
            return 0
        return max(self.phase(t - 1, k) for k in (m - 1, m, m + 1))

    def edge(self, m):
        return m == self.nx - 1 or (m == 0 and self.far)


def rolled(value, by, axis):
    return pltpu.roll(value, by % value.shape[axis], axis)


ITEMS = [("now", 0), ("now", 1), ("before", 0), ("before", 1)] + [
    (key, 0) for key in ("velocity", "eps", "delta", "tilt", "azimuth")
]


def edge_rows(tile):
    placed = [
        (item, m, 0, 2, 2 * (item * tile.nx + m)) for item in range(len(ITEMS)) for m in range(tile.nx)
    ]
    base = 2 * len(ITEMS) * tile.nx
    placed += [(item, m, 2, 1, base + item * tile.nx + m) for item in range(2) for m in range(tile.nx)]
    return placed, base + 2 * tile.nx


def pack_edges(tile, raw):
    placed, total = edge_rows(tile)
    assert tile.nx % 4 == 0
    outs = {"odd": (total, tile.nz), "even": (total, tile.nz), "near": (2, tile.ny, tile.nz)}
    if tile.far:
        outs["far"] = outs["near"]
    outs.update({key: (value.shape, value.dtype) for key, value in raw.items()})

    def body(r):
        copies = {}
        for i, key in enumerate(raw):
            copies[key] = pltpu.make_async_copy(r[key + "_hbm"], r[key], r["done"].at[i])
            copies[key].start()
        odd = is_odd("gy") == 1
        sub = lax.broadcasted_iota(jnp.int32, (8, tile.nz), 0)
        blocks = {}
        for item, m, first, count, place in placed:
            key, c = ITEMS[item]
            if key in copies:
                copies.pop(key).wait()
                if key == "now":
                    for part in range(2):
                        r["near"][part] = r["now"][0, part, tile.place(tile.nx - 1)]
                        if tile.far:
                            r["far"][part] = r["now"][0, part, tile.place(0)]
            here, slot = tile.place(m), place % 8
            ref = r[key].at[0, c] if key in ("now", "before") else r[key]
            for end, start, from_row in (("top", tile.ny - 8, 8 - first - count), ("low", 0, first)):
                block = ref[here, pl.ds(start, 8), :].astype(F32)
                moved = rolled(block, slot - from_row, 0) if slot != from_row else block
                old = blocks.get(end)
                blocks[end] = moved if slot == 0 else jnp.where(sub >= slot, moved, old)
            if slot + count == 8:
                rows = pl.ds(place - slot, 8)
                r["even"][rows, :] = jnp.where(odd, blocks["low"], blocks["top"])
                r["odd"][rows, :] = jnp.where(odd, blocks["top"], blocks["low"])

    ins = {key + "_hbm": value for key, value in raw.items()}
    spaces = {key: pltpu.HBM for key in ins}
    return run_kernel(
        body, ins, outs, spaces=spaces, copies=len(raw), name="pack_edges", flops=10**6
    )


def halo_block(tile, r, item, m):
    odd = is_odd("gy") == 1
    has_upper = lax.axis_index("gy") < tile.gy - 1
    has_lower = lax.axis_index("gy") > 0
    sub = lax.broadcasted_iota(jnp.int32, (8, tile.nz), 0)
    result = jnp.zeros((8, tile.nz), F32)
    for i, plane, first, count, place in edge_rows(tile)[0]:
        if (i, plane) != (item, m):
            continue
        slot = place % 8
        rows = pl.ds(place - slot, 8)
        even_got, odd_got = r["got_even"][rows, :], r["got_odd"][rows, :]
        upper = jnp.where(odd, odd_got, even_got)
        lower = jnp.where(odd, even_got, odd_got)
        upper = rolled(upper, first - slot, 0) if slot != first else upper
        bottom = 8 - first - count
        lower = rolled(lower, bottom - slot, 0) if slot != bottom else lower
        result = jnp.where((sub >= first) & (sub < first + count) & has_upper, upper, result)
        result = jnp.where((sub >= bottom) & (sub < bottom + count) & has_lower, lower, result)
    return result


def angle_tables(rows):
    level = lax.broadcasted_iota(jnp.int32, (rows, LANES), 1).astype(F32)
    theta = level * (0.5 * math.pi / LEVELS)
    azimuth = level * (2.0 * math.pi / LEVELS)
    sin_t, cos_t, sin_p, cos_p = jnp.sin(theta), jnp.cos(theta), jnp.sin(azimuth), jnp.cos(azimuth)
    return sin_t, cos_t, sin_p, cos_p


def store_weights(out, m, rows, j, tables, sign, velocity, eps, delta, tilt, azimuth):
    def look(table, level):
        return jnp.take_along_axis(table, level, axis=1)

    sin_t, cos_t = look(tables[0], tilt), look(tables[1], tilt)
    sin_p, cos_p = look(tables[2], azimuth), look(tables[3], azimuth)
    sin2_t, half_t = sin_t * sin_t, 0.5 * sin_t * cos_t
    speed_sq = velocity * velocity
    root = jnp.sqrt(1.0 + 2.0 * delta)
    values = (
        sin2_t * (cos_p * cos_p),
        sin2_t * (sin_p * sin_p),
        cos_t * cos_t,
        (0.5 * sign) * (sin2_t * (sin_p * cos_p)),
        half_t * sin_p,
        sign * (half_t * cos_p),
        speed_sq * (1.0 + 2.0 * eps),
        speed_sq * root,
        speed_sq,
    )
    for k, value in enumerate(values):
        out[k, m, rows, lanes_of(j)] = value


def x_sign():
    return 1.0 - 2.0 * is_odd("gx").astype(F32)


def own_state(tile, raw, forward):
    coefs = ("velocity", "eps", "delta", "tilt", "azimuth")

    def body(r):
        copy = pltpu.make_async_copy(r["forward_hbm"], r["forward"], r["done"].at[0])
        copy.start()
        tables = angle_tables(8)
        sign = x_sign()

        def plane(m, _):
            here = tile.place(m)
            for j in range(tile.nj):
                for start in range(0, tile.ny, 8):
                    rows = pl.ds(start, 8)
                    store_weights(
                        r["w"], m, rows, j, tables, sign,
                        *(r[key][here, rows, lanes_of(j)] for key in coefs),
                    )
            return 0

        lax.fori_loop(0, tile.nx, plane, 0)
        copy.wait()

    ins = {key: raw[key] for key in coefs}
    ins["forward_hbm"] = forward
    outs = {"w": (9, tile.nx, tile.ny, tile.nz), "forward": (forward.shape, forward.dtype)}
    return run_kernel(
        body, ins, outs, spaces={"forward_hbm": pltpu.HBM}, copies=1, name="own_state",
        flops=3 * 10**6,
    )


def surface_load(tile, cell, count, trace, after):
    channels = cell.shape[1]
    width = tile.ny * tile.gy

    def body(r):
        start_x = lax.axis_index("gx") * tile.nx
        start_y = lax.axis_index("gy") * tile.ny
        cell_here = r["cell"][...]
        slots = lax.broadcasted_iota(jnp.int32, (1, channels), 1)
        live = slots < r["count"][...].reshape(1, 1)
        if width & (width - 1) == 0:
            row_of = cell_here & (width - 1)
        else:
            row_of = lax.rem(cell_here, jnp.full_like(cell_here, width))
        place = lax.broadcasted_iota(jnp.int32, (tile.rows, 1), 0)
        place = jnp.where(place >= tile.ny + HALO, place - tile.rows, place) + start_y
        onehot = jnp.where(row_of == place, 1.0, 0.0)
        first = lax.broadcasted_iota(jnp.int32, (tile.rows, LANES), 1) == 0
        pad = jnp.zeros((8 - tile.steps, channels), F32)
        trace_here = r["trace"][0]
        loads = []
        for m in range(tile.nx):
            low = (start_x + tile.place(m)) * width
            inside = live & (cell_here >= low) & (cell_here < low + width)
            loads += [jnp.where(inside, trace_here, 0.0), pad]
        rest, parts = jnp.concatenate(loads, axis=0), []
        for _ in range(3):
            part = rest.astype(jnp.bfloat16)
            rest = rest - part.astype(F32)
            parts.append(part.astype(F32))
        group = 8 * tile.nx
        if 3 * group < LANES:
            parts.append(jnp.zeros((LANES - 3 * group, channels), F32))
        columns = lax.dot_general(
            onehot.astype(jnp.bfloat16), jnp.concatenate(parts, axis=0).astype(jnp.bfloat16),
            (((1,), (1,)), ((), ())), preferred_element_type=F32,
        )
        columns = columns + (rolled(columns, -group, 1) + rolled(columns, -2 * group, 1))
        for m in range(tile.nx):
            for t in range(tile.steps):
                column = rolled(columns, -8 * m - t, 1) if m + t else columns
                r["surface"][t, m] = jnp.where(first, column, 0.0)

    assert tile.steps <= 8 and 24 * tile.nx <= LANES
    ins = {"cell": cell, "count": count, "trace": trace, "after": after}
    outs = {"surface": (tile.steps, tile.nx, tile.rows, LANES)}
    out = run_kernel(body, ins, outs, name="surface_load", flops=2 * 10**6)
    return out["surface"]


def halo_edges(tile, got_even, got_odd, after):
    outs = {"near": (2, 8, tile.nz)}
    if tile.far:
        outs["far"] = outs["near"]

    def body(r):
        for key in outs:
            for c in range(2):
                r[key][c] = halo_block(tile, r, c, tile.nx - 1 if key == "near" else 0)

    ins = {"got_odd": got_odd, "got_even": got_even, "after": after}
    return run_kernel(body, ins, outs, name="halo_edges", flops=10**5)


def halo_state(tile, got_even, got_odd, after):
    outs = {"uh": (4, tile.nx, 8, tile.nz), "wh": (9, tile.nx, 8, tile.nz)}

    def body(r):
        tables = angle_tables(8)
        sign = x_sign()
        for m in range(tile.nx):
            for item in range(4):
                r["uh"][item, m] = halo_block(tile, r, item, m)
            coefs = [halo_block(tile, r, item, m) for item in range(4, 9)]
            for j in range(tile.nj):
                part = [value[:, j * LANES : (j + 1) * LANES] for value in coefs]
                store_weights(
                    r["wh"], m, pl.ds(0, 8), j, tables, sign, *part[:3],
                    part[3].astype(jnp.int32), part[4].astype(jnp.int32),
                )

    ins = {"got_odd": got_odd, "got_even": got_even, "after": after}
    return run_kernel(body, ins, outs, name="halo_state", flops=10**6)


class Stage:
    def __init__(self, tile, state, ops, pieces, name, after=None):
        self.tile, self.state, self.ops, self.pieces, self.name = tile, state, ops, pieces, name
        self.ins, self.outs, self.scratch = {}, {}, {}
        if after is not None:
            self.ins["after"] = after

    def need(self, key):
        if key not in self.outs and key not in self.scratch:
            self.ins[key] = self.state[key]

    def run(self):
        tile = self.tile
        for t, m in self.ops:
            last = t == tile.steps - 1
            for key in ("w", "forward"):
                self.need(key)
            for k in (m - 1, m, m + 1):
                if k == -1 and not tile.far:
                    continue
                if k in (-1, tile.nx):
                    key = "xf" if k == -1 else "xn"
                    self.need((key, t))
                    if t == 0:
                        self.need((key + "h", t))
                elif t == 0:
                    for key in ("now", "uh"):
                        self.need(key)
                else:
                    self.need(("u", t, k))
            if t <= 1:
                for key in ("before" if t == 0 else "now", "uh"):
                    self.need(key)
            else:
                self.need(("u", t - 1, m))
            if not last:
                self.need("wh")
            self.need("surface")
            if t > 0:
                self.need(("g", t - 1, m))
            rows = tile.ny if last else tile.rows
            self.outs[("u", t + 1, m)] = (2, rows, tile.nz)
            if not last and tile.edge(m):
                self.outs[("e", t + 1, m)] = (2 * tile.ny + 8, tile.nz)
            total = (tile.nj, 3, tile.ny, LANES)
            if last and any(m in planes for planes in self.pieces):
                self.scratch[("g", t, m)] = pltpu.VMEM(total, F32)
            else:
                self.outs[("g", t, m)] = total
        for planes in self.pieces:
            for m in planes:
                self.need(("g", tile.steps - 1, m))
            block = (len(planes), 3, tile.ny, tile.nz // tile.src)
            if self.halved(planes):
                self.outs[("keep", planes)] = (2, *block)
                self.outs[("send", planes)] = (2, *block)
            else:
                for k in range(tile.src):
                    self.outs[("s", planes, k)] = block
        flops = len(self.ops) * 2 * 10**6 + 10**5
        out = run_kernel(self.body, self.ins, self.outs, self.scratch, name=self.name, flops=flops)
        self.state.update(out)

    def body(self, r):
        tile = self.tile
        for t, m in self.ops:
            self.update(r, t, m)
        me = lax.axis_index("src")
        per = tile.nj // tile.src
        for planes in self.pieces:
            for i, m in enumerate(planes):
                for k in range(tile.src):
                    owner = jnp.bitwise_xor(me, k)
                    if self.halved(planes):
                        second = tile.second[tile.plan[planes][1]][1]
                        first = 1 if second > 1 else 2
                        kind = "keep" if k in (0, second) else "send"
                        target = r[(kind, planes)].at[0 if k in (0, first) else 1]
                    else:
                        target = r[("s", planes, k)]
                    for part in range(per):
                        target[i, :, :, lanes_of(part)] = r[("g", tile.steps - 1, m)][
                            owner * per + part
                        ]

    def halved(self, planes):
        return self.tile.plan[planes][1] is not None

    def field(self, r, t, m, c, j):
        tile, lanes = self.tile, lanes_of(j)
        if m == -1 and not tile.far:
            return None
        if m in (-1, tile.nx):
            key = "xf" if m == -1 else "xn"
            if t == 0:
                own, halo = r[(key, t)][c, :, lanes], r[(key + "h", t)][c, :, lanes]
            else:
                own = r[(key, t)][pl.ds(c * tile.ny, tile.ny), lanes]
                halo = r[(key, t)][pl.ds(2 * tile.ny, 8), lanes]
                if c == 1:
                    sub = lax.broadcasted_iota(jnp.int32, (8, LANES), 0)
                    halo = jnp.where(sub < HALO, rolled(halo, -2, 0), rolled(halo, 2, 0))
            return jnp.concatenate([own, halo], axis=0)
        if t > 0:
            return r[("u", t, m)][c, :, lanes]
        ref, item = (r["now"], c) if t == 0 else (r["before"], 2 + c)
        return jnp.concatenate(
            [ref[0, c, tile.place(m), :, lanes], r["uh"][item, m, :, lanes]], axis=0
        )

    def update(self, r, t, m):
        tile = self.tile
        last = t == tile.steps - 1
        rows = tile.ny if last else tile.rows
        lane = lax.broadcasted_iota(jnp.int32, (tile.rows, LANES), 1)
        at_first, at_last = lane == 0, lane == LANES - 1

        def weight(k, j):
            own = r["w"][k, m, :, lanes_of(j)]
            return own if last else jnp.concatenate([own, r["wh"][k, m, :, lanes_of(j)]], axis=0)

        centers, halves = [], []
        for c in range(2):
            center = [self.field(r, t, m, c, j) for j in range(tile.nj)]
            total_x, diff_x = [], []
            for j in range(tile.nj):
                above, below = self.field(r, t, m + 1, c, j), self.field(r, t, m - 1, c, j)
                total_x.append(above if below is None else above + below)
                diff_x.append(above if below is None else above - below)
            centers.append(center)
            halves.append((total_x, diff_x))

        def deeper(blocks):
            moved = [rolled(block, -1, 1) for block in blocks] + [0.0]
            return [jnp.where(at_last, moved[j + 1], moved[j]) for j in range(tile.nj)]

        def shallower(blocks):
            moved = [rolled(block, 1, 1) for block in blocks] + [0.0]
            return [jnp.where(at_first, moved[j - 1], moved[j]) for j in range(tile.nj)]

        shifted = []
        for c in range(2):
            diff_x = halves[c][1]
            shifted.append(
                (deeper(centers[c]), shallower(centers[c]), deeper(diff_x), shallower(diff_x))
            )

        def both(block):
            return rolled(block, -1, 0)[:rows], rolled(block, 1, 0)[:rows]

        for j in range(tile.nj):
            weights = [weight(k, j) for k in range(6)]
            results = []
            for c in range(2):
                center = centers[c][j]
                total_x, diff_x = halves[c][0][j], halves[c][1][j]
                below, above, diff_below, diff_above = (part[j] for part in shifted[c])
                total_z, slope_z = (below + above)[:rows], below - above
                mixed_xz = (diff_below - diff_above)[:rows]
                up, down = both(center)
                total_y = up + down
                up, down = both(diff_x)
                mixed_xy = up - down
                up, down = both(slope_z)
                mixed_yz = up - down
                total_x, center = total_x[:rows], center[:rows]
                axial = (
                    weights[0] * total_x + weights[1] * total_y + weights[2] * total_z
                    + weights[3] * mixed_xy + weights[4] * mixed_yz + weights[5] * mixed_xz
                )
                if c == 0:
                    results.append(total_x + total_y + total_z - 4.0 * center - axial)
                else:
                    results.append(axial - 2.0 * center)
            horiz, axial = results
            stretched, rooted, speed_sq = (weight(k, j) for k in range(6, 9))
            before = [self.field(r, t - 1, m, c, j)[:rows] for c in range(2)]
            new_p = (
                2.0 * centers[0][j][:rows] - before[0] + stretched * horiz + rooted * axial
            )
            new_q = 2.0 * centers[1][j][:rows] - before[1] + rooted * horiz + speed_sq * axial
            if j == 0:
                new_p = new_p + r["surface"][t, m][:rows]
            r[("u", t + 1, m)][0, :, lanes_of(j)] = new_p
            r[("u", t + 1, m)][1, :, lanes_of(j)] = new_q
            if ("e", t + 1, m) in r:
                edge, lanes = r[("e", t + 1, m)], lanes_of(j)
                edge[: tile.ny, lanes] = new_p[: tile.ny]
                edge[tile.ny : 2 * tile.ny, lanes] = new_q[: tile.ny]
                sub = lax.broadcasted_iota(jnp.int32, (8, LANES), 0)
                p_rows, q_rows = new_p[tile.ny :], new_q[tile.ny :]
                q_rows = jnp.where(sub < HALO, rolled(q_rows, 2, 0), rolled(q_rows, -2, 0))
                edge[2 * tile.ny :, lanes] = jnp.where((sub < 2) | (sub >= 6), p_rows, q_rows)
            here = tile.place(m)
            forward_p = r["forward"][t, 0, 0, here, :, lanes_of(j)].astype(F32)
            forward_q = r["forward"][t, 0, 1, here, :, lanes_of(j)].astype(F32)
            horiz, axial = horiz[: tile.ny], axial[: tile.ny]
            terms = (
                forward_p * horiz,
                forward_p * axial + forward_q * horiz,
                forward_q * axial,
            )
            for k, term in enumerate(terms):
                if t > 0:
                    term = term + r[("g", t - 1, m)][j, k]
                r[("g", t, m)][j, k] = term


def xor_swap(tile, block, k):
    return lax.ppermute(block, "src", [(i, i ^ k) for i in range(tile.src)])


def second_round(tile, state, pieces, k, after, along):
    ins, outs, start = {"after": after}, {}, 0
    if along is not None:
        ins["along"] = state[("s", along, k)]
        start = len(along)
    count = start
    for planes in pieces:
        ins[("keep", planes)], ins[("got", planes)] = state[("keep", planes)], state[("got", planes)]
        outs[("s", planes, 0)] = state[("keep", planes)].shape[1:]
        count += len(planes)
    outs["passed"] = (count, *outs[("s", pieces[0], 0)][1:])

    def body(r):
        if along is not None:
            r["passed"][:start] = r["along"][...]
        at = start
        for planes in pieces:
            keep, got = r[("keep", planes)], r[("got", planes)]
            r[("s", planes, 0)][...] = keep[0] + got[0]
            r["passed"][at : at + len(planes)] = keep[1] + got[1]
            at += len(planes)

    state.update(run_kernel(body, ins, outs, name="second_round", flops=10**5))
    got = xor_swap(tile, state["passed"], k)
    at = start
    if along is not None:
        state[("r", along, k)] = (got, 0)
    for planes in pieces:
        state[("r", planes, k)] = (got, at)
        at += len(planes)


def combine(tile, state, pieces):
    depth = tile.nz // tile.src
    ins = {key: state[key] for key in ("velocity", "eps", "delta")}
    starts = {}
    for k in ORDER:
        for planes in pieces:
            if ("r", planes, k) in state:
                ins[("r", planes, k)], starts[(planes, k)] = state[("r", planes, k)]
    for planes in pieces:
        ins[("s", planes, 0)] = state[("s", planes, 0)]
    shape = (tile.nx, tile.ny, depth)

    def body(r):
        lanes = pl.ds(pl.multiple_of(lax.axis_index("src") * depth, LANES), depth)
        for planes in pieces:
            for i, m in enumerate(planes):
                here = tile.place(m)
                sums = []
                for item in range(3):
                    total = r[("s", planes, 0)][i, item]
                    for k in range(1, tile.src):
                        if (planes, k) in starts:
                            total = total + r[("r", planes, k)][starts[(planes, k)] + i, item]
                    sums.append(total)
                velocity = r["velocity"][here, :, lanes]
                root = jnp.sqrt(1.0 + 2.0 * r["delta"][here, :, lanes])
                stretch = 1.0 + 2.0 * r["eps"][here, :, lanes]
                speed_sq = velocity * velocity
                r["gv"][here] = 2.0 * velocity * (stretch * sums[0] + root * sums[1] + sums[2])
                r["ge"][here] = 2.0 * speed_sq * sums[0]
                r["gd"][here] = speed_sq / root * sums[1]

    out = run_kernel(body, ins, {"gv": shape, "ge": shape, "gd": shape}, name="combine", flops=10**6, final=True)
    return out["gv"], out["ge"], out["gd"]


def final_fields(tile, state):
    keys = [("u", tile.steps, m) for m in range(tile.nx)]

    def body(r):
        for m, key in enumerate(keys):
            for c in range(2):
                r["out"][0, c, tile.place(m)] = r[key][c]


    outs = {"out": (1, 2, tile.nx, tile.ny, tile.nz)}
    out = run_kernel(
        body, {key: state[key] for key in keys}, outs, name="final_fields", flops=10**6, final=True
    )
    return out["out"]


def on_device(
    mesh,
    adjoint_now,
    adjoint_before,
    forward_field,
    velocity,
    thomsen_eps,
    thomsen_delta,
    tilt_level,
    azimuth_level,
    channel_cell,
    channel_count,
    residual_trace,
):
    tile = Tile(mesh, velocity, forward_field.shape[0])
    raw = {
        "now": adjoint_now,
        "before": adjoint_before,
        "velocity": velocity,
        "eps": thomsen_eps,
        "delta": thomsen_delta,
        "tilt": tilt_level,
        "azimuth": azimuth_level,
    }
    edges = pack_edges(tile, raw)
    state = {key: edges[key] for key in raw}

    def exchange(key, t, near, far):
        state[("xn" + key, t)] = swap(near, "gx", tile.gx, 0)
        if tile.far:
            state[("xf" + key, t)] = swap(far, "gx", tile.gx, 1)

    got_odd = swap_rows(tile, edges["odd"], 1)
    got_even = swap_rows(tile, edges["even"], 0)
    exchange("", 0, edges["near"], edges.get("far"))
    state.update(own_state(tile, state, forward_field))
    state["surface"] = surface_load(
        tile, channel_cell, channel_count, residual_trace, state["w"]
    )
    halo = halo_edges(tile, got_even, got_odd, state["surface"])
    exchange("h", 0, halo["near"], halo.get("far"))
    state.update(halo_state(tile, got_even, got_odd, halo["near"]))

    ops = [(t, m) for t in range(tile.steps) for m in range(tile.nx)]
    pieces = list(tile.plan)
    for phase in range(tile.steps + 1):
        mine = [op for op in ops if max(tile.phase(*op), op[0] // 2) == phase]
        front = [op for op in mine if phase > 0 and op[0] == phase - 1 and tile.edge(op[1])]
        bulk = [op for op in mine if op not in front]
        done = [planes for planes in pieces if tile.plan[planes][0] == phase]
        if phase == tile.steps:
            front, bulk = mine, []
        if front:
            Stage(tile, state, front, [] if bulk else done, f"front_{phase}", state.get("token")).run()
            state["token"] = state[("u", phase, tile.nx - 1)]
            if phase < tile.steps:
                exchange("", phase, state[("e", phase, tile.nx - 1)], state.get(("e", phase, 0)))
        if bulk:
            Stage(tile, state, bulk, done, f"bulk_{phase}").run()
            state["token"] = state[("u", bulk[0][0] + 1, bulk[0][1])]
        later = [(name, k) for name, (when, k, _) in tile.second.items() if when == phase]
        direct = [planes for planes in done if tile.plan[planes][1] is None]
        joined = [k for name, k in later if tile.second[name][2] and direct]
        for planes in done:
            if planes not in direct:
                first = 1 if tile.second[tile.plan[planes][1]][1] > 1 else 2
                state[("got", planes)] = xor_swap(tile, state[("send", planes)], first)
                continue
            for k in range(tile.src - 1, 0, -1):
                if k not in joined:
                    state[("r", planes, k)] = (xor_swap(tile, state[("s", planes, k)], k), 0)
        for name, k in later:
            group = [planes for planes in pieces if tile.plan[planes][1] == name]
            along = direct[0] if k in joined else None
            after = state["token"]
            second_round(tile, state, group, k, after, along)
            if phase < tile.steps:
                state["token"] = state["passed"]
    following = final_fields(tile, state)
    return (following, *combine(tile, state, pieces))


def solution(mesh):
    placed = (
        P("src", None, "gx", "gy", None),
        P("src", None, "gx", "gy", None),
        P(None, "src", None, "gx", "gy", None),
        P("gx", "gy", None),
        P("gx", "gy", None),
        P("gx", "gy", None),
        P("gx", "gy", None),
        P("gx", "gy", None),
        P("src", None),
        P("src"),
        P("src", None, None),
    )

    def program(*args):
        return on_device(mesh, *args)

    return jax.shard_map(
        program,
        mesh=mesh,
        in_specs=placed,
        out_specs=(
            P("src", None, "gx", "gy", None),
            P("gx", "gy", "src"),
            P("gx", "gy", "src"),
            P("gx", "gy", "src"),
        ),
        check_vma=False,
    )
```

```python
import math

import jax
import jax.numpy as jnp
from jax import lax
from jax.experimental import pallas as pl
from jax.experimental.pallas import tpu as pltpu
from jax.sharding import PartitionSpec as P

LEVELS = 32
LANES = 128
HALO = 4
ORDER = (3, 2, 1)
WAVE = (
    {(0, 1): (1, "a"), (2,): (2, "b"), (3,): (3, None)},
    {"a": (2, 2, False), "b": (3, 3, True)},
)
VMEM_LIMIT = 8 * 1024 * 1024
F32 = jnp.float32


def run_kernel(body, ins, outs, scratch=None, spaces=None, copies=0, name=None, flops=0, final=False):
    scratch, spaces = scratch or {}, spaces or {}
    names = list(ins) + list(outs) + list(scratch) + ["done"]
    ins = {
        key: pltpu.with_memory_space_constraint(value, pltpu.HBM)
        if spaces.get(key) == pltpu.HBM
        else value
        for key, value in ins.items()
    }

    def kernel(*refs):
        body(dict(zip(names, refs)))

    results = pl.pallas_call(
        kernel,
        name=name,
        out_shape=[
            jax.ShapeDtypeStruct(shape, F32) if final else pltpu.VMEM(shape, kind)
            for shape, kind in (
                entry if isinstance(entry[0], tuple) else (entry, F32) for entry in outs.values()
            )
        ],
        in_specs=[
            pl.BlockSpec(memory_space=spaces.get(key, pltpu.VMEM)) for key in ins
        ],
        out_specs=[pl.BlockSpec(memory_space=pltpu.VMEM)] * len(outs),
        scratch_shapes=list(scratch.values())
        + [pltpu.SemaphoreType.DMA((copies,))] * (copies > 0),
        compiler_params=pltpu.CompilerParams(vmem_limit_bytes=VMEM_LIMIT),
        cost_estimate=pl.CostEstimate(flops=flops, bytes_accessed=flops // 8, transcendentals=0),
    )(*ins.values())
    return dict(zip(outs, results))


def pair_swaps(count, first):
    pairs = []
    for low in range(first, count - 1, 2):
        pairs += [(low, low + 1), (low + 1, low)]
    return pairs


def swap(block, axis, count, first):
    return lax.ppermute(block, axis, pair_swaps(count, first))


def swap_rows(tile, block, first):
    pairs = dict(pair_swaps(tile.gy, first))
    across = dict(pair_swaps(tile.src, 0))
    joint = []
    for s in range(tile.src):
        for y in range(tile.gy):
            target = (s, pairs[y]) if y in pairs else (across.get(s, s), y)
            joint.append((s * tile.gy + y, target[0] * tile.gy + target[1]))
    return lax.ppermute(block, ("src", "gy"), joint)


def lanes_of(j):
    return pl.ds(j * LANES, LANES)


def is_odd(axis):
    return lax.rem(lax.axis_index(axis), 2)


class Tile:
    def __init__(self, mesh, velocity, steps):
        self.nx, self.ny, self.nz = velocity.shape
        self.steps = steps
        self.nj = self.nz // LANES
        self.rows = self.ny + 2 * HALO
        self.gx, self.gy, self.src = mesh.shape["gx"], mesh.shape["gy"], mesh.shape["src"]
        self.far = self.gx > 2
        self.plan, self.second = self.reduction()

    def reduction(self):
        last = self.steps - 1
        ready = [self.phase(last, m) for m in range(self.nx)]
        if self.src == 4 and ready == [0, 1, 2, 3]:
            return WAVE
        pieces = {}
        for m, phase in enumerate(ready):
            pieces.setdefault(phase, []).append(m)
        return {tuple(planes): (phase, None) for phase, planes in pieces.items()}, {}

    def place(self, m):
        return m + is_odd("gx") * (self.nx - 1 - 2 * m)

    def phase(self, t, m):
        if m == self.nx or m == -1:
            return t + 2 if (m == self.nx or self.far) else 0
        if t < 0:
            return 0
        return max(self.phase(t - 1, k) for k in (m - 1, m, m + 1))

    def edge(self, m):
        return m == self.nx - 1 or (m == 0 and self.far)


def rolled(value, by, axis):
    return pltpu.roll(value, by % value.shape[axis], axis)


ITEMS = [("now", 0), ("now", 1), ("before", 0), ("before", 1)] + [
    (key, 0) for key in ("velocity", "eps", "delta", "tilt", "azimuth")
]


def edge_rows(tile):
    placed = [
        (item, m, 0, 2, 2 * (item * tile.nx + m)) for item in range(len(ITEMS)) for m in range(tile.nx)
    ]
    base = 2 * len(ITEMS) * tile.nx
    placed += [(item, m, 2, 1, base + item * tile.nx + m) for item in range(2) for m in range(tile.nx)]
    return placed, base + 2 * tile.nx


def pack_edges(tile, raw):
    placed, total = edge_rows(tile)
    assert tile.nx % 4 == 0
    outs = {"odd": (total, tile.nz), "even": (total, tile.nz), "near": (2, tile.ny, tile.nz)}
    if tile.far:
        outs["far"] = outs["near"]
    outs.update({key: (value.shape, value.dtype) for key, value in raw.items()})

    def body(r):
        copies = {}
        for i, key in enumerate(raw):
            copies[key] = pltpu.make_async_copy(r[key + "_hbm"], r[key], r["done"].at[i])
            copies[key].start()
        odd = is_odd("gy") == 1
        sub = lax.broadcasted_iota(jnp.int32, (8, tile.nz), 0)
        blocks = {}
        for item, m, first, count, place in placed:
            key, c = ITEMS[item]
            if key in copies:
                copies.pop(key).wait()
                if key == "now":
                    for part in range(2):
                        r["near"][part] = r["now"][0, part, tile.place(tile.nx - 1)]
                        if tile.far:
                            r["far"][part] = r["now"][0, part, tile.place(0)]
            here, slot = tile.place(m), place % 8
            ref = r[key].at[0, c] if key in ("now", "before") else r[key]
            for end, start, from_row in (("top", tile.ny - 8, 8 - first - count), ("low", 0, first)):
                block = ref[here, pl.ds(start, 8), :].astype(F32)
                moved = rolled(block, slot - from_row, 0) if slot != from_row else block
                old = blocks.get(end)
                blocks[end] = moved if slot == 0 else jnp.where(sub >= slot, moved, old)
            if slot + count == 8:
                rows = pl.ds(place - slot, 8)
                r["even"][rows, :] = jnp.where(odd, blocks["low"], blocks["top"])
                r["odd"][rows, :] = jnp.where(odd, blocks["top"], blocks["low"])

    ins = {key + "_hbm": value for key, value in raw.items()}
    spaces = {key: pltpu.HBM for key in ins}
    return run_kernel(
        body, ins, outs, spaces=spaces, copies=len(raw), name="pack_edges", flops=10**6
    )


def halo_block(tile, r, item, m):
    odd = is_odd("gy") == 1
    has_upper = lax.axis_index("gy") < tile.gy - 1
    has_lower = lax.axis_index("gy") > 0
    sub = lax.broadcasted_iota(jnp.int32, (8, tile.nz), 0)
    result = jnp.zeros((8, tile.nz), F32)
    for i, plane, first, count, place in edge_rows(tile)[0]:
        if (i, plane) != (item, m):
            continue
        slot = place % 8
        rows = pl.ds(place - slot, 8)
        even_got, odd_got = r["got_even"][rows, :], r["got_odd"][rows, :]
        upper = jnp.where(odd, odd_got, even_got)
        lower = jnp.where(odd, even_got, odd_got)
        upper = rolled(upper, first - slot, 0) if slot != first else upper
        bottom = 8 - first - count
        lower = rolled(lower, bottom - slot, 0) if slot != bottom else lower
        result = jnp.where((sub >= first) & (sub < first + count) & has_upper, upper, result)
        result = jnp.where((sub >= bottom) & (sub < bottom + count) & has_lower, lower, result)
    return result


def angle_tables(rows):
    level = lax.broadcasted_iota(jnp.int32, (rows, LANES), 1).astype(F32)
    theta = level * (0.5 * math.pi / LEVELS)
    azimuth = level * (2.0 * math.pi / LEVELS)
    sin_t, cos_t, sin_p, cos_p = jnp.sin(theta), jnp.cos(theta), jnp.sin(azimuth), jnp.cos(azimuth)
    return sin_t, cos_t, sin_p, cos_p


def store_weights(out, m, rows, j, tables, sign, velocity, eps, delta, tilt, azimuth):
    def look(table, level):
        return jnp.take_along_axis(table, level, axis=1)

    sin_t, cos_t = look(tables[0], tilt), look(tables[1], tilt)
    sin_p, cos_p = look(tables[2], azimuth), look(tables[3], azimuth)
    sin2_t, half_t = sin_t * sin_t, 0.5 * sin_t * cos_t
    speed_sq = velocity * velocity
    root = jnp.sqrt(1.0 + 2.0 * delta)
    values = (
        sin2_t * (cos_p * cos_p),
        sin2_t * (sin_p * sin_p),
        cos_t * cos_t,
        (0.5 * sign) * (sin2_t * (sin_p * cos_p)),
        half_t * sin_p,
        sign * (half_t * cos_p),
        speed_sq * (1.0 + 2.0 * eps),
        speed_sq * root,
        speed_sq,
    )
    for k, value in enumerate(values):
        out[k, m, rows, lanes_of(j)] = value


def x_sign():
    return 1.0 - 2.0 * is_odd("gx").astype(F32)


def own_state(tile, raw, forward):
    coefs = ("velocity", "eps", "delta", "tilt", "azimuth")

    def body(r):
        copy = pltpu.make_async_copy(r["forward_hbm"], r["forward"], r["done"].at[0])
        copy.start()
        tables = angle_tables(8)
        sign = x_sign()

        def plane(m, _):
            here = tile.place(m)
            for j in range(tile.nj):
                for start in range(0, tile.ny, 8):
                    rows = pl.ds(start, 8)
                    store_weights(
                        r["w"], m, rows, j, tables, sign,
                        *(r[key][here, rows, lanes_of(j)] for key in coefs),
                    )
            return 0

        lax.fori_loop(0, tile.nx, plane, 0)
        copy.wait()

    ins = {key: raw[key] for key in coefs}
    ins["forward_hbm"] = forward
    outs = {"w": (9, tile.nx, tile.ny, tile.nz), "forward": (forward.shape, forward.dtype)}
    return run_kernel(
        body, ins, outs, spaces={"forward_hbm": pltpu.HBM}, copies=1, name="own_state",
        flops=3 * 10**6,
    )


def surface_load(tile, cell, count, trace, after):
    channels = cell.shape[1]
    width = tile.ny * tile.gy

    def body(r):
        start_x = lax.axis_index("gx") * tile.nx
        start_y = lax.axis_index("gy") * tile.ny
        cell_here = r["cell"][...]
        slots = lax.broadcasted_iota(jnp.int32, (1, channels), 1)
        live = slots < r["count"][...].reshape(1, 1)
        if width & (width - 1) == 0:
            row_of = cell_here & (width - 1)
        else:
            row_of = lax.rem(cell_here, jnp.full_like(cell_here, width))
        place = lax.broadcasted_iota(jnp.int32, (tile.rows, 1), 0)
        place = jnp.where(place >= tile.ny + HALO, place - tile.rows, place) + start_y
        onehot = jnp.where(row_of == place, 1.0, 0.0)
        first = lax.broadcasted_iota(jnp.int32, (tile.rows, LANES), 1) == 0
        pad = jnp.zeros((8 - tile.steps, channels), F32)
        trace_here = r["trace"][0]
        loads = []
        for m in range(tile.nx):
            low = (start_x + tile.place(m)) * width
            inside = live & (cell_here >= low) & (cell_here < low + width)
            loads += [jnp.where(inside, trace_here, 0.0), pad]
        rest, parts = jnp.concatenate(loads, axis=0), []
        for _ in range(3):
            part = rest.astype(jnp.bfloat16)
            rest = rest - part.astype(F32)
            parts.append(part.astype(F32))
        group = 8 * tile.nx
        if 3 * group < LANES:
            parts.append(jnp.zeros((LANES - 3 * group, channels), F32))
        columns = lax.dot_general(
            onehot.astype(jnp.bfloat16), jnp.concatenate(parts, axis=0).astype(jnp.bfloat16),
            (((1,), (1,)), ((), ())), preferred_element_type=F32,
        )
        columns = columns + (rolled(columns, -group, 1) + rolled(columns, -2 * group, 1))
        for m in range(tile.nx):
            for t in range(tile.steps):
                column = rolled(columns, -8 * m - t, 1) if m + t else columns
                r["surface"][t, m] = jnp.where(first, column, 0.0)

    assert tile.steps <= 8 and 24 * tile.nx <= LANES
    ins = {"cell": cell, "count": count, "trace": trace, "after": after}
    outs = {"surface": (tile.steps, tile.nx, tile.rows, LANES)}
    out = run_kernel(body, ins, outs, name="surface_load", flops=2 * 10**6)
    return out["surface"]


def halo_edges(tile, got_even, got_odd, after):
    outs = {"near": (2, 8, tile.nz)}
    if tile.far:
        outs["far"] = outs["near"]

    def body(r):
        for key in outs:
            for c in range(2):
                r[key][c] = halo_block(tile, r, c, tile.nx - 1 if key == "near" else 0)

    ins = {"got_odd": got_odd, "got_even": got_even, "after": after}
    return run_kernel(body, ins, outs, name="halo_edges", flops=10**5)


def halo_state(tile, got_even, got_odd, after):
    outs = {"uh": (4, tile.nx, 8, tile.nz), "wh": (9, tile.nx, 8, tile.nz)}

    def body(r):
        tables = angle_tables(8)
        sign = x_sign()
        for m in range(tile.nx):
            for item in range(4):
                r["uh"][item, m] = halo_block(tile, r, item, m)
            coefs = [halo_block(tile, r, item, m) for item in range(4, 9)]
            for j in range(tile.nj):
                part = [value[:, j * LANES : (j + 1) * LANES] for value in coefs]
                store_weights(
                    r["wh"], m, pl.ds(0, 8), j, tables, sign, *part[:3],
                    part[3].astype(jnp.int32), part[4].astype(jnp.int32),
                )

    ins = {"got_odd": got_odd, "got_even": got_even, "after": after}
    return run_kernel(body, ins, outs, name="halo_state", flops=10**6)


class Stage:
    def __init__(self, tile, state, ops, pieces, name, after=None):
        self.tile, self.state, self.ops, self.pieces, self.name = tile, state, ops, pieces, name
        self.ins, self.outs, self.scratch = {}, {}, {}
        if after is not None:
            self.ins["after"] = after

    def need(self, key):
        if key not in self.outs and key not in self.scratch:
            self.ins[key] = self.state[key]

    def run(self):
        tile = self.tile
        for t, m in self.ops:
            last = t == tile.steps - 1
            for key in ("w", "forward"):
                self.need(key)
            if ("part", t, m) in self.state:
                self.need(("part", t, m))
            for k in (m - 1, m, m + 1):
                if k == -1 and not tile.far:
                    continue
                if k == m - 1 and ("part", t, m) in self.state:
                    continue
                if k in (-1, tile.nx):
                    key = "xf" if k == -1 else "xn"
                    self.need((key, t))
                    if t == 0:
                        self.need((key + "h", t))
                elif t == 0:
                    for key in ("now", "uh"):
                        self.need(key)
                else:
                    self.need(("u", t, k))
            if t <= 1:
                for key in ("before" if t == 0 else "now", "uh"):
                    self.need(key)
            else:
                self.need(("u", t - 1, m))
            if not last:
                self.need("wh")
            self.need("surface")
            if t > 0:
                self.need(("g", t - 1, m))
            rows = tile.ny if last else tile.rows
            self.outs[("u", t + 1, m)] = (2, rows, tile.nz)
            if not last and tile.edge(m):
                self.outs[("e", t + 1, m)] = (2 * tile.ny + 8, tile.nz)
            total = (tile.nj, 3, tile.ny, LANES)
            if last and any(m in planes for planes in self.pieces):
                self.scratch[("g", t, m)] = pltpu.VMEM(total, F32)
            else:
                self.outs[("g", t, m)] = total
        for planes in self.pieces:
            for m in planes:
                self.need(("g", tile.steps - 1, m))
            block = (len(planes), 3, tile.ny, tile.nz // tile.src)
            if self.halved(planes):
                self.outs[("keep", planes)] = (2, *block)
                self.outs[("send", planes)] = (2, *block)
            else:
                for k in range(tile.src):
                    self.outs[("s", planes, k)] = block
        flops = len(self.ops) * 2 * 10**6 + 10**5
        out = run_kernel(self.body, self.ins, self.outs, self.scratch, name=self.name, flops=flops)
        self.state.update(out)

    def body(self, r):
        tile = self.tile
        for t, m in self.ops:
            self.update(r, t, m)
        me = lax.axis_index("src")
        per = tile.nj // tile.src
        for planes in self.pieces:
            for i, m in enumerate(planes):
                for k in range(tile.src):
                    owner = jnp.bitwise_xor(me, k)
                    if self.halved(planes):
                        second = tile.second[tile.plan[planes][1]][1]
                        first = 1 if second > 1 else 2
                        kind = "keep" if k in (0, second) else "send"
                        target = r[(kind, planes)].at[0 if k in (0, first) else 1]
                    else:
                        target = r[("s", planes, k)]
                    for part in range(per):
                        target[i, :, :, lanes_of(part)] = r[("g", tile.steps - 1, m)][
                            owner * per + part
                        ]

    def halved(self, planes):
        return self.tile.plan[planes][1] is not None

    def field(self, r, t, m, c, j):
        tile, lanes = self.tile, lanes_of(j)
        if m == -1 and not tile.far:
            return None
        if m in (-1, tile.nx):
            key = "xf" if m == -1 else "xn"
            if t == 0:
                own, halo = r[(key, t)][c, :, lanes], r[(key + "h", t)][c, :, lanes]
            else:
                own = r[(key, t)][pl.ds(c * tile.ny, tile.ny), lanes]
                halo = r[(key, t)][pl.ds(2 * tile.ny, 8), lanes]
                if c == 1:
                    sub = lax.broadcasted_iota(jnp.int32, (8, LANES), 0)
                    halo = jnp.where(sub < HALO, rolled(halo, -2, 0), rolled(halo, 2, 0))
            return jnp.concatenate([own, halo], axis=0)
        if t > 0:
            return r[("u", t, m)][c, :, lanes]
        ref, item = (r["now"], c) if t == 0 else (r["before"], 2 + c)
        return jnp.concatenate(
            [ref[0, c, tile.place(m), :, lanes], r["uh"][item, m, :, lanes]], axis=0
        )

    def operators(self, r, t, m, rows, weight, local, above):
        tile = self.tile
        lane = lax.broadcasted_iota(jnp.int32, (tile.rows, LANES), 1)
        at_first, at_last = lane == 0, lane == LANES - 1

        def deeper(blocks):
            moved = [rolled(block, -1, 1) for block in blocks] + [0.0]
            return [jnp.where(at_last, moved[j + 1], moved[j]) for j in range(tile.nj)]

        def shallower(blocks):
            moved = [rolled(block, 1, 1) for block in blocks] + [0.0]
            return [jnp.where(at_first, moved[j - 1], moved[j]) for j in range(tile.nj)]

        def both(block):
            return rolled(block, -1, 0)[:rows], rolled(block, 1, 0)[:rows]

        centers, halves, shifted = [], [], []
        for c in range(2):
            total_x, diff_x = [], []
            for j in range(tile.nj):
                up = self.field(r, t, m + 1, c, j) if above else None
                down = self.field(r, t, m - 1, c, j) if local else None
                if down is None:
                    total_x.append(up)
                    diff_x.append(up)
                else:
                    total_x.append(down if up is None else up + down)
                    diff_x.append(-down if up is None else up - down)
            halves.append((total_x, diff_x))
            moved = [deeper(diff_x), shallower(diff_x)]
            if local:
                centers.append([self.field(r, t, m, c, j) for j in range(tile.nj)])
                moved += [deeper(centers[c]), shallower(centers[c])]
            shifted.append(moved)

        for j in range(tile.nj):
            weights = [weight(k, j) for k in range(6)]
            results = []
            for c in range(2):
                total_x, diff_x = halves[c][0][j][:rows], halves[c][1][j]
                mixed_xz = (shifted[c][0][j] - shifted[c][1][j])[:rows]
                up, down = both(diff_x)
                axial = weights[0] * total_x + weights[3] * (up - down) + weights[5] * mixed_xz
                laplace = total_x
                if local:
                    center = centers[c][j]
                    below, above_z = shifted[c][2][j], shifted[c][3][j]
                    total_z, slope_z = (below + above_z)[:rows], below - above_z
                    up, down = both(center)
                    total_y = up + down
                    up, down = both(slope_z)
                    axial = axial + (
                        weights[1] * total_y + weights[2] * total_z + weights[4] * (up - down)
                    )
                    center = center[:rows]
                    laplace = laplace + total_y + total_z - 4.0 * center
                    results.append(laplace - axial if c == 0 else axial - 2.0 * center)
                else:
                    results.append(laplace - axial if c == 0 else axial)
            yield results

    def weight_of(self, r, m, last):
        def weight(k, j):
            own = r["w"][k, m, :, lanes_of(j)]
            return own if last else jnp.concatenate([own, r["wh"][k, m, :, lanes_of(j)]], axis=0)

        return weight

    def update(self, r, t, m):
        tile = self.tile
        last = t == tile.steps - 1
        rows = tile.ny if last else tile.rows
        weight = self.weight_of(r, m, last)
        ahead = ("part", t, m) in r
        spatial = self.operators(r, t, m, rows, weight, not ahead, True)
        for j in range(tile.nj):
            horiz, axial = next(spatial)
            if ahead:
                horiz = horiz + r[("part", t, m)][0, :, lanes_of(j)]
                axial = axial + r[("part", t, m)][1, :, lanes_of(j)]
            centers = [self.field(r, t, m, c, j)[:rows] for c in range(2)]
            stretched, rooted, speed_sq = (weight(k, j) for k in range(6, 9))
            before = [self.field(r, t - 1, m, c, j)[:rows] for c in range(2)]
            new_p = 2.0 * centers[0] - before[0] + stretched * horiz + rooted * axial
            new_q = 2.0 * centers[1] - before[1] + rooted * horiz + speed_sq * axial
            if j == 0:
                new_p = new_p + r["surface"][t, m][:rows]
            r[("u", t + 1, m)][0, :, lanes_of(j)] = new_p
            r[("u", t + 1, m)][1, :, lanes_of(j)] = new_q
            if ("e", t + 1, m) in r:
                edge, lanes = r[("e", t + 1, m)], lanes_of(j)
                edge[: tile.ny, lanes] = new_p[: tile.ny]
                edge[tile.ny : 2 * tile.ny, lanes] = new_q[: tile.ny]
                sub = lax.broadcasted_iota(jnp.int32, (8, LANES), 0)
                p_rows, q_rows = new_p[tile.ny :], new_q[tile.ny :]
                q_rows = jnp.where(sub < HALO, rolled(q_rows, 2, 0), rolled(q_rows, -2, 0))
                edge[2 * tile.ny :, lanes] = jnp.where((sub < 2) | (sub >= 6), p_rows, q_rows)
            here = tile.place(m)
            forward_p = r["forward"][t, 0, 0, here, :, lanes_of(j)].astype(F32)
            forward_q = r["forward"][t, 0, 1, here, :, lanes_of(j)].astype(F32)
            horiz, axial = horiz[: tile.ny], axial[: tile.ny]
            terms = (
                forward_p * horiz,
                forward_p * axial + forward_q * horiz,
                forward_q * axial,
            )
            for k, term in enumerate(terms):
                if t > 0:
                    term = term + r[("g", t - 1, m)][j, k]
                r[("g", t, m)][j, k] = term


def run_ahead(tile, state, ops, name):
    stage = Stage(tile, state, [], [], name)
    ins, outs = {"w": state["w"], "wh": state["wh"]}, {}
    for t, m in ops:
        for k in (m - 1, m):
            ins[("u", t, k)] = state[("u", t, k)]
        rows = tile.ny if t == tile.steps - 1 else tile.rows
        outs[("part", t, m)] = (2, rows, tile.nz)

    def body(r):
        for t, m in ops:
            last = t == tile.steps - 1
            rows = tile.ny if last else tile.rows
            spatial = stage.operators(r, t, m, rows, stage.weight_of(r, m, last), True, False)
            for j, (horiz, axial) in enumerate(spatial):
                r[("part", t, m)][0, :, lanes_of(j)] = horiz
                r[("part", t, m)][1, :, lanes_of(j)] = axial

    state.update(run_kernel(body, ins, outs, name=name, flops=10**6))


def xor_swap(tile, block, k):
    return lax.ppermute(block, "src", [(i, i ^ k) for i in range(tile.src)])


def second_round(tile, state, pieces, k, after, along):
    ins, outs, start = {"after": after}, {}, 0
    if along is not None:
        ins["along"] = state[("s", along, k)]
        start = len(along)
    count = start
    for planes in pieces:
        ins[("keep", planes)], ins[("got", planes)] = state[("keep", planes)], state[("got", planes)]
        outs[("s", planes, 0)] = state[("keep", planes)].shape[1:]
        count += len(planes)
    outs["passed"] = (count, *outs[("s", pieces[0], 0)][1:])

    def body(r):
        if along is not None:
            r["passed"][:start] = r["along"][...]
        at = start
        for planes in pieces:
            keep, got = r[("keep", planes)], r[("got", planes)]
            r[("s", planes, 0)][...] = keep[0] + got[0]
            r["passed"][at : at + len(planes)] = keep[1] + got[1]
            at += len(planes)

    state.update(run_kernel(body, ins, outs, name="second_round", flops=10**5))
    got = xor_swap(tile, state["passed"], k)
    at = start
    if along is not None:
        state[("r", along, k)] = (got, 0)
    for planes in pieces:
        state[("r", planes, k)] = (got, at)
        at += len(planes)


def combine(tile, state, pieces):
    depth = tile.nz // tile.src
    ins = {key: state[key] for key in ("velocity", "eps", "delta")}
    starts = {}
    for k in ORDER:
        for planes in pieces:
            if ("r", planes, k) in state:
                ins[("r", planes, k)], starts[(planes, k)] = state[("r", planes, k)]
    for planes in pieces:
        ins[("s", planes, 0)] = state[("s", planes, 0)]
    shape = (tile.nx, tile.ny, depth)

    def body(r):
        lanes = pl.ds(pl.multiple_of(lax.axis_index("src") * depth, LANES), depth)
        for planes in pieces:
            for i, m in enumerate(planes):
                here = tile.place(m)
                sums = []
                for item in range(3):
                    total = r[("s", planes, 0)][i, item]
                    for k in range(1, tile.src):
                        if (planes, k) in starts:
                            total = total + r[("r", planes, k)][starts[(planes, k)] + i, item]
                    sums.append(total)
                velocity = r["velocity"][here, :, lanes]
                root = jnp.sqrt(1.0 + 2.0 * r["delta"][here, :, lanes])
                stretch = 1.0 + 2.0 * r["eps"][here, :, lanes]
                speed_sq = velocity * velocity
                r["gv"][here] = 2.0 * velocity * (stretch * sums[0] + root * sums[1] + sums[2])
                r["ge"][here] = 2.0 * speed_sq * sums[0]
                r["gd"][here] = speed_sq / root * sums[1]

    out = run_kernel(body, ins, {"gv": shape, "ge": shape, "gd": shape}, name="combine", flops=10**6, final=True)
    return out["gv"], out["ge"], out["gd"]


def final_fields(tile, state):
    keys = [("u", tile.steps, m) for m in range(tile.nx)]

    def body(r):
        for m, key in enumerate(keys):
            for c in range(2):
                r["out"][0, c, tile.place(m)] = r[key][c]


    outs = {"out": (1, 2, tile.nx, tile.ny, tile.nz)}
    out = run_kernel(
        body, {key: state[key] for key in keys}, outs, name="final_fields", flops=10**6, final=True
    )
    return out["out"]


def on_device(
    mesh,
    adjoint_now,
    adjoint_before,
    forward_field,
    velocity,
    thomsen_eps,
    thomsen_delta,
    tilt_level,
    azimuth_level,
    channel_cell,
    channel_count,
    residual_trace,
):
    tile = Tile(mesh, velocity, forward_field.shape[0])
    raw = {
        "now": adjoint_now,
        "before": adjoint_before,
        "velocity": velocity,
        "eps": thomsen_eps,
        "delta": thomsen_delta,
        "tilt": tilt_level,
        "azimuth": azimuth_level,
    }
    edges = pack_edges(tile, raw)
    state = {key: edges[key] for key in raw}

    def exchange(key, t, near, far):
        state[("xn" + key, t)] = swap(near, "gx", tile.gx, 0)
        if tile.far:
            state[("xf" + key, t)] = swap(far, "gx", tile.gx, 1)

    got_odd = swap_rows(tile, edges["odd"], 1)
    got_even = swap_rows(tile, edges["even"], 0)
    exchange("", 0, edges["near"], edges.get("far"))
    state.update(own_state(tile, state, forward_field))
    state["surface"] = surface_load(
        tile, channel_cell, channel_count, residual_trace, state["w"]
    )
    halo = halo_edges(tile, got_even, got_odd, state["surface"])
    exchange("h", 0, halo["near"], halo.get("far"))
    state.update(halo_state(tile, got_even, got_odd, halo["near"]))

    ops = [(t, m) for t in range(tile.steps) for m in range(tile.nx)]
    pieces = list(tile.plan)
    for phase in range(tile.steps + 1):
        mine = [op for op in ops if max(tile.phase(*op), op[0] // 2) == phase]
        front = [op for op in mine if phase > 0 and op[0] == phase - 1 and tile.edge(op[1])]
        bulk = [op for op in mine if op not in front]
        done = [planes for planes in pieces if tile.plan[planes][0] == phase]
        if phase == tile.steps:
            front, bulk = mine, []
        if front:
            Stage(tile, state, front, [] if bulk else done, f"front_{phase}", state.get("token")).run()
            state["token"] = state[("u", phase, tile.nx - 1)]
            if phase < tile.steps:
                exchange("", phase, state[("e", phase, tile.nx - 1)], state.get(("e", phase, 0)))
        if bulk:
            Stage(tile, state, bulk, done, f"bulk_{phase}").run()
            state["token"] = state[("u", bulk[0][0] + 1, bulk[0][1])]
        later = [(name, k) for name, (when, k, _) in tile.second.items() if when == phase]
        direct = [planes for planes in done if tile.plan[planes][1] is None]
        joined = [k for name, k in later if tile.second[name][2] and direct]
        for planes in done:
            if planes not in direct:
                first = 1 if tile.second[tile.plan[planes][1]][1] > 1 else 2
                state[("got", planes)] = xor_swap(tile, state[("send", planes)], first)
                continue
            for k in range(tile.src - 1, 0, -1):
                if k not in joined:
                    state[("r", planes, k)] = (xor_swap(tile, state[("s", planes, k)], k), 0)
        if phase == 1 and not tile.far and tile.steps == 3:
            run_ahead(tile, state, [(1, tile.nx - 1), (2, tile.nx - 2)], "ahead")
        for name, k in later:
            group = [planes for planes in pieces if tile.plan[planes][1] == name]
            along = direct[0] if k in joined else None
            after = state["token"]
            second_round(tile, state, group, k, after, along)
            if phase < tile.steps:
                state["token"] = state["passed"]
    following = final_fields(tile, state)
    return (following, *combine(tile, state, pieces))


def solution(mesh):
    placed = (
        P("src", None, "gx", "gy", None),
        P("src", None, "gx", "gy", None),
        P(None, "src", None, "gx", "gy", None),
        P("gx", "gy", None),
        P("gx", "gy", None),
        P("gx", "gy", None),
        P("gx", "gy", None),
        P("gx", "gy", None),
        P("src", None),
        P("src"),
        P("src", None, None),
    )

    def program(*args):
        return on_device(mesh, *args)

    return jax.shard_map(
        program,
        mesh=mesh,
        in_specs=placed,
        out_specs=(
            P("src", None, "gx", "gy", None),
            P("gx", "gy", "src"),
            P("gx", "gy", "src"),
            P("gx", "gy", "src"),
        ),
        check_vma=False,
    )
```

```python
import math

import jax
import jax.numpy as jnp
from jax import lax
from jax.experimental import pallas as pl
from jax.experimental.pallas import tpu as pltpu
from jax.sharding import PartitionSpec as P

LEVELS = 32
LANES = 128
HALO = 4
ORDER = (3, 2, 1)
WAVE = (
    {(0, 1): (1, "a"), (2,): (2, "b"), (3,): (3, None)},
    {"a": (2, 2, False), "b": (3, 3, True)},
)
VMEM_LIMIT = 8 * 1024 * 1024
F32 = jnp.float32


def run_kernel(body, ins, outs, scratch=None, spaces=None, copies=0, name=None, flops=0, final=False):
    scratch, spaces = scratch or {}, spaces or {}
    names = list(ins) + list(outs) + list(scratch) + ["done"]
    ins = {
        key: pltpu.with_memory_space_constraint(value, pltpu.HBM)
        if spaces.get(key) == pltpu.HBM
        else value
        for key, value in ins.items()
    }

    def kernel(*refs):
        body(dict(zip(names, refs)))

    results = pl.pallas_call(
        kernel,
        name=name,
        out_shape=[
            jax.ShapeDtypeStruct(shape, F32) if final else pltpu.VMEM(shape, kind)
            for shape, kind in (
                entry if isinstance(entry[0], tuple) else (entry, F32) for entry in outs.values()
            )
        ],
        in_specs=[
            pl.BlockSpec(memory_space=spaces.get(key, pltpu.VMEM)) for key in ins
        ],
        out_specs=[pl.BlockSpec(memory_space=pltpu.VMEM)] * len(outs),
        scratch_shapes=list(scratch.values())
        + [pltpu.SemaphoreType.DMA((copies,))] * (copies > 0),
        compiler_params=pltpu.CompilerParams(vmem_limit_bytes=VMEM_LIMIT),
        cost_estimate=pl.CostEstimate(flops=flops, bytes_accessed=flops // 8, transcendentals=0),
    )(*ins.values())
    return dict(zip(outs, results))


def pair_swaps(count, first):
    pairs = []
    for low in range(first, count - 1, 2):
        pairs += [(low, low + 1), (low + 1, low)]
    return pairs


def swap(block, axis, count, first):
    return lax.ppermute(block, axis, pair_swaps(count, first))


def swap_rows(tile, block, first):
    pairs = dict(pair_swaps(tile.gy, first))
    across = dict(pair_swaps(tile.src, 0))
    joint = []
    for s in range(tile.src):
        for y in range(tile.gy):
            target = (s, pairs[y]) if y in pairs else (across.get(s, s), y)
            joint.append((s * tile.gy + y, target[0] * tile.gy + target[1]))
    return lax.ppermute(block, ("src", "gy"), joint)


def lanes_of(j):
    return pl.ds(j * LANES, LANES)


def is_odd(axis):
    return lax.rem(lax.axis_index(axis), 2)


class Tile:
    def __init__(self, mesh, velocity, steps):
        self.nx, self.ny, self.nz = velocity.shape
        self.steps = steps
        self.nj = self.nz // LANES
        self.rows = self.ny + 2 * HALO
        self.gx, self.gy, self.src = mesh.shape["gx"], mesh.shape["gy"], mesh.shape["src"]
        self.far = self.gx > 2
        self.plan, self.second = self.reduction()

    def reduction(self):
        last = self.steps - 1
        ready = [self.phase(last, m) for m in range(self.nx)]
        if self.src == 4 and ready == [0, 1, 2, 3]:
            return WAVE
        pieces = {}
        for m, phase in enumerate(ready):
            pieces.setdefault(phase, []).append(m)
        return {tuple(planes): (phase, None) for phase, planes in pieces.items()}, {}

    def place(self, m):
        return m + is_odd("gx") * (self.nx - 1 - 2 * m)

    def phase(self, t, m):
        if m == self.nx or m == -1:
            return t + 2 if (m == self.nx or self.far) else 0
        if t < 0:
            return 0
        return max(self.phase(t - 1, k) for k in (m - 1, m, m + 1))

    def edge(self, m):
        return m == self.nx - 1 or (m == 0 and self.far)


def rolled(value, by, axis):
    return pltpu.roll(value, by % value.shape[axis], axis)


ITEMS = [("now", 0), ("now", 1), ("before", 0), ("before", 1)] + [
    (key, 0) for key in ("velocity", "eps", "delta", "tilt", "azimuth")
]


def edge_rows(tile):
    placed = [
        (item, m, 0, 2, 2 * (item * tile.nx + m)) for item in range(len(ITEMS)) for m in range(tile.nx)
    ]
    base = 2 * len(ITEMS) * tile.nx
    placed += [(item, m, 2, 1, base + item * tile.nx + m) for item in range(2) for m in range(tile.nx)]
    return placed, base + 2 * tile.nx


def pack_edges(tile, raw):
    placed, total = edge_rows(tile)
    assert tile.nx % 4 == 0
    outs = {"odd": (total, tile.nz), "even": (total, tile.nz), "near": (2, tile.ny, tile.nz)}
    if tile.far:
        outs["far"] = outs["near"]
    outs.update({key: (value.shape, value.dtype) for key, value in raw.items()})

    def body(r):
        copies = {}
        for i, key in enumerate(raw):
            copies[key] = pltpu.make_async_copy(r[key + "_hbm"], r[key], r["done"].at[i])
            copies[key].start()
        odd = is_odd("gy") == 1
        sub = lax.broadcasted_iota(jnp.int32, (8, tile.nz), 0)
        blocks = {}
        for item, m, first, count, place in placed:
            key, c = ITEMS[item]
            if key in copies:
                copies.pop(key).wait()
                if key == "now":
                    for part in range(2):
                        r["near"][part] = r["now"][0, part, tile.place(tile.nx - 1)]
                        if tile.far:
                            r["far"][part] = r["now"][0, part, tile.place(0)]
            here, slot = tile.place(m), place % 8
            ref = r[key].at[0, c] if key in ("now", "before") else r[key]
            for end, start, from_row in (("top", tile.ny - 8, 8 - first - count), ("low", 0, first)):
                block = ref[here, pl.ds(start, 8), :].astype(F32)
                moved = rolled(block, slot - from_row, 0) if slot != from_row else block
                old = blocks.get(end)
                blocks[end] = moved if slot == 0 else jnp.where(sub >= slot, moved, old)
            if slot + count == 8:
                rows = pl.ds(place - slot, 8)
                r["even"][rows, :] = jnp.where(odd, blocks["low"], blocks["top"])
                r["odd"][rows, :] = jnp.where(odd, blocks["top"], blocks["low"])

    ins = {key + "_hbm": value for key, value in raw.items()}
    spaces = {key: pltpu.HBM for key in ins}
    return run_kernel(
        body, ins, outs, spaces=spaces, copies=len(raw), name="pack_edges", flops=10**6
    )


def halo_block(tile, r, item, m):
    odd = is_odd("gy") == 1
    has_upper = lax.axis_index("gy") < tile.gy - 1
    has_lower = lax.axis_index("gy") > 0
    sub = lax.broadcasted_iota(jnp.int32, (8, tile.nz), 0)
    result = jnp.zeros((8, tile.nz), F32)
    for i, plane, first, count, place in edge_rows(tile)[0]:
        if (i, plane) != (item, m):
            continue
        slot = place % 8
        rows = pl.ds(place - slot, 8)
        even_got, odd_got = r["got_even"][rows, :], r["got_odd"][rows, :]
        upper = jnp.where(odd, odd_got, even_got)
        lower = jnp.where(odd, even_got, odd_got)
        upper = rolled(upper, first - slot, 0) if slot != first else upper
        bottom = 8 - first - count
        lower = rolled(lower, bottom - slot, 0) if slot != bottom else lower
        result = jnp.where((sub >= first) & (sub < first + count) & has_upper, upper, result)
        result = jnp.where((sub >= bottom) & (sub < bottom + count) & has_lower, lower, result)
    return result


def angle_tables(rows):
    level = lax.broadcasted_iota(jnp.int32, (rows, LANES), 1).astype(F32)
    theta = level * (0.5 * math.pi / LEVELS)
    azimuth = level * (2.0 * math.pi / LEVELS)
    sin_t, cos_t, sin_p, cos_p = jnp.sin(theta), jnp.cos(theta), jnp.sin(azimuth), jnp.cos(azimuth)
    return sin_t, cos_t, sin_p, cos_p


def store_weights(out, m, rows, j, tables, sign, velocity, eps, delta, tilt, azimuth):
    def look(table, level):
        return jnp.take_along_axis(table, level, axis=1)

    sin_t, cos_t = look(tables[0], tilt), look(tables[1], tilt)
    sin_p, cos_p = look(tables[2], azimuth), look(tables[3], azimuth)
    sin2_t, half_t = sin_t * sin_t, 0.5 * sin_t * cos_t
    speed_sq = velocity * velocity
    root = jnp.sqrt(1.0 + 2.0 * delta)
    values = (
        sin2_t * (cos_p * cos_p),
        sin2_t * (sin_p * sin_p),
        cos_t * cos_t,
        (0.5 * sign) * (sin2_t * (sin_p * cos_p)),
        half_t * sin_p,
        sign * (half_t * cos_p),
        speed_sq * (1.0 + 2.0 * eps),
        speed_sq * root,
        speed_sq,
    )
    for k, value in enumerate(values):
        out[k, m, rows, lanes_of(j)] = value


def x_sign():
    return 1.0 - 2.0 * is_odd("gx").astype(F32)


def own_state(tile, raw, forward):
    coefs = ("velocity", "eps", "delta", "tilt", "azimuth")

    def body(r):
        copy = pltpu.make_async_copy(r["forward_hbm"], r["forward"], r["done"].at[0])
        copy.start()
        tables = angle_tables(8)
        sign = x_sign()

        def plane(m, _):
            here = tile.place(m)
            for j in range(tile.nj):
                for start in range(0, tile.ny, 8):
                    rows = pl.ds(start, 8)
                    store_weights(
                        r["w"], m, rows, j, tables, sign,
                        *(r[key][here, rows, lanes_of(j)] for key in coefs),
                    )
            return 0

        lax.fori_loop(0, tile.nx, plane, 0)
        copy.wait()

    ins = {key: raw[key] for key in coefs}
    ins["forward_hbm"] = forward
    outs = {"w": (9, tile.nx, tile.ny, tile.nz), "forward": (forward.shape, forward.dtype)}
    return run_kernel(
        body, ins, outs, spaces={"forward_hbm": pltpu.HBM}, copies=1, name="own_state",
        flops=3 * 10**6,
    )


def surface_load(tile, cell, count, trace, after):
    channels = cell.shape[1]
    width = tile.ny * tile.gy

    def body(r):
        start_x = lax.axis_index("gx") * tile.nx
        start_y = lax.axis_index("gy") * tile.ny
        cell_here = r["cell"][...]
        slots = lax.broadcasted_iota(jnp.int32, (1, channels), 1)
        live = slots < r["count"][...].reshape(1, 1)
        if width & (width - 1) == 0:
            row_of = cell_here & (width - 1)
        else:
            row_of = lax.rem(cell_here, jnp.full_like(cell_here, width))
        place = lax.broadcasted_iota(jnp.int32, (tile.rows, 1), 0)
        place = jnp.where(place >= tile.ny + HALO, place - tile.rows, place) + start_y
        onehot = jnp.where(row_of == place, 1.0, 0.0)
        first = lax.broadcasted_iota(jnp.int32, (tile.rows, LANES), 1) == 0
        pad = jnp.zeros((8 - tile.steps, channels), F32)
        trace_here = r["trace"][0]
        loads = []
        for m in range(tile.nx):
            low = (start_x + tile.place(m)) * width
            inside = live & (cell_here >= low) & (cell_here < low + width)
            loads += [jnp.where(inside, trace_here, 0.0), pad]
        rest, parts = jnp.concatenate(loads, axis=0), []
        for _ in range(3):
            part = rest.astype(jnp.bfloat16)
            rest = rest - part.astype(F32)
            parts.append(part.astype(F32))
        group = 8 * tile.nx
        if 3 * group < LANES:
            parts.append(jnp.zeros((LANES - 3 * group, channels), F32))
        columns = lax.dot_general(
            onehot.astype(jnp.bfloat16), jnp.concatenate(parts, axis=0).astype(jnp.bfloat16),
            (((1,), (1,)), ((), ())), preferred_element_type=F32,
        )
        columns = columns + (rolled(columns, -group, 1) + rolled(columns, -2 * group, 1))
        for m in range(tile.nx):
            for t in range(tile.steps):
                column = rolled(columns, -8 * m - t, 1) if m + t else columns
                r["surface"][t, m] = jnp.where(first, column, 0.0)

    assert tile.steps <= 8 and 24 * tile.nx <= LANES
    ins = {"cell": cell, "count": count, "trace": trace, "after": after}
    outs = {"surface": (tile.steps, tile.nx, tile.rows, LANES)}
    out = run_kernel(body, ins, outs, name="surface_load", flops=2 * 10**6)
    return out["surface"]


def halo_edges(tile, got_even, got_odd, after):
    outs = {"near": (2, 8, tile.nz)}
    if tile.far:
        outs["far"] = outs["near"]

    def body(r):
        for key in outs:
            for c in range(2):
                r[key][c] = halo_block(tile, r, c, tile.nx - 1 if key == "near" else 0)

    ins = {"got_odd": got_odd, "got_even": got_even, "after": after}
    return run_kernel(body, ins, outs, name="halo_edges", flops=10**5)


def halo_state(tile, got_even, got_odd, after):
    outs = {"uh": (4, tile.nx, 8, tile.nz), "wh": (9, tile.nx, 8, tile.nz)}

    def body(r):
        tables = angle_tables(8)
        sign = x_sign()
        for m in range(tile.nx):
            for item in range(4):
                r["uh"][item, m] = halo_block(tile, r, item, m)
            coefs = [halo_block(tile, r, item, m) for item in range(4, 9)]
            for j in range(tile.nj):
                part = [value[:, j * LANES : (j + 1) * LANES] for value in coefs]
                store_weights(
                    r["wh"], m, pl.ds(0, 8), j, tables, sign, *part[:3],
                    part[3].astype(jnp.int32), part[4].astype(jnp.int32),
                )

    ins = {"got_odd": got_odd, "got_even": got_even, "after": after}
    return run_kernel(body, ins, outs, name="halo_state", flops=10**6)


class Stage:
    def __init__(self, tile, state, ops, pieces, name, after=None):
        self.tile, self.state, self.ops, self.pieces, self.name = tile, state, ops, pieces, name
        self.ins, self.outs, self.scratch = {}, {}, {}
        if after is not None:
            self.ins["after"] = after

    def need(self, key):
        if key not in self.outs and key not in self.scratch:
            self.ins[key] = self.state[key]

    def run(self):
        tile = self.tile
        for t, m in self.ops:
            last = t == tile.steps - 1
            for key in ("w", "forward"):
                self.need(key)
            if ("part", t, m) in self.state:
                self.need(("part", t, m))
            for k in (m - 1, m, m + 1):
                if k == -1 and not tile.far:
                    continue
                if k == m - 1 and ("part", t, m) in self.state:
                    continue
                if k in (-1, tile.nx):
                    key = "xf" if k == -1 else "xn"
                    self.need((key, t))
                    if t == 0:
                        self.need((key + "h", t))
                elif t == 0:
                    for key in ("now", "uh"):
                        self.need(key)
                else:
                    self.need(("u", t, k))
            if t <= 1:
                for key in ("before" if t == 0 else "now", "uh"):
                    self.need(key)
            else:
                self.need(("u", t - 1, m))
            if not last:
                self.need("wh")
            self.need("surface")
            if t > 0:
                self.need(("g", t - 1, m))
            rows = tile.ny if last else tile.rows
            self.outs[("u", t + 1, m)] = (2, rows, tile.nz)
            if not last and tile.edge(m):
                self.outs[("e", t + 1, m)] = (2 * tile.ny + 8, tile.nz)
            total = (tile.nj, 3, tile.ny, LANES)
            if last and any(m in planes for planes in self.pieces):
                self.scratch[("g", t, m)] = pltpu.VMEM(total, F32)
            else:
                self.outs[("g", t, m)] = total
        for planes in self.pieces:
            for m in planes:
                self.need(("g", tile.steps - 1, m))
            block = (len(planes), 3, tile.ny, tile.nz // tile.src)
            if self.halved(planes):
                self.outs[("keep", planes)] = (2, *block)
                self.outs[("send", planes)] = (2, *block)
            else:
                for k in range(tile.src):
                    self.outs[("s", planes, k)] = block
        flops = len(self.ops) * 2 * 10**6 + 10**5
        out = run_kernel(self.body, self.ins, self.outs, self.scratch, name=self.name, flops=flops)
        self.state.update(out)

    def body(self, r):
        tile = self.tile
        for t, m in self.ops:
            self.update(r, t, m)
        me = lax.axis_index("src")
        per = tile.nj // tile.src
        for planes in self.pieces:
            for i, m in enumerate(planes):
                for k in range(tile.src):
                    owner = jnp.bitwise_xor(me, k)
                    if self.halved(planes):
                        second = tile.second[tile.plan[planes][1]][1]
                        first = 1 if second > 1 else 2
                        kind = "keep" if k in (0, second) else "send"
                        target = r[(kind, planes)].at[0 if k in (0, first) else 1]
                    else:
                        target = r[("s", planes, k)]
                    for part in range(per):
                        target[i, :, :, lanes_of(part)] = r[("g", tile.steps - 1, m)][
                            owner * per + part
                        ]

    def halved(self, planes):
        return self.tile.plan[planes][1] is not None

    def field(self, r, t, m, c, j):
        tile, lanes = self.tile, lanes_of(j)
        if m == -1 and not tile.far:
            return None
        if m in (-1, tile.nx):
            key = "xf" if m == -1 else "xn"
            if t == 0:
                own, halo = r[(key, t)][c, :, lanes], r[(key + "h", t)][c, :, lanes]
            else:
                own = r[(key, t)][pl.ds(c * tile.ny, tile.ny), lanes]
                halo = r[(key, t)][pl.ds(2 * tile.ny, 8), lanes]
                if c == 1:
                    sub = lax.broadcasted_iota(jnp.int32, (8, LANES), 0)
                    halo = jnp.where(sub < HALO, rolled(halo, -2, 0), rolled(halo, 2, 0))
            return jnp.concatenate([own, halo], axis=0)
        if t > 0:
            return r[("u", t, m)][c, :, lanes]
        ref, item = (r["now"], c) if t == 0 else (r["before"], 2 + c)
        return jnp.concatenate(
            [ref[0, c, tile.place(m), :, lanes], r["uh"][item, m, :, lanes]], axis=0
        )

    def operators(self, r, t, m, rows, weight, local, above):
        tile = self.tile
        lane = lax.broadcasted_iota(jnp.int32, (tile.rows, LANES), 1)
        at_first, at_last = lane == 0, lane == LANES - 1

        def deeper(blocks):
            moved = [rolled(block, -1, 1) for block in blocks] + [0.0]
            return [jnp.where(at_last, moved[j + 1], moved[j]) for j in range(tile.nj)]

        def shallower(blocks):
            moved = [rolled(block, 1, 1) for block in blocks] + [0.0]
            return [jnp.where(at_first, moved[j - 1], moved[j]) for j in range(tile.nj)]

        def both(block):
            return rolled(block, -1, 0)[:rows], rolled(block, 1, 0)[:rows]

        centers, halves, shifted = [], [], []
        for c in range(2):
            total_x, diff_x = [], []
            for j in range(tile.nj):
                up = self.field(r, t, m + 1, c, j) if above else None
                down = self.field(r, t, m - 1, c, j) if local else None
                if down is None:
                    total_x.append(up)
                    diff_x.append(up)
                else:
                    total_x.append(down if up is None else up + down)
                    diff_x.append(-down if up is None else up - down)
            halves.append((total_x, diff_x))
            moved = [deeper(diff_x), shallower(diff_x)]
            if local:
                centers.append([self.field(r, t, m, c, j) for j in range(tile.nj)])
                moved += [deeper(centers[c]), shallower(centers[c])]
            shifted.append(moved)

        for j in range(tile.nj):
            weights = [weight(k, j) for k in range(6)]
            results = []
            for c in range(2):
                total_x, diff_x = halves[c][0][j][:rows], halves[c][1][j]
                mixed_xz = (shifted[c][0][j] - shifted[c][1][j])[:rows]
                up, down = both(diff_x)
                axial = weights[0] * total_x + weights[3] * (up - down) + weights[5] * mixed_xz
                laplace = total_x
                if local:
                    center = centers[c][j]
                    below, above_z = shifted[c][2][j], shifted[c][3][j]
                    total_z, slope_z = (below + above_z)[:rows], below - above_z
                    up, down = both(center)
                    total_y = up + down
                    up, down = both(slope_z)
                    axial = axial + (
                        weights[1] * total_y + weights[2] * total_z + weights[4] * (up - down)
                    )
                    center = center[:rows]
                    laplace = laplace + total_y + total_z - 4.0 * center
                    results.append(laplace - axial if c == 0 else axial - 2.0 * center)
                else:
                    results.append(laplace - axial if c == 0 else axial)
            yield results

    def weight_of(self, r, m, last):
        def weight(k, j):
            own = r["w"][k, m, :, lanes_of(j)]
            return own if last else jnp.concatenate([own, r["wh"][k, m, :, lanes_of(j)]], axis=0)

        return weight

    def update(self, r, t, m):
        tile = self.tile
        last = t == tile.steps - 1
        rows = tile.ny if last else tile.rows
        weight = self.weight_of(r, m, last)
        ahead = ("part", t, m) in r
        spatial = self.operators(r, t, m, rows, weight, not ahead, True)
        for j in range(tile.nj):
            horiz, axial = next(spatial)
            if ahead:
                horiz = horiz + r[("part", t, m)][0, :, lanes_of(j)]
                axial = axial + r[("part", t, m)][1, :, lanes_of(j)]
            centers = [self.field(r, t, m, c, j)[:rows] for c in range(2)]
            stretched, rooted, speed_sq = (weight(k, j) for k in range(6, 9))
            before = [self.field(r, t - 1, m, c, j)[:rows] for c in range(2)]
            new_p = 2.0 * centers[0] - before[0] + stretched * horiz + rooted * axial
            new_q = 2.0 * centers[1] - before[1] + rooted * horiz + speed_sq * axial
            if j == 0:
                new_p = new_p + r["surface"][t, m][:rows]
            r[("u", t + 1, m)][0, :, lanes_of(j)] = new_p
            r[("u", t + 1, m)][1, :, lanes_of(j)] = new_q
            if ("e", t + 1, m) in r:
                edge, lanes = r[("e", t + 1, m)], lanes_of(j)
                edge[: tile.ny, lanes] = new_p[: tile.ny]
                edge[tile.ny : 2 * tile.ny, lanes] = new_q[: tile.ny]
                sub = lax.broadcasted_iota(jnp.int32, (8, LANES), 0)
                p_rows, q_rows = new_p[tile.ny :], new_q[tile.ny :]
                q_rows = jnp.where(sub < HALO, rolled(q_rows, 2, 0), rolled(q_rows, -2, 0))
                edge[2 * tile.ny :, lanes] = jnp.where((sub < 2) | (sub >= 6), p_rows, q_rows)
            here = tile.place(m)
            forward_p = r["forward"][t, 0, 0, here, :, lanes_of(j)].astype(F32)
            forward_q = r["forward"][t, 0, 1, here, :, lanes_of(j)].astype(F32)
            horiz, axial = horiz[: tile.ny], axial[: tile.ny]
            terms = (
                forward_p * horiz,
                forward_p * axial + forward_q * horiz,
                forward_q * axial,
            )
            for k, term in enumerate(terms):
                if t > 0:
                    term = term + r[("g", t - 1, m)][j, k]
                r[("g", t, m)][j, k] = term


def run_ahead(tile, state, ops, name):
    stage = Stage(tile, state, [], [], name)
    ins, outs = {"w": state["w"], "wh": state["wh"]}, {}
    for t, m in ops:
        for key in ("now", "uh") if t == 0 else (("u", t, m - 1), ("u", t, m)):
            ins[key] = state[key]
        rows = tile.ny if t == tile.steps - 1 else tile.rows
        outs[("part", t, m)] = (2, rows, tile.nz)

    def body(r):
        for t, m in ops:
            last = t == tile.steps - 1
            rows = tile.ny if last else tile.rows
            spatial = stage.operators(r, t, m, rows, stage.weight_of(r, m, last), True, False)
            for j, (horiz, axial) in enumerate(spatial):
                r[("part", t, m)][0, :, lanes_of(j)] = horiz
                r[("part", t, m)][1, :, lanes_of(j)] = axial

    state.update(run_kernel(body, ins, outs, name=name, flops=10**6))


def xor_swap(tile, block, k):
    return lax.ppermute(block, "src", [(i, i ^ k) for i in range(tile.src)])


def second_round(tile, state, pieces, k, after, along):
    ins, outs, start = {"after": after}, {}, 0
    if along is not None:
        ins["along"] = state[("s", along, k)]
        start = len(along)
    count = start
    for planes in pieces:
        ins[("keep", planes)], ins[("got", planes)] = state[("keep", planes)], state[("got", planes)]
        outs[("s", planes, 0)] = state[("keep", planes)].shape[1:]
        count += len(planes)
    outs["passed"] = (count, *outs[("s", pieces[0], 0)][1:])

    def body(r):
        if along is not None:
            r["passed"][:start] = r["along"][...]
        at = start
        for planes in pieces:
            keep, got = r[("keep", planes)], r[("got", planes)]
            r[("s", planes, 0)][...] = keep[0] + got[0]
            r["passed"][at : at + len(planes)] = keep[1] + got[1]
            at += len(planes)

    state.update(run_kernel(body, ins, outs, name="second_round", flops=10**5))
    got = xor_swap(tile, state["passed"], k)
    at = start
    if along is not None:
        state[("r", along, k)] = (got, 0)
    for planes in pieces:
        state[("r", planes, k)] = (got, at)
        at += len(planes)


def combine(tile, state, pieces):
    depth = tile.nz // tile.src
    ins = {key: state[key] for key in ("velocity", "eps", "delta")}
    starts = {}
    for k in ORDER:
        for planes in pieces:
            if ("r", planes, k) in state:
                ins[("r", planes, k)], starts[(planes, k)] = state[("r", planes, k)]
    for planes in pieces:
        ins[("s", planes, 0)] = state[("s", planes, 0)]
    shape = (tile.nx, tile.ny, depth)

    def body(r):
        lanes = pl.ds(pl.multiple_of(lax.axis_index("src") * depth, LANES), depth)
        for planes in pieces:
            for i, m in enumerate(planes):
                here = tile.place(m)
                sums = []
                for item in range(3):
                    total = r[("s", planes, 0)][i, item]
                    for k in range(1, tile.src):
                        if (planes, k) in starts:
                            total = total + r[("r", planes, k)][starts[(planes, k)] + i, item]
                    sums.append(total)
                velocity = r["velocity"][here, :, lanes]
                root = jnp.sqrt(1.0 + 2.0 * r["delta"][here, :, lanes])
                stretch = 1.0 + 2.0 * r["eps"][here, :, lanes]
                speed_sq = velocity * velocity
                r["gv"][here] = 2.0 * velocity * (stretch * sums[0] + root * sums[1] + sums[2])
                r["ge"][here] = 2.0 * speed_sq * sums[0]
                r["gd"][here] = speed_sq / root * sums[1]

    out = run_kernel(body, ins, {"gv": shape, "ge": shape, "gd": shape}, name="combine", flops=10**6, final=True)
    return out["gv"], out["ge"], out["gd"]


def final_fields(tile, state):
    keys = [("u", tile.steps, m) for m in range(tile.nx)]

    def body(r):
        for m, key in enumerate(keys):
            for c in range(2):
                r["out"][0, c, tile.place(m)] = r[key][c]


    outs = {"out": (1, 2, tile.nx, tile.ny, tile.nz)}
    out = run_kernel(
        body, {key: state[key] for key in keys}, outs, name="final_fields", flops=10**6, final=True
    )
    return out["out"]


def on_device(
    mesh,
    adjoint_now,
    adjoint_before,
    forward_field,
    velocity,
    thomsen_eps,
    thomsen_delta,
    tilt_level,
    azimuth_level,
    channel_cell,
    channel_count,
    residual_trace,
):
    tile = Tile(mesh, velocity, forward_field.shape[0])
    raw = {
        "now": adjoint_now,
        "before": adjoint_before,
        "velocity": velocity,
        "eps": thomsen_eps,
        "delta": thomsen_delta,
        "tilt": tilt_level,
        "azimuth": azimuth_level,
    }
    edges = pack_edges(tile, raw)
    state = {key: edges[key] for key in raw}

    def exchange(key, t, near, far):
        state[("xn" + key, t)] = swap(near, "gx", tile.gx, 0)
        if tile.far:
            state[("xf" + key, t)] = swap(far, "gx", tile.gx, 1)

    got_odd = swap_rows(tile, edges["odd"], 1)
    got_even = swap_rows(tile, edges["even"], 0)
    exchange("", 0, edges["near"], edges.get("far"))
    state.update(own_state(tile, state, forward_field))
    state["surface"] = surface_load(
        tile, channel_cell, channel_count, residual_trace, state["w"]
    )
    halo = halo_edges(tile, got_even, got_odd, state["surface"])
    exchange("h", 0, halo["near"], halo.get("far"))
    state.update(halo_state(tile, got_even, got_odd, halo["near"]))

    ops = [(t, m) for t in range(tile.steps) for m in range(tile.nx)]
    pieces = list(tile.plan)
    for phase in range(tile.steps + 1):
        mine = [op for op in ops if max(tile.phase(*op), op[0] // 2) == phase]
        front = [op for op in mine if phase > 0 and op[0] == phase - 1 and tile.edge(op[1])]
        bulk = [op for op in mine if op not in front]
        done = [planes for planes in pieces if tile.plan[planes][0] == phase]
        if phase == tile.steps:
            front, bulk = mine, []
        if front:
            Stage(tile, state, front, [] if bulk else done, f"front_{phase}", state.get("token")).run()
            state["token"] = state[("u", phase, tile.nx - 1)]
            if phase < tile.steps:
                exchange("", phase, state[("e", phase, tile.nx - 1)], state.get(("e", phase, 0)))
        if bulk:
            Stage(tile, state, bulk, done, f"bulk_{phase}").run()
            state["token"] = state[("u", bulk[0][0] + 1, bulk[0][1])]
        later = [(name, k) for name, (when, k, _) in tile.second.items() if when == phase]
        direct = [planes for planes in done if tile.plan[planes][1] is None]
        joined = [k for name, k in later if tile.second[name][2] and direct]
        for planes in done:
            if planes not in direct:
                first = 1 if tile.second[tile.plan[planes][1]][1] > 1 else 2
                state[("got", planes)] = xor_swap(tile, state[("send", planes)], first)
                continue
            for k in range(tile.src - 1, 0, -1):
                if k not in joined:
                    state[("r", planes, k)] = (xor_swap(tile, state[("s", planes, k)], k), 0)
        ahead = {0: [(0, tile.nx - 1)], 1: [(1, tile.nx - 1), (2, tile.nx - 2)]}.get(phase)
        if ahead and not tile.far and tile.steps == 3:
            run_ahead(tile, state, ahead, f"ahead_{phase}")
        for name, k in later:
            group = [planes for planes in pieces if tile.plan[planes][1] == name]
            along = direct[0] if k in joined else None
            after = state["token"]
            second_round(tile, state, group, k, after, along)
            if phase < tile.steps:
                state["token"] = state["passed"]
    following = final_fields(tile, state)
    return (following, *combine(tile, state, pieces))


def solution(mesh):
    placed = (
        P("src", None, "gx", "gy", None),
        P("src", None, "gx", "gy", None),
        P(None, "src", None, "gx", "gy", None),
        P("gx", "gy", None),
        P("gx", "gy", None),
        P("gx", "gy", None),
        P("gx", "gy", None),
        P("gx", "gy", None),
        P("src", None),
        P("src"),
        P("src", None, None),
    )

    def program(*args):
        return on_device(mesh, *args)

    return jax.shard_map(
        program,
        mesh=mesh,
        in_specs=placed,
        out_specs=(
            P("src", None, "gx", "gy", None),
            P("gx", "gy", "src"),
            P("gx", "gy", "src"),
            P("gx", "gy", "src"),
        ),
        check_vma=False,
    )
```
